128 devices in a mesh: src: 4 (over x), grp: 32 (over z, y, core).
Axes of the slice: x: 4, y: 4, z: 4, core: 2. Of those that a mesh axis runs over, the one named last changes fastest.
Arguments:
- source_points: bfloat16 [32768, 64], P('src'), may hold values from -6 to 6
- source_logmass: float32 [32768], P('src'), may hold values from -1 to 1
- target_points: bfloat16 [524288, 64], P(('src', 'grp')), may hold values from -1.796875 to 1.796875
- target_logmass: float32 [524288], P(('src', 'grp')), may hold values from -1 to 1
- target_potential: float32 [524288], P(('src', 'grp')), may hold values from -1.5 to 61.5
- tile_slot: int32 [256, 256], P('src', 'grp'), may hold values from 0 to 31, as said below
- tile_counts: int32 [256, 32], P('src', 'grp'), may hold values from 2 to 8
- fetch_ids: int32 [16, 256], P('src', 'grp'), may hold values from 0 to 31, as said below
Outputs:
- source_field: float32 [32768], P('src')
- target_field: float32 [524288], P(('src', 'grp'))
The draws below stay inside these ranges and needn't reach their ends.
Inputs may be any that keep to these rules, and one draw needn't show every extreme that they name: `tile_slot`: within one source block and group the live slots name distinct entries; every entry 0 to 31 of a device's fetch list is named by some live slot of that device. `fetch_ids`: each device names 8 distinct blocks of each peer in its group; every target block is named by some device of its group.
All inputs are finite; a program needn't handle non-finite values.
Results may differ from the reference program's by a relative error of at most 0.0003.
Values may be sent and summed in bfloat16 or wider, within the bound.
No kernel may reach another device: no remote copies, remote signals or barrier semaphores. Data moves between devices by JAX's collectives and lax.ppermute only.
A program may use at most 64 MiB of HBM per device.

```python
import math
import jax
import jax.numpy as jnp
from jax import lax

D = 64
BLOCK = 128
SB = 64
TB_DEV = 32
KG = 8
ITERS = 3
CAP = 8
SBLOCKS = 256
SOURCES = 32768
TBLOCKS = 4096
TARGETS = 524288
N_SRC = 4
N_GRP = 32


def tile_plan(key):
    key = jax.random.fold_in(key, 11)
    keys = jax.random.split(key, 5)
    device_ids = jnp.arange(N_SRC, dtype=jnp.int32)[:, None, None] * N_GRP + jnp.arange(N_GRP, dtype=jnp.int32)[None, None, :]
    chosen = jax.random.randint(keys[1], (), 0, N_SRC * N_GRP)
    heavy = (jax.random.randint(keys[0], (N_SRC, 1, N_GRP), 0, 16) == 0) | (device_ids == chosen)
    upper = jax.random.randint(keys[2], (N_SRC, SB, N_GRP), KG // 2, KG + 1)
    counts = jnp.where(heavy, upper, 2)
    place = jax.random.randint(keys[3], (), 0, SB)
    counts = jnp.where((device_ids == chosen) & (jnp.arange(SB, dtype=jnp.int32)[None, :, None] == place), KG, counts)
    starts = jnp.cumsum(counts, axis=1) - counts
    rotation = jax.random.randint(keys[4], (N_SRC, 1, N_GRP, 1), 0, N_SRC * CAP)
    slot_ids = (starts[..., None] + jnp.arange(KG, dtype=jnp.int32)[None, None, None, :] + rotation) % (N_SRC * CAP)
    return (slot_ids.reshape(SBLOCKS, N_GRP * KG).astype(jnp.int32), counts.reshape(SBLOCKS, N_GRP).astype(jnp.int32))


def draw_tile_slot(key, part):
    return tile_plan(key)[0]


def draw_tile_counts(key, part):
    return tile_plan(key)[1]


def draw_fetch_ids(key, part):
    key = jax.random.fold_in(key, 3)
    keys = jax.random.split(key, N_SRC * N_GRP)
    orders = jax.vmap(lambda one_key: jax.random.permutation(one_key, TB_DEV))(keys).reshape(1, N_SRC, N_GRP, TB_DEV)
    position = (jnp.arange(N_SRC, dtype=jnp.int32)[:, None, None, None] * CAP + jnp.arange(CAP, dtype=jnp.int32)[None, None, None, :]) % TB_DEV
    spread_orders = jnp.broadcast_to(orders, (N_SRC, N_SRC, N_GRP, TB_DEV))
    picked = jnp.take_along_axis(spread_orders, jnp.broadcast_to(position, (N_SRC, N_SRC, N_GRP, CAP)), axis=3)
    return picked.reshape(N_SRC * N_SRC, N_GRP * CAP).astype(jnp.int32)


def draw_source_points(key, part):
    key = jax.random.fold_in(key, 1)
    first, second = jax.random.split(key)
    base = jnp.clip(jax.random.normal(first, (SOURCES, D), jnp.float32), -4.0, 4.0)
    scale = jnp.exp(jax.random.uniform(second, (SOURCES, 1), jnp.float32, math.log(0.7), math.log(1.4)))
    return (0.3 * base * scale).astype(jnp.bfloat16)


def draw_target_potential(key, part):
    key = jax.random.fold_in(key, 5)
    first, second = jax.random.split(key)
    rough = jnp.clip(0.5 * jax.random.normal(first, (TBLOCKS, BLOCK), jnp.float32), -1.5, 1.5)
    offset = jax.random.uniform(second, (TBLOCKS, 1), jnp.float32, 0.0, 60.0)
    return (offset + rough).reshape(TARGETS).astype(jnp.float32)


def block_scale(rng, dims, cuts, smallest, top_value):
    loudness = 1.0
    for dim, shards_of in cuts:
        steps = jax.random.uniform(jax.random.fold_in(jax.random.fold_in(rng, 6), dim), (shards_of,), jnp.float32, smallest / len(cuts), top_value / len(cuts))
        loudness = loudness * jnp.repeat(jnp.exp(steps), dims[dim] // shards_of).reshape((-1,) + (1,) * (len(dims) - 1 - dim))
    return loudness


def scatter_about(key, shape, spread, reach, shards=(), kind=jnp.bfloat16):
    result = jax.random.normal(key, shape, jnp.float32) * spread
    if len(shards) > 0:
        result = block_scale(key, shape, shards, -0.22, 0.18) * result
    return jnp.clip(result, min=-reach, max=reach).astype(kind)


def setup_inputs(seed: int = 0) -> dict:
    seeds = jax.random.split(jax.random.key(seed), 9)
    return {
        "source_points": draw_source_points(jax.random.fold_in(seeds[8], 71), 0),
        "source_logmass": jnp.clip(jax.random.uniform(seeds[1], (SOURCES,), jnp.float32, -1.0, 1.0) * block_scale(seeds[1], (SOURCES,), ((0, 4),), -0.4, 0.0), -1.0, 1.0),
        "target_points": scatter_about(seeds[2], (TARGETS, D), 0.3, 1.796875, ((0, 128),)),
        "target_logmass": jnp.clip(jax.random.uniform(seeds[3], (TARGETS,), jnp.float32, -1.0, 1.0) * block_scale(seeds[3], (TARGETS,), ((0, 128),), -0.4, 0.0), -1.0, 1.0),
        "target_potential": draw_target_potential(jax.random.fold_in(seeds[8], 71), 0),
        "tile_slot": draw_tile_slot(jax.random.fold_in(seeds[8], 71), 0),
        "tile_counts": draw_tile_counts(jax.random.fold_in(seeds[8], 71), 0),
        "fetch_ids": draw_fetch_ids(jax.random.fold_in(seeds[8], 71), 0),
    }


EPSILON = 0.25
LOWEST = -1e30


def target_blocks(tile_slot, fetch_ids):
    holder = (jnp.arange(SBLOCKS, dtype=jnp.int32) // SB)[:, None, None]
    slot_ids = tile_slot.reshape(SBLOCKS, N_GRP, KG)
    peer_ids = slot_ids // CAP
    column = slot_ids % CAP
    group_ids = jnp.arange(N_GRP, dtype=jnp.int32)[None, :, None]
    local_ids = fetch_ids[holder * N_SRC + peer_ids, group_ids * CAP + column]
    return ((peer_ids * N_GRP + group_ids) * TB_DEV + local_ids).astype(jnp.int32).reshape(SBLOCKS, N_GRP * KG)


def tile_costs(block_points, block_sq, block_ids, target_pts, target_sq):
    others = target_pts[block_ids].astype(jnp.float32)
    products = jnp.einsum("bid,bkjd->bkij", block_points.astype(jnp.float32), others)
    return 0.5 * (block_sq[:, None, :, None] + target_sq[block_ids][:, :, None, :]) - products


def reference(source_points, source_logmass, target_points, target_logmass, target_potential, tile_slot, tile_counts, fetch_ids):
    block_ids = target_blocks(tile_slot, fetch_ids)
    alive_mask = (jnp.arange(KG, dtype=jnp.int32)[None, None, :] < tile_counts[:, :, None]).reshape(SBLOCKS, N_GRP * KG)
    per_turn = math.gcd(SBLOCKS, 8)
    turns = SBLOCKS // per_turn
    points = source_points.reshape(turns, per_turn, BLOCK, D)
    source_sq = jnp.sum(jnp.square(source_points.astype(jnp.float32)), -1).reshape(turns, per_turn, BLOCK)
    target_pts = target_points.reshape(TBLOCKS, BLOCK, D)
    target_sq = jnp.sum(jnp.square(target_points.astype(jnp.float32)), -1).reshape(TBLOCKS, BLOCK)
    ids_turns = block_ids.reshape(turns, per_turn, N_GRP * KG)
    alive_turns = alive_mask.reshape(turns, per_turn, N_GRP * KG)
    target_mass = target_logmass.reshape(TBLOCKS, BLOCK)
    potential = target_potential.reshape(TBLOCKS, BLOCK)
    source_field = source_logmass
    for sweep_index in range(ITERS):
        def row_turn(turn_input, potential=potential):
            block_points, block_sq, turn_ids, turn_alive = turn_input
            tile_cost = tile_costs(block_points, block_sq, turn_ids, target_pts, target_sq)
            scores = jnp.where(turn_alive[:, :, None, None], (potential[turn_ids][:, :, None, :] - tile_cost) / EPSILON, LOWEST)
            row_top = jnp.max(scores, axis=(1, 3))
            row_mass = jnp.sum(jnp.exp(scores - row_top[:, None, :, None]), axis=(1, 3))
            return row_top, row_mass

        row_top, row_mass = lax.map(row_turn, (points, source_sq, ids_turns, alive_turns))
        source_field = EPSILON * source_logmass - EPSILON * (row_top.reshape(-1) + jnp.log(row_mass.reshape(-1)))
        field_turns = source_field.reshape(turns, per_turn, BLOCK)

        def column_turn(turn_input):
            block_points, block_sq, turn_ids, turn_alive, block_field = turn_input
            tile_cost = tile_costs(block_points, block_sq, turn_ids, target_pts, target_sq)
            scores = jnp.where(turn_alive[:, :, None, None], (block_field[:, None, :, None] - tile_cost) / EPSILON, LOWEST)
            col_top = jnp.max(scores, axis=2)
            col_mass = jnp.sum(jnp.exp(scores - col_top[:, :, None, :]), axis=2)
            return col_top, jnp.where(turn_alive[:, :, None], col_mass, 0.0)

        col_top, col_mass = lax.map(column_turn, (points, source_sq, ids_turns, alive_turns, field_turns))
        flat_ids = block_ids.reshape(-1)
        col_top = col_top.reshape(-1, BLOCK)
        col_mass = col_mass.reshape(-1, BLOCK)
        block_peak = jnp.full((TBLOCKS, BLOCK), LOWEST, jnp.float32).at[flat_ids].max(col_top)
        block_mass = jnp.zeros((TBLOCKS, BLOCK), jnp.float32).at[flat_ids].add(col_mass * jnp.exp(col_top - block_peak[flat_ids]))
        potential = EPSILON * target_mass - EPSILON * (block_peak + jnp.log(block_mass))
    return source_field, potential.reshape(-1)
```

```python
import functools

import jax
import jax.numpy as jnp
from jax import lax
from jax.experimental import pallas as pl
from jax.experimental.pallas import tpu as pltpu
from jax.sharding import PartitionSpec as P

D = 64
BLOCK = 128
KG = 8
ITERS = 3
EPSILON = 0.25
LOWEST = -1e30
LOG2E = 1.4426950408889634
SCALE = LOG2E / EPSILON
UNROLL = 8
GROUP = 32


def plan_kernel(blocks, slots_ref, counts_ref, block_ref, slot_ref, total_ref):
    def one_block(b, position):
        for k in range(KG):
            block_ref[position + k] = b
            slot_ref[position + k] = slots_ref[b * KG + k]
        return position + counts_ref[b]

    total = lax.fori_loop(0, blocks, one_block, jnp.int32(0))
    for k in range(UNROLL):
        block_ref[total + k] = blocks
        slot_ref[total + k] = GROUP
    total_ref[0] = (total + UNROLL - 1) // UNROLL


def plan(tile_slot, tile_counts):
    blocks = tile_counts.shape[0]
    room = blocks * KG + UNROLL + KG
    smem = pl.BlockSpec(memory_space=pltpu.SMEM)
    return pl.pallas_call(
        functools.partial(plan_kernel, blocks),
        out_shape=(
            jax.ShapeDtypeStruct((room,), jnp.int32),
            jax.ShapeDtypeStruct((room,), jnp.int32),
            jax.ShapeDtypeStruct((1,), jnp.int32),
        ),
        in_specs=[smem, smem],
        out_specs=(smem, smem, smem),
    )(tile_slot.reshape(-1), tile_counts.reshape(-1))


def split3(values):
    high = values.astype(jnp.bfloat16)
    rest = values - high.astype(jnp.float32)
    middle = rest.astype(jnp.bfloat16)
    low = (rest - middle.astype(jnp.float32)).astype(jnp.bfloat16)
    return high, middle, low


def nt_dot(left, right):
    return lax.dot_general(left, right, (((1,), (1,)), ((), ())), preferred_element_type=jnp.float32)


def pass_kernel(
    total_ref, left_ids, right_ids, left_ref, right_ref, bias_ref, out_ref, columns, peaks, masses
):
    lefts, rights = left_ref.shape[0], right_ref.shape[0]
    diagonal = lax.broadcasted_iota(jnp.int32, (BLOCK, BLOCK), 0) == lax.broadcasted_iota(
        jnp.int32, (BLOCK, BLOCK), 1
    )
    eye = jnp.where(diagonal, 1.0, 0.0).astype(jnp.bfloat16)
    for group in range(lefts // GROUP):
        high, middle, low = split3(bias_ref[group * GROUP : (group + 1) * GROUP, :])
        parts = jnp.concatenate([high, middle, low, jnp.zeros_like(high)], axis=0)
        columns[group] = nt_dot(eye, parts).astype(jnp.bfloat16)
    peaks[...] = jnp.full_like(peaks, LOWEST)
    masses[...] = jnp.zeros_like(masses)
    lane = lax.broadcasted_iota(jnp.int32, (BLOCK, BLOCK), 1)
    lane = jnp.where(lane < 3 * GROUP, lane % GROUP, -1)

    def step(t, carry):
        for u in range(UNROLL):
            left_id = jnp.minimum(left_ids[t * UNROLL + u], lefts - 1)
            right_id = right_ids[t * UNROLL + u]
            picked = jnp.where(lane == left_id % GROUP, 1.0, 0.0).astype(jnp.bfloat16)
            left = jnp.concatenate([left_ref[left_id], columns[left_id // GROUP]], axis=1)
            right = jnp.concatenate([right_ref[jnp.minimum(right_id, rights - 1)], picked], axis=1)
            scores = nt_dot(left, right).reshape(BLOCK // 8, 8, BLOCK)
            old = peaks[u, right_id]
            top = jnp.maximum(old, jnp.max(scores, axis=0))
            mass = jnp.sum(jnp.exp2(scores - top[None]), axis=0)
            masses[u, right_id] = masses[u, right_id] * jnp.exp2(old - top) + mass
            peaks[u, right_id] = top
        return carry

    lax.fori_loop(0, total_ref[0], step, 0)

    def finish(r, carry):
        tops = [peaks[u, r] for u in range(UNROLL)]
        top = functools.reduce(jnp.maximum, tops)
        top = jnp.max(top, axis=0, keepdims=True)
        mass = sum(masses[u, r] * jnp.exp2(tops[u] - top) for u in range(UNROLL))
        mass = jnp.sum(mass, axis=0, keepdims=True)
        out_ref[pl.ds(r, 1), :] = top + jnp.log2(mass)
        return carry

    lax.fori_loop(0, rights, finish, 0, unroll=8)


def log_sums(total, left_ids, right_ids, left, right, bias):
    smem = pl.BlockSpec(memory_space=pltpu.SMEM)
    vmem = pl.BlockSpec(memory_space=pltpu.VMEM)
    rights = right.shape[0]
    return pl.pallas_call(
        pass_kernel,
        out_shape=jax.ShapeDtypeStruct((rights, BLOCK), jnp.float32),
        in_specs=[smem, smem, smem, vmem, vmem, vmem],
        out_specs=vmem,
        scratch_shapes=[
            pltpu.VMEM((left.shape[0] // GROUP, BLOCK, BLOCK), jnp.bfloat16),
            pltpu.VMEM((UNROLL, rights + 1, 8, BLOCK), jnp.float32),
            pltpu.VMEM((UNROLL, rights + 1, 8, BLOCK), jnp.float32),
        ],
        compiler_params=pltpu.CompilerParams(vmem_limit_bytes=40 * 1024 * 1024),
    )(total, left_ids, right_ids, left, right, bias)


def combine(values, axis):
    top = jnp.max(values, axis=axis, keepdims=True)
    return jnp.squeeze(top, axis) + jnp.log2(jnp.sum(jnp.exp2(values - top), axis=axis))


def shards(
    source_points,
    source_logmass,
    target_points,
    target_logmass,
    target_potential,
    tile_slot,
    tile_counts,
    fetch_ids,
):
    peers = lax.axis_size("src")
    groups = lax.axis_size("grp")
    blocks = tile_counts.shape[0]
    per_peer = fetch_ids.shape[1]
    owned = target_potential.shape[0] // BLOCK
    fetched_count = peers * per_peer
    sources = source_points.shape[0]
    share = sources // groups

    def across(values):
        return lax.all_to_all(values, "src", split_axis=0, concat_axis=0, tiled=True)

    block_list, slot_list, total = plan(tile_slot, tile_counts)
    requested = across(fetch_ids)
    target_sq = jnp.sum(jnp.square(target_points.astype(jnp.float32)), -1)
    start = SCALE * (target_potential - 0.5 * target_sq)
    halves = target_points.reshape(owned, 2, BLOCK // 2, D)
    packed = jnp.concatenate([halves[:, 0], halves[:, 1]], axis=-1)
    fetched = across(packed[requested]).reshape(fetched_count, BLOCK // 2, 2 * D)
    mass_rows = LOG2E * target_logmass.reshape(owned, BLOCK)
    potentials = across(start.reshape(owned, BLOCK)[requested]).reshape(fetched_count, BLOCK)
    low_half, high_half = fetched[:, :, :D], fetched[:, :, D:]
    targets = jnp.concatenate(
        [
            jnp.concatenate([low_half, low_half], axis=-1),
            jnp.concatenate([high_half, high_half], axis=-1),
        ],
        axis=1,
    )
    wide = source_points.astype(jnp.float32)
    source_sq = jnp.sum(jnp.square(wide), -1)
    scaled = SCALE * wide
    high = lax.reduce_precision(scaled, 8, 7)
    points = jnp.concatenate(
        [high.astype(jnp.bfloat16), (scaled - high).astype(jnp.bfloat16)], axis=-1
    ).reshape(blocks, BLOCK, 2 * D)
    my_mass = LOG2E * lax.dynamic_slice(
        source_logmass, (lax.axis_index("grp") * share,), (share,)
    )
    mine = jnp.arange(owned, dtype=jnp.int32)[:, None, None] == requested[None]

    for sweep_index in range(ITERS):
        rows = log_sums(total, slot_list, block_list, targets, points, potentials)
        rows = lax.all_to_all(rows.reshape(groups, share), "grp", 0, 0, tiled=True)
        field = my_mass - combine(rows, 0)
        field = lax.all_to_all(
            jnp.broadcast_to(field[None], (groups, share)), "grp", 0, 0, tiled=True
        ).reshape(blocks, BLOCK)
        cols = log_sums(total, block_list, slot_list, points, targets, field)
        back = across(cols.reshape(peers, per_peer, BLOCK))
        parts = jnp.max(jnp.where(mine[..., None], back[None], LOWEST), axis=2)
        owned_pot = mass_rows - combine(parts, 1)
        if sweep_index < ITERS - 1:
            potentials = across(owned_pot[requested]).reshape(fetched_count, BLOCK)
    source_field = field.reshape(-1) * (1.0 / SCALE) + 0.5 * source_sq
    target_field = owned_pot.reshape(-1) * (1.0 / SCALE) + 0.5 * target_sq
    return (source_field, target_field)


def solution(mesh):
    return jax.shard_map(
        shards,
        mesh=mesh,
        in_specs=(
            P("src", None),
            P("src"),
            P(("src", "grp"), None),
            P(("src", "grp")),
            P(("src", "grp")),
            P("src", "grp"),
            P("src", "grp"),
            P("src", "grp"),
        ),
        out_specs=(P("src"), P(("src", "grp"))),
        check_vma=False,
    )
```

```python
import functools

import jax
import jax.numpy as jnp
from jax import lax
from jax.experimental import pallas as pl
from jax.experimental.pallas import tpu as pltpu
from jax.sharding import PartitionSpec as P

D = 64
BLOCK = 128
KG = 8
ITERS = 3
EPSILON = 0.25
LOWEST = -1e30
LOG2E = 1.4426950408889634
SCALE = LOG2E / EPSILON
PAIRS = 32
COPIES = 2
GROUP = 32


def plan_kernel(
    blocks, slots_ref, counts_ref, col_left, col_right, col_total, row_left, row_right, row_total, lists, sizes
):
    stride = blocks + KG
    for q in range(GROUP + 1):
        sizes[q] = 0

    def one_block(b, position):
        count = counts_ref[b]
        for k in range(KG):
            live = k < count
            slot = jnp.where(live, slots_ref[b * KG + k], GROUP)
            if k % 2 == 0:
                col_left[position + k // 2] = b
            col_right[2 * position + k] = slot
            size = sizes[slot]
            lists[slot * stride + size] = b
            sizes[slot] = jnp.where(live, size + 1, 0)
        return position + (count + 1) // 2

    total = lax.fori_loop(0, blocks, one_block, jnp.int32(0))
    col_total[0] = (total + PAIRS - 1) // PAIRS

    def pad_cols(k, carry):
        col_left[total + k] = 0
        col_right[2 * (total + k)] = GROUP
        col_right[2 * (total + k) + 1] = GROUP
        return carry

    lax.fori_loop(0, PAIRS, pad_cols, 0)

    def one_slot(q, position):
        size = sizes[q]
        lists[q * stride + size] = blocks

        def one_pair(k, carry):
            row_left[position + k] = q
            row_right[2 * (position + k)] = lists[q * stride + 2 * k]
            row_right[2 * (position + k) + 1] = lists[q * stride + 2 * k + 1]
            return carry

        lax.fori_loop(0, (size + 1) // 2, one_pair, 0)
        return position + (size + 1) // 2

    rows = lax.fori_loop(0, GROUP, one_slot, jnp.int32(0))
    row_total[0] = (rows + PAIRS - 1) // PAIRS

    def pad_rows(k, carry):
        row_left[rows + k] = 0
        row_right[2 * (rows + k)] = blocks
        row_right[2 * (rows + k) + 1] = blocks
        return carry

    lax.fori_loop(0, PAIRS, pad_rows, 0)


def plan(tile_slot, tile_counts):
    blocks = tile_counts.shape[0]
    col_room = blocks * KG // 2 + PAIRS + KG
    row_room = blocks * KG // 2 + GROUP + PAIRS
    smem = pl.BlockSpec(memory_space=pltpu.SMEM)
    shapes = [(col_room,), (2 * col_room,), (1,), (row_room,), (2 * row_room,), (1,)]
    out = pl.pallas_call(
        functools.partial(plan_kernel, blocks),
        out_shape=[jax.ShapeDtypeStruct(shape, jnp.int32) for shape in shapes],
        in_specs=[smem, smem],
        out_specs=[smem] * len(shapes),
        scratch_shapes=[
            pltpu.SMEM(((GROUP + 1) * (blocks + KG),), jnp.int32),
            pltpu.SMEM((GROUP + 1,), jnp.int32),
        ],
    )(tile_slot.reshape(-1), tile_counts.reshape(-1))
    return out[:3], out[3:]


def split3(values):
    high = values.astype(jnp.bfloat16)
    rest = values - high.astype(jnp.float32)
    middle = rest.astype(jnp.bfloat16)
    low = (rest - middle.astype(jnp.float32)).astype(jnp.bfloat16)
    return high, middle, low


def pass_kernel(
    left_ids, right_ids, total_ref, left_ref, right_ref, bias_ref, out_ref, columns, peaks, masses
):
    lefts, rights = left_ref.shape[0], right_ref.shape[0]
    square = (BLOCK, BLOCK)
    lane = lax.broadcasted_iota(jnp.int32, square, 1)
    eye = jnp.where(lane == lax.broadcasted_iota(jnp.int32, square, 0), 1.0, 0.0).astype(jnp.bfloat16)
    lane = jnp.where(lane < 3 * GROUP, lane % GROUP, -1)
    for group in range(lefts // GROUP):
        high, middle, low = split3(bias_ref[group * GROUP : (group + 1) * GROUP, :])
        parts = jnp.concatenate([high, middle, low, jnp.zeros_like(high)], axis=0)
        turned = lax.dot_general(
            eye, parts, (((1,), (1,)), ((), ())), preferred_element_type=jnp.float32
        )

        def fill(k, carry, group=group, turned=turned):
            columns[group * GROUP + k] = jnp.where(lane == k, turned, 0.0).astype(jnp.bfloat16)
            return carry

        lax.fori_loop(0, GROUP, fill, 0, unroll=4)
    peaks[...] = jnp.full_like(peaks, LOWEST)
    masses[...] = jnp.zeros_like(masses)
    ones = jnp.ones((BLOCK, 2 * BLOCK), jnp.bfloat16)

    def fold(copy, r, scores):
        scores = scores.reshape(BLOCK // 8, 8, BLOCK)
        old = peaks[copy, r]
        top = jnp.maximum(old, jnp.max(scores, axis=0))
        mass = jnp.sum(jnp.exp2(scores - top[None]), axis=0)
        masses[copy, r] = masses[copy, r] * jnp.exp2(old - top) + mass
        peaks[copy, r] = top

    def step(t, carry):
        for u in range(PAIRS):
            i = t * PAIRS + u
            l, first, second = left_ids[i], right_ids[2 * i], right_ids[2 * i + 1]
            left = jnp.concatenate([left_ref[l], columns[l]], axis=1)
            right = jnp.concatenate(
                [right_ref[jnp.minimum(first, rights - 1)], right_ref[jnp.minimum(second, rights - 1)]],
                axis=1,
            )
            scores = jnp.dot(
                left, jnp.concatenate([right, ones], axis=0), preferred_element_type=jnp.float32
            )
            fold((2 * u) % COPIES, first, scores[:, :BLOCK])
            fold((2 * u + 1) % COPIES, second, scores[:, BLOCK:])
        return carry

    lax.fori_loop(0, total_ref[0], step, 0)

    def finish(octet, carry):
        rows = []
        for k in range(8):
            r = octet * 8 + k
            tops = [peaks[copy, r] for copy in range(COPIES)]
            top = jnp.max(functools.reduce(jnp.maximum, tops), axis=0, keepdims=True)
            mass = sum(masses[copy, r] * jnp.exp2(tops[copy] - top) for copy in range(COPIES))
            rows.append(top + jnp.log2(jnp.sum(mass, axis=0, keepdims=True)))
        out_ref[pl.ds(pl.multiple_of(octet * 8, 8), 8), :] = jnp.concatenate(rows, axis=0)
        return carry

    lax.fori_loop(0, rights // 8, finish, 0)


def log_sums(pairs, left, right, bias):
    smem = pl.BlockSpec(memory_space=pltpu.SMEM)
    vmem = pl.BlockSpec(memory_space=pltpu.VMEM)
    lefts, rights = left.shape[0], right.shape[0]
    return pl.pallas_call(
        pass_kernel,
        out_shape=jax.ShapeDtypeStruct((rights, BLOCK), jnp.float32),
        in_specs=[smem, smem, smem, vmem, vmem, vmem],
        out_specs=vmem,
        scratch_shapes=[
            pltpu.VMEM((lefts, BLOCK, BLOCK), jnp.bfloat16),
            pltpu.VMEM((COPIES, rights + 1, 8, BLOCK), jnp.float32),
            pltpu.VMEM((COPIES, rights + 1, 8, BLOCK), jnp.float32),
        ],
        compiler_params=pltpu.CompilerParams(vmem_limit_bytes=40 * 1024 * 1024),
    )(*pairs, left, right, bias)


def combine(values, axis):
    top = jnp.max(values, axis=axis, keepdims=True)
    return jnp.squeeze(top, axis) + jnp.log2(jnp.sum(jnp.exp2(values - top), axis=axis))


def shards(
    source_points,
    source_logmass,
    target_points,
    target_logmass,
    target_potential,
    tile_slot,
    tile_counts,
    fetch_ids,
):
    peers = lax.axis_size("src")
    groups = lax.axis_size("grp")
    blocks = tile_counts.shape[0]
    per_peer = fetch_ids.shape[1]
    owned = target_potential.shape[0] // BLOCK
    fetched_count = peers * per_peer
    sources = source_points.shape[0]
    share = sources // groups

    def across(values):
        return lax.all_to_all(values, "src", split_axis=0, concat_axis=0, tiled=True)

    col_pairs, row_pairs = plan(tile_slot, tile_counts)
    requested = across(fetch_ids)
    target_sq = jnp.sum(jnp.square(target_points.astype(jnp.float32)), -1)
    start = SCALE * (target_potential - 0.5 * target_sq)
    halves = target_points.reshape(owned, 2, BLOCK // 2, D)
    packed = jnp.concatenate([halves[:, 0], halves[:, 1]], axis=-1)
    fetched = across(packed[requested]).reshape(fetched_count, BLOCK // 2, 2 * D)
    mass_rows = LOG2E * target_logmass.reshape(owned, BLOCK)
    potentials = across(start.reshape(owned, BLOCK)[requested]).reshape(fetched_count, BLOCK)
    low_half, high_half = fetched[:, :, :D], fetched[:, :, D:]
    targets = jnp.concatenate(
        [
            jnp.concatenate([low_half, low_half], axis=-1),
            jnp.concatenate([high_half, high_half], axis=-1),
        ],
        axis=1,
    )
    wide = source_points.astype(jnp.float32)
    source_sq = jnp.sum(jnp.square(wide), -1)
    scaled = SCALE * wide
    high = lax.reduce_precision(scaled, 8, 7)
    points = jnp.concatenate(
        [high.astype(jnp.bfloat16), (scaled - high).astype(jnp.bfloat16)], axis=-1
    ).reshape(blocks, BLOCK, 2 * D)
    points_turned = points.transpose(0, 2, 1)
    targets_turned = targets.transpose(0, 2, 1)
    my_mass = LOG2E * lax.dynamic_slice(
        source_logmass, (lax.axis_index("grp") * share,), (share,)
    )
    mine = jnp.arange(owned, dtype=jnp.int32)[:, None, None] == requested[None]

    for sweep_index in range(ITERS):
        rows = log_sums(row_pairs, targets, points_turned, potentials)
        rows = lax.all_to_all(rows.reshape(groups, share), "grp", 0, 0, tiled=True)
        field = my_mass - combine(rows, 0)
        field = lax.all_to_all(
            jnp.broadcast_to(field[None], (groups, share)), "grp", 0, 0, tiled=True
        ).reshape(blocks, BLOCK)
        cols = log_sums(col_pairs, points, targets_turned, field)
        back = across(cols.reshape(peers, per_peer, BLOCK))
        parts = jnp.max(jnp.where(mine[..., None], back[None], LOWEST), axis=2)
        owned_pot = mass_rows - combine(parts, 1)
        if sweep_index < ITERS - 1:
            potentials = across(owned_pot[requested]).reshape(fetched_count, BLOCK)
    source_field = field.reshape(-1) * (1.0 / SCALE) + 0.5 * source_sq
    target_field = owned_pot.reshape(-1) * (1.0 / SCALE) + 0.5 * target_sq
    return (source_field, target_field)


def solution(mesh):
    return jax.shard_map(
        shards,
        mesh=mesh,
        in_specs=(
            P("src", None),
            P("src"),
            P(("src", "grp"), None),
            P(("src", "grp")),
            P(("src", "grp")),
            P("src", "grp"),
            P("src", "grp"),
            P("src", "grp"),
        ),
        out_specs=(P("src"), P(("src", "grp"))),
        check_vma=False,
    )
```

```python
import functools

import jax
import jax.numpy as jnp
from jax import lax
from jax.experimental import pallas as pl
from jax.experimental.pallas import tpu as pltpu
from jax.sharding import PartitionSpec as P

D = 64
BLOCK = 128
KG = 8
ITERS = 3
EPSILON = 0.25
LOWEST = -1e30
LOG2E = 1.4426950408889634
SCALE = LOG2E / EPSILON
PAIRS = 32
COPIES = 2
GROUP = 32
EXTRA = 16


def plan_kernel(
    blocks, slots_ref, counts_ref, col_left, col_right, col_total, row_left, row_right, row_total, lists, sizes
):
    stride = blocks + KG
    for q in range(GROUP + 1):
        sizes[q] = 0

    def one_block(b, position):
        count = counts_ref[b]
        for k in range(KG):
            live = k < count
            slot = jnp.where(live, slots_ref[b * KG + k], GROUP)
            if k % 2 == 0:
                col_left[position + k // 2] = b
            col_right[2 * position + k] = slot
            size = sizes[slot]
            lists[slot * stride + size] = b
            sizes[slot] = jnp.where(live, size + 1, 0)
        return position + (count + 1) // 2

    total = lax.fori_loop(0, blocks, one_block, jnp.int32(0))
    col_total[0] = (total + PAIRS - 1) // PAIRS

    def pad_cols(k, carry):
        col_left[total + k] = 0
        col_right[2 * (total + k)] = GROUP
        col_right[2 * (total + k) + 1] = GROUP
        return carry

    lax.fori_loop(0, PAIRS, pad_cols, 0)

    def one_slot(q, position):
        size = sizes[q]
        lists[q * stride + size] = blocks

        def one_pair(k, carry):
            row_left[position + k] = q
            row_right[2 * (position + k)] = lists[q * stride + 2 * k]
            row_right[2 * (position + k) + 1] = lists[q * stride + 2 * k + 1]
            return carry

        lax.fori_loop(0, (size + 1) // 2, one_pair, 0)
        return position + (size + 1) // 2

    rows = lax.fori_loop(0, GROUP, one_slot, jnp.int32(0))
    row_total[0] = (rows + PAIRS - 1) // PAIRS

    def pad_rows(k, carry):
        row_left[rows + k] = 0
        row_right[2 * (rows + k)] = blocks
        row_right[2 * (rows + k) + 1] = blocks
        return carry

    lax.fori_loop(0, PAIRS, pad_rows, 0)


def plan(tile_slot, tile_counts):
    blocks = tile_counts.shape[0]
    col_room = blocks * KG // 2 + PAIRS + KG
    row_room = blocks * KG // 2 + GROUP + PAIRS
    smem = pl.BlockSpec(memory_space=pltpu.SMEM)
    shapes = [(col_room,), (2 * col_room,), (1,), (row_room,), (2 * row_room,), (1,)]
    out = pl.pallas_call(
        functools.partial(plan_kernel, blocks),
        out_shape=[jax.ShapeDtypeStruct(shape, jnp.int32) for shape in shapes],
        in_specs=[smem, smem],
        out_specs=[smem] * len(shapes),
        scratch_shapes=[
            pltpu.SMEM(((GROUP + 1) * (blocks + KG),), jnp.int32),
            pltpu.SMEM((GROUP + 1,), jnp.int32),
        ],
    )(tile_slot.reshape(-1), tile_counts.reshape(-1))
    return out[:3], out[3:]


def split3(values):
    high = values.astype(jnp.bfloat16)
    rest = values - high.astype(jnp.float32)
    middle = rest.astype(jnp.bfloat16)
    low = (rest - middle.astype(jnp.float32)).astype(jnp.bfloat16)
    return high, middle, low


def log_sum(values):
    top = functools.reduce(jnp.maximum, values)
    return top + jnp.log2(sum(jnp.exp2(value - top) for value in values))


def pack_kernel(place_ref, ids_ref, points_ref, potential_ref, logmass_ref, out_ref):
    place = place_ref[0]
    peers = ids_ref.shape[0] // out_ref.shape[0]
    per_peer = out_ref.shape[0] // peers
    for d in range(peers):
        other = lax.rem(place - d + peers, peers)

        def one_block(c, carry, d=d, other=other):
            t = ids_ref[(d * peers + place) * per_peer + c]
            block = points_ref[:, pl.ds(pl.multiple_of(t * BLOCK, BLOCK), BLOCK)]
            wide = block.astype(jnp.float32)
            norm = jnp.sum(wide * wide, axis=0, keepdims=True)
            start = SCALE * (potential_ref[pl.ds(t, 1), :] - 0.5 * norm)
            mass = LOG2E * logmass_ref[pl.ds(t, 1), :]
            rows = [part.astype(jnp.float32) for part in split3(start) + split3(mass)]
            rows.append(jnp.zeros((EXTRA - len(rows), BLOCK), jnp.float32))
            out_ref[other * per_peer + c, :D, :] = block
            out_ref[other * per_peer + c, D:, :] = jnp.concatenate(rows, axis=0).astype(jnp.bfloat16)
            return carry

        lax.fori_loop(0, per_peer, one_block, 0, unroll=4)


def unpack_kernel(in_ref, left_ref, start_ref, mass_ref):
    def one_block(q, carry):
        turned = in_ref[q, :D, :].T
        left_ref[q] = jnp.concatenate([turned, turned], axis=1)
        rows = in_ref[q, D:, :].astype(jnp.float32)
        start_ref[pl.ds(q, 1), :] = rows[0:1] + rows[1:2] + rows[2:3]
        mass_ref[pl.ds(q, 1), :] = rows[3:4] + rows[4:5] + rows[5:6]
        return carry

    lax.fori_loop(0, in_ref.shape[0], one_block, 0, unroll=4)


def source_kernel(points_ref, right_ref, left_ref, norm_ref):
    def one_block(b, carry):
        wide = points_ref[:, pl.ds(pl.multiple_of(b * BLOCK, BLOCK), BLOCK)].astype(jnp.float32)
        norm_ref[pl.ds(b, 1), :] = 0.5 * jnp.sum(wide * wide, axis=0, keepdims=True)
        scaled = SCALE * wide
        high = scaled.astype(jnp.bfloat16)
        low = (scaled - high.astype(jnp.float32)).astype(jnp.bfloat16)
        both = jnp.concatenate([high, low], axis=0)
        right_ref[b] = both
        left_ref[b] = both.T
        return carry

    lax.fori_loop(0, right_ref.shape[0], one_block, 0, unroll=4)


def start_bias(start_ref):
    return start_ref[...]


def field_bias(near, *rest):
    *far, mass_ref = rest
    return mass_ref[...] - log_sum([near[...]] + [ref[...] for ref in far])


def potential_bias(near, *rest):
    *far, chosen_ref, mass_ref = rest
    sums = jnp.concatenate([near[...]] + [ref[...] for ref in far], axis=0)
    chosen = chosen_ref[...]
    dot = functools.partial(jnp.dot, preferred_element_type=jnp.float32)
    parts = sum(dot(chosen, part) for part in split3(sums))
    known = dot(chosen, jnp.ones_like(chosen)) > 0.5
    parts = jnp.where(known, parts, LOWEST)
    count = near.shape[0]
    return mass_ref[...] - log_sum([parts[k * count : (k + 1) * count] for k in range(len(far) + 1)])


def pass_kernel(bias_of, bias_count, stacked, *refs):
    left_ids, right_ids, total_ref, left_ref, right_ref = refs[:5]
    bias_refs = refs[5 : 5 + bias_count]
    out_ref, bias_ref, columns, peaks, masses = refs[5 + bias_count :]
    lefts, rights = left_ref.shape[0], right_ref.shape[0]
    square = (BLOCK, BLOCK)
    lane = lax.broadcasted_iota(jnp.int32, square, 1)
    eye = jnp.where(lane == lax.broadcasted_iota(jnp.int32, square, 0), 1.0, 0.0).astype(jnp.bfloat16)
    lane = jnp.where(lane < 3 * GROUP, lane % GROUP, -1)
    bias_ref[...] = bias_of(*bias_refs)
    for group in range(lefts // GROUP):
        high, middle, low = split3(bias_ref[group * GROUP : (group + 1) * GROUP, :])
        parts = jnp.concatenate([high, middle, low, jnp.zeros_like(high)], axis=0)
        turned = lax.dot_general(
            eye, parts, (((1,), (1,)), ((), ())), preferred_element_type=jnp.float32
        )

        def fill(k, carry, group=group, turned=turned):
            columns[group * GROUP + k] = jnp.where(lane == k, turned, 0.0).astype(jnp.bfloat16)
            return carry

        lax.fori_loop(0, GROUP, fill, 0, unroll=4)
    peaks[...] = jnp.full_like(peaks, LOWEST)
    masses[...] = jnp.zeros_like(masses)
    ones = jnp.ones((BLOCK, 2 * BLOCK), jnp.bfloat16)

    def fold(copy, r, scores):
        scores = scores.reshape(BLOCK // 8, 8, BLOCK)
        old = peaks[copy, r]
        top = jnp.maximum(old, jnp.max(scores, axis=0))
        mass = jnp.sum(jnp.exp2(scores - top[None]), axis=0)
        masses[copy, r] = masses[copy, r] * jnp.exp2(old - top) + mass
        peaks[copy, r] = top

    def right_block(r):
        r = jnp.minimum(r, rights - 1)
        if stacked:
            return right_ref[r]
        block = right_ref[r, :D, :]
        return jnp.concatenate([block, block], axis=0)

    def step(t, carry):
        for u in range(PAIRS):
            i = t * PAIRS + u
            l, first, second = left_ids[i], right_ids[2 * i], right_ids[2 * i + 1]
            left = jnp.concatenate([left_ref[l], columns[l]], axis=1)
            right = jnp.concatenate([right_block(first), right_block(second)], axis=1)
            scores = jnp.dot(
                left, jnp.concatenate([right, ones], axis=0), preferred_element_type=jnp.float32
            )
            fold((2 * u) % COPIES, first, scores[:, :BLOCK])
            fold((2 * u + 1) % COPIES, second, scores[:, BLOCK:])
        return carry

    lax.fori_loop(0, total_ref[0], step, 0)

    def finish(octet, carry):
        rows = []
        for k in range(8):
            r = octet * 8 + k
            tops = [peaks[copy, r] for copy in range(COPIES)]
            top = jnp.max(functools.reduce(jnp.maximum, tops), axis=0, keepdims=True)
            mass = sum(masses[copy, r] * jnp.exp2(tops[copy] - top) for copy in range(COPIES))
            rows.append(top + jnp.log2(jnp.sum(mass, axis=0, keepdims=True)))
        out_ref[pl.ds(pl.multiple_of(octet * 8, 8), 8), :] = jnp.concatenate(rows, axis=0)
        return carry

    lax.fori_loop(0, rights // 8, finish, 0)


SMEM = pl.BlockSpec(memory_space=pltpu.SMEM)
VMEM = pl.BlockSpec(memory_space=pltpu.VMEM)
PARAMS = pltpu.CompilerParams(vmem_limit_bytes=40 * 1024 * 1024)


def log_sums(pairs, left, right, bias_of, bias, stacked):
    lefts, rights = left.shape[0], right.shape[0]
    return pl.pallas_call(
        functools.partial(pass_kernel, bias_of, len(bias), stacked),
        out_shape=[
            jax.ShapeDtypeStruct((rights, BLOCK), jnp.float32),
            jax.ShapeDtypeStruct((lefts, BLOCK), jnp.float32),
        ],
        in_specs=[SMEM] * 3 + [VMEM] * (2 + len(bias)),
        out_specs=[VMEM, VMEM],
        scratch_shapes=[
            pltpu.VMEM((lefts, BLOCK, BLOCK), jnp.bfloat16),
            pltpu.VMEM((COPIES, rights + 1, 8, BLOCK), jnp.float32),
            pltpu.VMEM((COPIES, rights + 1, 8, BLOCK), jnp.float32),
        ],
        compiler_params=PARAMS,
    )(*pairs, left, right, *bias)


def shape(dims, dtype=jnp.float32):
    return jax.ShapeDtypeStruct(dims, dtype)


def ring(values, axis, size, stride=1):
    places = lax.axis_size(axis)
    out = [values]
    for d in range(1, size):
        pairs = []
        for i in range(places):
            place = i // stride % size
            pairs.append((i, i + ((place + d) % size - place) * stride))
        out.append(lax.ppermute(values, axis, pairs))
    return out


def shards(
    source_points,
    source_logmass,
    target_points,
    target_logmass,
    target_potential,
    tile_slot,
    tile_counts,
    fetch_ids,
):
    peers = lax.axis_size("src")
    blocks = tile_counts.shape[0]
    per_peer = fetch_ids.shape[1]
    owned = target_potential.shape[0] // BLOCK
    count = peers * per_peer
    place = lax.axis_index("src")

    ids = jnp.stack(ring(fetch_ids, "src", peers))
    packed = pl.pallas_call(
        pack_kernel,
        out_shape=shape((count, D + EXTRA, BLOCK), jnp.bfloat16),
        in_specs=[SMEM, SMEM, VMEM, VMEM, VMEM],
        out_specs=VMEM,
        compiler_params=PARAMS,
    )(
        place.reshape(1),
        ids.reshape(-1),
        target_points.T,
        target_potential.reshape(owned, BLOCK),
        target_logmass.reshape(owned, BLOCK),
    )
    col_pairs, row_pairs = plan(tile_slot, tile_counts)
    points_right, points_left, source_half = pl.pallas_call(
        source_kernel,
        out_shape=[
            shape((blocks, 2 * D, BLOCK), jnp.bfloat16),
            shape((blocks, BLOCK, 2 * D), jnp.bfloat16),
            shape((blocks, BLOCK)),
        ],
        in_specs=[VMEM],
        out_specs=[VMEM] * 3,
        compiler_params=PARAMS,
    )(source_points.T)
    fetched = lax.all_to_all(packed, "src", split_axis=0, concat_axis=0, tiled=True)
    targets_left, potentials, slot_mass = pl.pallas_call(
        unpack_kernel,
        out_shape=[shape((count, BLOCK, 2 * D), jnp.bfloat16), shape((count, BLOCK)), shape((count, BLOCK))],
        in_specs=[VMEM],
        out_specs=[VMEM] * 3,
        compiler_params=PARAMS,
    )(fetched)
    source_mass = LOG2E * source_logmass.reshape(blocks, BLOCK)

    same = ids[:, :, None, :] == ids[0][None, :, :, None]
    same = same[:, :, :, None, :] & jnp.eye(peers, dtype=bool)[None, :, None, :, None]
    same = same.reshape(peers, count, 1, count) & jnp.eye(peers, dtype=bool)[:, None, :, None]
    chosen = same.reshape(peers * count, peers * count).astype(jnp.bfloat16)

    for sweep_index in range(ITERS):
        if sweep_index == 0:
            rows, _ = log_sums(row_pairs, targets_left, points_right, start_bias, [potentials], True)
        else:
            rows, _ = log_sums(
                row_pairs, targets_left, points_right, potential_bias, [*col_parts, chosen, slot_mass], True
            )
        rows = log_sum(ring(rows, "grp", 2, 1))
        rows = log_sum(ring(rows, "grp", 4, 2))
        row_parts = ring(rows, "grp", 4, 8)
        cols, field = log_sums(
            col_pairs, points_left, fetched, field_bias, [*row_parts, source_mass], False
        )
        if sweep_index < ITERS - 1:
            col_parts = ring(cols, "src", peers)
    source_field = field * (1.0 / SCALE) + source_half

    back = lax.all_to_all(
        cols.reshape(peers, per_peer, BLOCK), "src", split_axis=0, concat_axis=0, tiled=True
    )
    requested = jnp.take(
        lax.dynamic_slice(ids, (0, place, 0), (peers, 1, per_peer))[:, 0],
        lax.rem(place - jnp.arange(peers) + peers, peers),
        axis=0,
    )
    mine = jnp.arange(owned, dtype=jnp.int32)[:, None, None] == requested[None]
    parts = jnp.max(jnp.where(mine[..., None], back[None], LOWEST), axis=2)
    owned_pot = LOG2E * target_logmass.reshape(owned, BLOCK) - log_sum(
        [parts[:, s] for s in range(peers)]
    )
    target_half = 0.5 * jnp.sum(jnp.square(target_points.astype(jnp.float32)), -1)
    target_field = owned_pot.reshape(-1) * (1.0 / SCALE) + target_half
    return (source_field.reshape(-1), target_field)


def solution(mesh):
    return jax.shard_map(
        shards,
        mesh=mesh,
        in_specs=(
            P("src", None),
            P("src"),
            P(("src", "grp"), None),
            P(("src", "grp")),
            P(("src", "grp")),
            P("src", "grp"),
            P("src", "grp"),
            P("src", "grp"),
        ),
        out_specs=(P("src"), P(("src", "grp"))),
        check_vma=False,
    )
```

```python
import functools

import jax
import jax.numpy as jnp
from jax import lax
from jax.experimental import pallas as pl
from jax.experimental.pallas import tpu as pltpu
from jax.sharding import PartitionSpec as P

D = 64
BLOCK = 128
KG = 8
ITERS = 3
EPSILON = 0.25
LOWEST = -1e30
LOG2E = 1.4426950408889634
SCALE = LOG2E / EPSILON
PAIRS = 32
COPIES = 2
GROUP = 32
EXTRA = 16
HEAD = 4


SMEM = pl.BlockSpec(memory_space=pltpu.SMEM)
VMEM = pl.BlockSpec(memory_space=pltpu.VMEM)
PARAMS = pltpu.CompilerParams(vmem_limit_bytes=16 * 1024 * 1024)


def plan_kernel(half_ref, near_ref, far_ref, col_ref, row_ref, lists, sizes):
    halves = near_ref.shape[1] // 2
    slots = 2 * GROUP
    stride = halves + KG
    first = half_ref[0] * halves
    for q in range(slots):
        sizes[q] = 0

    def one_block(b, position):
        start = HEAD + 4 * position

        def place(slot, tile):
            col_ref[start + 4 * (tile // 2) + 1 + tile % 2] = slot

        def append(slot):
            size = sizes[slot]
            lists[slot * stride + size] = b
            sizes[slot] = size + 1

        tiles = jnp.int32(0)
        for group, ref in enumerate((near_ref, far_ref)):
            count = ref[KG, first + b]
            for k in range(2):
                slot = ref[k, first + b] + group * GROUP
                place(slot, tiles + k)
                append(slot)

            def more(k, carry, ref=ref, group=group, tiles=tiles):
                slot = ref[k, first + b] + group * GROUP
                place(slot, tiles + k)
                append(slot)
                return carry

            lax.fori_loop(2, count, more, 0)
            tiles = tiles + count
        place(slots, tiles)
        for k in range(KG):
            col_ref[start + 4 * k] = b
        return position + (tiles + 1) // 2

    def finish(ref, pairs, none):
        ref[0] = (pairs + PAIRS - 1) // PAIRS

        def pad(k, carry):
            at = HEAD + 4 * (pairs + k)
            ref[at] = 0
            ref[at + 1] = none
            ref[at + 2] = none
            return carry

        lax.fori_loop(0, ref[0] * PAIRS - pairs, pad, 0)

    finish(col_ref, lax.fori_loop(0, halves, one_block, jnp.int32(0)), slots)

    def one_slot(q, position):
        size = sizes[q]
        lists[q * stride + size] = halves

        def one_pair(k, carry):
            at = HEAD + 4 * (position + k)
            row_ref[at] = q
            row_ref[at + 1] = lists[q * stride + 2 * k]
            row_ref[at + 2] = lists[q * stride + 2 * k + 1]
            return carry

        lax.fori_loop(0, (size + 1) // 2, one_pair, 0)
        return position + (size + 1) // 2

    finish(row_ref, lax.fori_loop(0, slots, one_slot, jnp.int32(0)), halves)


def plan(half, near, far):
    halves = near.shape[1] // 2
    col_room = HEAD + 4 * (halves * KG + PAIRS + KG)
    row_room = HEAD + 4 * (halves * KG + 2 * GROUP + PAIRS)
    return pl.pallas_call(
        plan_kernel,
        out_shape=[shape((col_room,), jnp.int32), shape((row_room,), jnp.int32)],
        in_specs=[SMEM] * 3,
        out_specs=[SMEM] * 2,
        scratch_shapes=[
            pltpu.SMEM((2 * GROUP * (halves + KG),), jnp.int32),
            pltpu.SMEM((2 * GROUP,), jnp.int32),
        ],
    )(half.reshape(1), near, far)


def split3(values):
    high = values.astype(jnp.bfloat16)
    rest = values - high.astype(jnp.float32)
    middle = rest.astype(jnp.bfloat16)
    low = (rest - middle.astype(jnp.float32)).astype(jnp.bfloat16)
    return high, middle, low


def log_sum(values):
    top = functools.reduce(jnp.maximum, values)
    return top + jnp.log2(sum(jnp.exp2(value - top) for value in values))


def pack_kernel(place_ref, ids_ref, points_ref, potential_ref, logmass_ref, out_ref):
    place = place_ref[0]
    peers = ids_ref.shape[0] // out_ref.shape[0]
    per_peer = out_ref.shape[0] // peers
    for d in range(peers):
        other = lax.rem(place - d + peers, peers)

        def one_block(c, carry, d=d, other=other):
            t = ids_ref[(d * peers + place) * per_peer + c]
            block = points_ref[:, pl.ds(pl.multiple_of(t * BLOCK, BLOCK), BLOCK)]
            wide = block.astype(jnp.float32)
            norm = jnp.sum(wide * wide, axis=0, keepdims=True)
            start = SCALE * (potential_ref[pl.ds(t, 1), :] - 0.5 * norm)
            mass = LOG2E * logmass_ref[pl.ds(t, 1), :]
            rows = [part.astype(jnp.float32) for part in split3(start) + split3(mass)]
            rows.append(jnp.zeros((EXTRA - len(rows), BLOCK), jnp.float32))
            out_ref[other * per_peer + c, :D, :] = block
            out_ref[other * per_peer + c, D:, :] = jnp.concatenate(rows, axis=0).astype(jnp.bfloat16)
            return carry

        lax.fori_loop(0, per_peer, one_block, 0, unroll=4)


def unpack_kernel(near_ref, far_ref, right_ref, left_ref, start_ref, mass_ref):
    for group, in_ref in enumerate((near_ref, far_ref)):

        def one_block(q, carry, group=group, in_ref=in_ref):
            block = in_ref[q, :D, :]
            turned = block.T
            to = group * GROUP + q
            right_ref[to] = jnp.concatenate([block, block], axis=0)
            left_ref[to] = jnp.concatenate([turned, turned], axis=1)
            rows = in_ref[q, D:, :].astype(jnp.float32)
            start_ref[pl.ds(to, 1), :] = rows[0:1] + rows[1:2] + rows[2:3]
            mass_ref[pl.ds(to, 1), :] = rows[3:4] + rows[4:5] + rows[5:6]
            return carry

        lax.fori_loop(0, GROUP, one_block, 0, unroll=4)


def source_kernel(half_ref, points_ref, right_ref, left_ref, norm_ref):
    halves = right_ref.shape[0]
    first = half_ref[0] * halves

    def one_block(b, carry):
        at = pl.multiple_of((first + b) * BLOCK, BLOCK)
        wide = points_ref[:, pl.ds(at, BLOCK)].astype(jnp.float32)
        norm_ref[pl.ds(b, 1), :] = 0.5 * jnp.sum(wide * wide, axis=0, keepdims=True)
        scaled = SCALE * wide
        high = scaled.astype(jnp.bfloat16)
        low = (scaled - high.astype(jnp.float32)).astype(jnp.bfloat16)
        both = jnp.concatenate([high, low], axis=0)
        right_ref[b] = both
        left_ref[b] = both.T
        return carry

    lax.fori_loop(0, halves, one_block, 0, unroll=4)


def start_bias(start_ref):
    return start_ref[...]


def field_bias(near, *rest):
    *far, mass_ref = rest
    return mass_ref[...] - log_sum([near[...]] + [ref[...] for ref in far])


def potential_bias(near, *rest):
    *far, chosen_ref, mass_ref = rest
    refs = [near, *far]
    dot = functools.partial(jnp.dot, preferred_element_type=jnp.float32)
    out = []
    for group in range(2):
        own = slice(group * GROUP, (group + 1) * GROUP)
        chosen = chosen_ref[group]
        sums = jnp.concatenate([ref[own, :] for ref in refs], axis=0)
        parts = sum(dot(chosen, part) for part in split3(sums))
        known = dot(chosen, jnp.ones_like(chosen)) > 0.5
        parts = jnp.where(known, parts, LOWEST)
        merged = log_sum([parts[k * GROUP : (k + 1) * GROUP] for k in range(len(refs))])
        out.append(mass_ref[own, :] - merged)
    return jnp.concatenate(out, axis=0)


def pass_kernel(bias_of, bias_count, *refs):
    list_ref, left_ref, right_ref = refs[:3]
    bias_refs = refs[3 : 3 + bias_count]
    out_ref, bias_ref, columns, peaks, masses = refs[3 + bias_count :]
    lefts, rights = left_ref.shape[0], right_ref.shape[0]
    square = (BLOCK, BLOCK)
    lane = lax.broadcasted_iota(jnp.int32, square, 1)
    eye = jnp.where(lane == lax.broadcasted_iota(jnp.int32, square, 0), 1.0, 0.0).astype(jnp.bfloat16)
    lane = jnp.where(lane < 3 * GROUP, lane % GROUP, -1)
    bias_ref[...] = bias_of(*bias_refs)
    for group in range(lefts // GROUP):
        high, middle, low = split3(bias_ref[group * GROUP : (group + 1) * GROUP, :])
        parts = jnp.concatenate([high, middle, low, jnp.zeros_like(high)], axis=0)
        turned = lax.dot_general(
            eye, parts, (((1,), (1,)), ((), ())), preferred_element_type=jnp.float32
        )

        def fill(k, carry, group=group, turned=turned):
            columns[group * GROUP + k] = jnp.where(lane == k, turned, 0.0).astype(jnp.bfloat16)
            return carry

        lax.fori_loop(0, GROUP, fill, 0, unroll=4)
    peaks[...] = jnp.full_like(peaks, LOWEST)
    masses[...] = jnp.zeros_like(masses)
    ones = jnp.ones((BLOCK, 2 * BLOCK), jnp.bfloat16)

    def fold(copy, r, scores):
        scores = scores.reshape(BLOCK // 8, 8, BLOCK)
        old = peaks[copy, r]
        top = jnp.maximum(old, jnp.max(scores, axis=0))
        mass = jnp.sum(jnp.exp2(scores - top[None]), axis=0)
        masses[copy, r] = masses[copy, r] * jnp.exp2(old - top) + mass
        peaks[copy, r] = top

    def right_block(r):
        return right_ref[jnp.minimum(r, rights - 1)]

    def step(t, carry):
        for u in range(PAIRS):
            at = HEAD + 4 * (t * PAIRS + u)
            l, first, second = list_ref[at], list_ref[at + 1], list_ref[at + 2]
            left = jnp.concatenate([left_ref[l], columns[l]], axis=1)
            right = jnp.concatenate([right_block(first), right_block(second)], axis=1)
            scores = jnp.dot(
                left, jnp.concatenate([right, ones], axis=0), preferred_element_type=jnp.float32
            )
            fold((2 * u) % COPIES, first, scores[:, :BLOCK])
            fold((2 * u + 1) % COPIES, second, scores[:, BLOCK:])
        return carry

    lax.fori_loop(0, list_ref[0], step, 0)

    def finish(octet, carry):
        rows = []
        for k in range(8):
            r = octet * 8 + k
            tops = [peaks[copy, r] for copy in range(COPIES)]
            top = jnp.max(functools.reduce(jnp.maximum, tops), axis=0, keepdims=True)
            mass = sum(masses[copy, r] * jnp.exp2(tops[copy] - top) for copy in range(COPIES))
            rows.append(top + jnp.log2(jnp.sum(mass, axis=0, keepdims=True)))
        out_ref[pl.ds(pl.multiple_of(octet * 8, 8), 8), :] = jnp.concatenate(rows, axis=0)
        return carry

    lax.fori_loop(0, rights // 8, finish, 0)


def shape(dims, dtype=jnp.float32):
    return jax.ShapeDtypeStruct(dims, dtype)


def log_sums(pairs, left, right, bias_of, bias):
    lefts, rights = left.shape[0], right.shape[0]
    return pl.pallas_call(
        functools.partial(pass_kernel, bias_of, len(bias)),
        out_shape=[shape((rights, BLOCK)), shape((lefts, BLOCK))],
        in_specs=[SMEM] + [VMEM] * (2 + len(bias)),
        out_specs=[VMEM, VMEM],
        scratch_shapes=[
            pltpu.VMEM((lefts, BLOCK, BLOCK), jnp.bfloat16),
            pltpu.VMEM((COPIES, rights + 1, 8, BLOCK), jnp.float32),
            pltpu.VMEM((COPIES, rights + 1, 8, BLOCK), jnp.float32),
        ],
        compiler_params=PARAMS,
    )(pairs, left, right, *bias)


def ring(values, axis, size, stride=1):
    places = lax.axis_size(axis)
    out = [values]
    for d in range(1, size):
        pairs = []
        for i in range(places):
            place = i // stride % size
            pairs.append((i, i + ((place + d) % size - place) * stride))
        out.append(lax.ppermute(values, axis, pairs))
    return out


def shards(
    source_points,
    source_logmass,
    target_points,
    target_logmass,
    target_potential,
    tile_slot,
    tile_counts,
    fetch_ids,
):
    peers = lax.axis_size("src")
    blocks = tile_counts.shape[0]
    halves = blocks // 2
    per_peer = fetch_ids.shape[1]
    owned = target_potential.shape[0] // BLOCK
    count = peers * per_peer
    place = lax.axis_index("src")
    half = lax.axis_index("grp") % 2

    def swap(values):
        return ring(values, "grp", 2, 1)[1]

    tiles = jnp.concatenate([tile_slot.T, tile_counts.T], axis=0)
    ids = jnp.stack(ring(fetch_ids, "src", peers))
    col_pairs, row_pairs = plan(half, tiles, swap(tiles))
    ids, col_pairs, row_pairs = lax.optimization_barrier((ids, col_pairs, row_pairs))
    packed = pl.pallas_call(
        pack_kernel,
        out_shape=shape((count, D + EXTRA, BLOCK), jnp.bfloat16),
        in_specs=[SMEM, SMEM, VMEM, VMEM, VMEM],
        out_specs=VMEM,
        compiler_params=PARAMS,
    )(
        place.reshape(1),
        ids.reshape(-1),
        target_points.T,
        target_potential.reshape(owned, BLOCK),
        target_logmass.reshape(owned, BLOCK),
    )
    fetched = lax.all_to_all(packed, "src", split_axis=0, concat_axis=0, tiled=True)
    points_right, points_left, source_half = pl.pallas_call(
        source_kernel,
        out_shape=[
            shape((halves, 2 * D, BLOCK), jnp.bfloat16),
            shape((halves, BLOCK, 2 * D), jnp.bfloat16),
            shape((halves, BLOCK)),
        ],
        in_specs=[SMEM, VMEM],
        out_specs=[VMEM] * 3,
        compiler_params=PARAMS,
    )(half.reshape(1), source_points.T)
    targets_right, targets_left, potentials, slot_mass = pl.pallas_call(
        unpack_kernel,
        out_shape=[
            shape((2 * count, 2 * D, BLOCK), jnp.bfloat16),
            shape((2 * count, BLOCK, 2 * D), jnp.bfloat16),
            shape((2 * count, BLOCK)),
            shape((2 * count, BLOCK)),
        ],
        in_specs=[VMEM] * 2,
        out_specs=[VMEM] * 4,
        compiler_params=PARAMS,
    )(fetched, swap(fetched))
    source_mass = LOG2E * lax.dynamic_slice(
        source_logmass.reshape(blocks, BLOCK), (half * halves, 0), (halves, BLOCK)
    )

    all_ids = jnp.stack([ids, swap(ids)])
    same = all_ids[:, :, :, None, :] == all_ids[:, :1, :, :, None]
    same = same[:, :, :, :, None, :] & jnp.eye(peers, dtype=bool)[:, None, :, None]
    same = same.reshape(2, peers, count, 1, count) & jnp.eye(peers, dtype=bool)[:, None, :, None]
    chosen = same.reshape(2, peers * count, peers * count).astype(jnp.bfloat16)

    for sweep_index in range(ITERS):
        if sweep_index == 0:
            rows, _ = log_sums(row_pairs, targets_left, points_right, start_bias, [potentials])
        else:
            rows, _ = log_sums(
                row_pairs, targets_left, points_right, potential_bias, [*col_parts, chosen, slot_mass]
            )
        rows = log_sum(ring(rows, "grp", 4, 2))
        row_parts = ring(rows, "grp", 4, 8)
        cols, field = log_sums(col_pairs, points_left, targets_right, field_bias, [*row_parts, source_mass])
        if sweep_index < ITERS - 1:
            other = swap(cols)
            cols = log_sum([cols, jnp.concatenate([other[count:], other[:count]], axis=0)])
            col_parts = ring(cols, "src", peers)
    field = field * (1.0 / SCALE) + source_half
    other = swap(field)
    low = half == 0
    source_field = jnp.concatenate([jnp.where(low, field, other), jnp.where(low, other, field)], axis=0)

    cols = log_sum([cols[:count], swap(cols[count:])]).reshape(peers, per_peer, BLOCK)
    back, requested = [], []
    for d in range(peers):
        wanted = lax.dynamic_slice(cols, ((place + d) % peers, 0, 0), (1, per_peer, BLOCK))[0]
        pairs = [(i, (i + d) % peers) for i in range(peers)]
        back.append(wanted if d == 0 else lax.ppermute(wanted, "src", pairs))
        requested.append(lax.dynamic_slice(ids, (d, place, 0), (1, 1, per_peer))[0, 0])
    blocks_here = jnp.arange(owned, dtype=jnp.int32)[:, None]
    parts = [
        jnp.max(jnp.where((blocks_here == wants[None])[..., None], sums[None], LOWEST), axis=1)
        for wants, sums in zip(requested, back)
    ]
    owned_pot = LOG2E * target_logmass.reshape(owned, BLOCK) - log_sum(parts)
    target_half = 0.5 * jnp.sum(jnp.square(target_points.astype(jnp.float32)), -1)
    target_field = owned_pot.reshape(-1) * (1.0 / SCALE) + target_half
    return (source_field.reshape(-1), target_field)


def solution(mesh):
    return jax.shard_map(
        shards,
        mesh=mesh,
        in_specs=(
            P("src", None),
            P("src"),
            P(("src", "grp"), None),
            P(("src", "grp")),
            P(("src", "grp")),
            P("src", "grp"),
            P("src", "grp"),
            P("src", "grp"),
        ),
        out_specs=(P("src"), P(("src", "grp"))),
        check_vma=False,
    )
```

```python
import functools

import jax
import jax.numpy as jnp
from jax import lax
from jax.experimental import pallas as pl
from jax.experimental.pallas import tpu as pltpu
from jax.sharding import PartitionSpec as P

D = 64
BLOCK = 128
KG = 8
ITERS = 3
EPSILON = 0.25
LOWEST = -1e30
LOG2E = 1.4426950408889634
SCALE = LOG2E / EPSILON
PAIRS = 32
COPIES = 2
GROUP = 32
EXTRA = 16
HEAD = 8
STRIDE = 64


SMEM = pl.BlockSpec(memory_space=pltpu.SMEM)
VMEM = pl.BlockSpec(memory_space=pltpu.VMEM)
HBM = pl.BlockSpec(memory_space=pltpu.HBM)
PARAMS = pltpu.CompilerParams(vmem_limit_bytes=48 * 1024 * 1024)


def shape(dims, dtype=jnp.float32):
    return jax.ShapeDtypeStruct(dims, dtype)


def start_copies(pairs, sems):
    copies = [pltpu.make_async_copy(src, dst, sems.at[k]) for k, (src, dst) in enumerate(pairs)]
    for copy in copies:
        copy.start()
    return copies


def plan_kernel(half_ref, near_ref, far_ref, col_ref, row_ref, lists, sizes):
    halves = near_ref.shape[1] // 2
    slots = 2 * GROUP
    first = half_ref[0] * halves
    col_right = HEAD + (col_ref.shape[0] - HEAD) // 3
    row_right = HEAD + (row_ref.shape[0] - HEAD) // 3

    def clear(q, carry):
        sizes[q] = 0
        return carry

    lax.fori_loop(0, slots + 1, clear, 0, unroll=8)

    def one_block(b, position):
        at = col_right + 2 * position
        tiles = jnp.int32(0)
        for group, ref in enumerate((near_ref, far_ref)):
            count = ref[KG, first + b]
            named = [ref[k, first + b] + group * GROUP for k in range(KG)]
            for k in range(KG):
                col_ref[at + tiles + k] = named[k]
            named = [slot if k < 2 else jnp.where(k < count, slot, slots) for k, slot in enumerate(named)]
            known = [sizes[slot] for slot in named]
            for slot, size in zip(named, known):
                lists[slot * STRIDE + size] = b
            for slot, size in zip(named, known):
                sizes[slot] = size + 1
            tiles = tiles + count
        col_ref[at + tiles] = slots
        for k in range(KG):
            col_ref[HEAD + position + k] = b
        return position + (tiles + 1) // 2

    def finish(ref, right, pairs, none):
        ref[0] = (pairs + PAIRS - 1) // PAIRS

        def pad(k, carry):
            ref[HEAD + pairs + k] = 0
            ref[right + 2 * (pairs + k)] = none
            ref[right + 2 * (pairs + k) + 1] = none
            return carry

        lax.fori_loop(0, ref[0] * PAIRS - pairs, pad, 0)

    finish(col_ref, col_right, lax.fori_loop(0, halves, one_block, jnp.int32(0)), slots)

    def one_slot(q, position):
        size = sizes[q]
        lists[q * STRIDE + size] = halves
        pairs = (size + 1) // 2

        def one_pair(k, carry):
            row_ref[HEAD + position + k] = q
            for j in range(2):
                row_ref[row_right + 2 * (position + k) + j] = lists[q * STRIDE + 2 * k + j]
            return carry

        for k in range(4):
            one_pair(k, 0)
        lax.fori_loop(4, pairs, one_pair, 0)
        return position + pairs

    finish(row_ref, row_right, lax.fori_loop(0, slots, one_slot, jnp.int32(0)), halves)


def plan(half, near, far):
    halves = near.shape[1] // 2
    room = halves * KG + 2 * GROUP + PAIRS + KG
    return pl.pallas_call(
        plan_kernel,
        out_shape=[shape((HEAD + 3 * room,), jnp.int32)] * 2,
        in_specs=[SMEM] * 3,
        out_specs=[SMEM] * 2,
        scratch_shapes=[
            pltpu.SMEM(((2 * GROUP + 1) * STRIDE,), jnp.int32),
            pltpu.SMEM((2 * GROUP + 1,), jnp.int32),
        ],
    )(half.reshape(1), near, far)


def split3(values):
    high = values.astype(jnp.bfloat16)
    rest = values - high.astype(jnp.float32)
    middle = rest.astype(jnp.bfloat16)
    low = (rest - middle.astype(jnp.float32)).astype(jnp.bfloat16)
    return high, middle, low


def log_sum(values):
    top = functools.reduce(jnp.maximum, values)
    return top + jnp.log2(sum(jnp.exp2(value - top) for value in values))


def pack_kernel(place_ref, *refs):
    *ids_refs, points_hbm, potential_hbm, logmass_hbm, out_ref, points, potential, logmass, sems = refs
    copies = start_copies(
        [(potential_hbm, potential), (logmass_hbm, logmass), (points_hbm, points)], sems
    )
    place = place_ref[0]
    peers, per_peer = ids_refs[0].shape
    for copy in copies:
        copy.wait()
    for d, ids_ref in enumerate(ids_refs):
        other = lax.rem(place - d + peers, peers)

        def one_block(c, carry, ids_ref=ids_ref, other=other):
            t = ids_ref[place, c]
            block = points[:, pl.ds(pl.multiple_of(t * BLOCK, BLOCK), BLOCK)]
            wide = block.astype(jnp.float32)
            norm = jnp.sum(wide * wide, axis=0, keepdims=True)
            start = SCALE * (potential[pl.ds(t, 1), :] - 0.5 * norm)
            mass = LOG2E * logmass[pl.ds(t, 1), :]
            rows = [part.astype(jnp.float32) for part in split3(start) + split3(mass)]
            rows.append(jnp.zeros((EXTRA - len(rows), BLOCK), jnp.float32))
            out_ref[other * per_peer + c, :D, :] = block
            out_ref[other * per_peer + c, D:, :] = jnp.concatenate(rows, axis=0).astype(jnp.bfloat16)
            return carry

        lax.fori_loop(0, per_peer, one_block, 0, unroll=8)


def pack(place, ids, points, potential, logmass):
    count = ids[0].size
    return pl.pallas_call(
        pack_kernel,
        out_shape=shape((count, D + EXTRA, BLOCK), jnp.bfloat16),
        in_specs=[SMEM] * (1 + len(ids)) + [HBM] * 3,
        out_specs=VMEM,
        scratch_shapes=[
            pltpu.VMEM(points.shape, points.dtype),
            pltpu.VMEM(potential.shape, potential.dtype),
            pltpu.VMEM(logmass.shape, logmass.dtype),
            pltpu.SemaphoreType.DMA((3,)),
        ],
        compiler_params=PARAMS,
    )(place.reshape(1), *ids, points, potential, logmass)


def unpack_kernel(group, in_ref, *refs):
    outs, (right, left, start, mass, sems) = refs[-9:-5], refs[-5:]

    def one_block(q, carry):
        block = in_ref[q, :D, :]
        both = jnp.concatenate([block, block], axis=0)
        right[q] = both
        left[q] = both.T
        rows = in_ref[q, D:, :].astype(jnp.float32)
        start[pl.ds(q, 1), :] = rows[0:1] + rows[1:2] + rows[2:3]
        mass[pl.ds(q, 1), :] = rows[3:4] + rows[4:5] + rows[5:6]
        return carry

    lax.fori_loop(0, GROUP, one_block, 0, unroll=8)
    own = pl.ds(group * GROUP, GROUP)
    pairs = [(value, out.at[own]) for value, out in zip((right, left, start, mass), outs)]
    for copy in start_copies(pairs, sems):
        copy.wait()


def unpack(group, fetched, before):
    parts = [((BLOCK, BLOCK), jnp.bfloat16)] * 2 + [((BLOCK,), jnp.float32)] * 2
    return pl.pallas_call(
        functools.partial(unpack_kernel, group),
        out_shape=[shape((2 * GROUP, *dims), dtype) for dims, dtype in parts],
        in_specs=[VMEM] + [HBM] * len(before),
        out_specs=[HBM] * 4,
        scratch_shapes=[pltpu.VMEM((GROUP, *dims), dtype) for dims, dtype in parts]
        + [pltpu.SemaphoreType.DMA((4,))],
        input_output_aliases={1 + k: k for k in range(len(before))},
        compiler_params=PARAMS,
    )(fetched, *before)


def source_kernel(half_ref, points_hbm, right_hbm, left_hbm, norm_ref, points, right, left, sems):
    halves = right.shape[0]
    at = pl.multiple_of(half_ref[0] * (halves * BLOCK), halves * BLOCK)
    copy = pltpu.make_async_copy(points_hbm.at[:, pl.ds(at, halves * BLOCK)], points, sems.at[0])
    copy.start()
    copy.wait()

    def one_block(b, carry):
        wide = points[:, pl.ds(pl.multiple_of(b * BLOCK, BLOCK), BLOCK)].astype(jnp.float32)
        norm_ref[pl.ds(b, 1), :] = 0.5 * jnp.sum(wide * wide, axis=0, keepdims=True)
        scaled = SCALE * wide
        high = scaled.astype(jnp.bfloat16)
        low = (scaled - high.astype(jnp.float32)).astype(jnp.bfloat16)
        both = jnp.concatenate([high, low], axis=0)
        right[b] = both
        left[b] = both.T
        return carry

    lax.fori_loop(0, halves, one_block, 0, unroll=4)
    for copy in start_copies([(right, right_hbm), (left, left_hbm)], sems):
        copy.wait()


def source(half, halves, points):
    blocks = (halves, BLOCK, BLOCK)
    return pl.pallas_call(
        source_kernel,
        out_shape=[shape(blocks, jnp.bfloat16), shape(blocks, jnp.bfloat16), shape((halves, BLOCK))],
        in_specs=[SMEM, HBM],
        out_specs=[HBM, HBM, VMEM],
        scratch_shapes=[
            pltpu.VMEM((D, halves * BLOCK), jnp.bfloat16),
            pltpu.VMEM(blocks, jnp.bfloat16),
            pltpu.VMEM(blocks, jnp.bfloat16),
            pltpu.SemaphoreType.DMA((2,)),
        ],
        compiler_params=PARAMS,
    )(half.reshape(1), points)


def start_bias(start_ref):
    return start_ref[...]


def field_bias(mass_ref, *parts):
    return mass_ref[...] - log_sum([ref[...] for ref in parts])


def potential_bias(mass_ref, chosen_ref, *refs):
    dot = functools.partial(jnp.dot, preferred_element_type=jnp.float32)
    out = []
    for group in range(2):
        own = slice(group * GROUP, (group + 1) * GROUP)
        chosen = chosen_ref[group]
        sums = jnp.concatenate([ref[own, :] for ref in refs], axis=0)
        parts = sum(dot(chosen, part) for part in split3(sums))
        known = dot(chosen, jnp.ones_like(chosen)) > 0.5
        parts = jnp.where(known, parts, LOWEST)
        merged = log_sum([parts[k * GROUP : (k + 1) * GROUP] for k in range(len(refs))])
        out.append(mass_ref[own, :] - merged)
    return jnp.concatenate(out, axis=0)


def pass_kernel(bias_of, fixed_count, parts_count, *refs):
    remote_count = 3 + fixed_count
    remotes, refs = refs[:remote_count], refs[remote_count:]
    bias_parts, refs = refs[:parts_count], refs[parts_count:]
    out_ref, bias_ref, columns, peaks, masses, sems = refs[:6]
    locals_ = refs[6:]
    copies = start_copies(list(zip(remotes, locals_))[::-1], sems)
    list_ref, left_ref, right_ref, *fixed = locals_
    lefts, rights = left_ref.shape[0], right_ref.shape[0]
    square = (BLOCK, BLOCK)
    lane = lax.broadcasted_iota(jnp.int32, square, 1)
    eye = jnp.where(lane == lax.broadcasted_iota(jnp.int32, square, 0), 1.0, 0.0).astype(jnp.bfloat16)
    lane = jnp.where(lane < 3 * GROUP, lane % GROUP, -1)
    peaks[...] = jnp.full_like(peaks, LOWEST)
    masses[...] = jnp.zeros_like(masses)
    for copy in copies[:fixed_count]:
        copy.wait()
    bias_ref[...] = bias_of(*fixed, *bias_parts)
    for group in range(lefts // GROUP):
        high, middle, low = split3(bias_ref[group * GROUP : (group + 1) * GROUP, :])
        parts = jnp.concatenate([high, middle, low, jnp.zeros_like(high)], axis=0)
        turned = lax.dot_general(
            eye, parts, (((1,), (1,)), ((), ())), preferred_element_type=jnp.float32
        )

        def fill(k, carry, group=group, turned=turned):
            columns[group * GROUP + k] = jnp.where(lane == k, turned, 0.0).astype(jnp.bfloat16)
            return carry

        lax.fori_loop(0, GROUP, fill, 0, unroll=4)
    for copy in copies[fixed_count:]:
        copy.wait()
    rights_at = HEAD + (list_ref.shape[0] - HEAD) // 3
    ones = jnp.ones((BLOCK, 2 * BLOCK), jnp.bfloat16)

    def fold(copy, r, scores):
        scores = scores.reshape(BLOCK // 8, 8, BLOCK)
        old = peaks[copy, r]
        top = jnp.maximum(old, jnp.max(scores, axis=0))
        mass = jnp.sum(jnp.exp2(scores - top[None]), axis=0)
        masses[copy, r] = masses[copy, r] * jnp.exp2(old - top) + mass
        peaks[copy, r] = top

    def right_block(r):
        return right_ref[jnp.minimum(r, rights - 1)]

    def step(t, carry):
        for u in range(PAIRS):
            i = t * PAIRS + u
            l = list_ref[HEAD + i]
            first, second = list_ref[rights_at + 2 * i], list_ref[rights_at + 2 * i + 1]
            left = jnp.concatenate([left_ref[l], columns[l]], axis=1)
            right = jnp.concatenate([right_block(first), right_block(second)], axis=1)
            scores = jnp.dot(
                left, jnp.concatenate([right, ones], axis=0), preferred_element_type=jnp.float32
            )
            fold((2 * u) % COPIES, first, scores[:, :BLOCK])
            fold((2 * u + 1) % COPIES, second, scores[:, BLOCK:])
        return carry

    lax.fori_loop(0, list_ref[0], step, 0)

    def finish(octet, carry):
        rows = []
        for k in range(8):
            r = octet * 8 + k
            tops = [peaks[copy, r] for copy in range(COPIES)]
            top = jnp.max(functools.reduce(jnp.maximum, tops), axis=0, keepdims=True)
            mass = sum(masses[copy, r] * jnp.exp2(tops[copy] - top) for copy in range(COPIES))
            rows.append(top + jnp.log2(jnp.sum(mass, axis=0, keepdims=True)))
        out_ref[pl.ds(pl.multiple_of(octet * 8, 8), 8), :] = jnp.concatenate(rows, axis=0)
        return carry

    lax.fori_loop(0, rights // 8, finish, 0)


def log_sums(pairs, left, right, bias_of, fixed, parts):
    lefts, rights = left.shape[0], right.shape[0]
    remotes = [pairs, left, right, *fixed]
    return pl.pallas_call(
        functools.partial(pass_kernel, bias_of, len(fixed), len(parts)),
        out_shape=[shape((rights, BLOCK)), shape((lefts, BLOCK))],
        in_specs=[HBM] * len(remotes) + [VMEM] * len(parts),
        out_specs=[VMEM, VMEM],
        scratch_shapes=[
            pltpu.VMEM((lefts, BLOCK, BLOCK), jnp.bfloat16),
            pltpu.VMEM((COPIES, rights + 1, 8, BLOCK), jnp.float32),
            pltpu.VMEM((COPIES, rights + 1, 8, BLOCK), jnp.float32),
            pltpu.SemaphoreType.DMA((len(remotes),)),
            pltpu.SMEM(pairs.shape, pairs.dtype),
        ]
        + [pltpu.VMEM(value.shape, value.dtype) for value in remotes[1:]],
        compiler_params=PARAMS,
    )(*remotes, *parts)


def ring(values, axis, size, stride=1):
    places = lax.axis_size(axis)
    out = [values]
    for d in range(1, size):
        pairs = []
        for i in range(places):
            place = i // stride % size
            pairs.append((i, i + ((place + d) % size - place) * stride))
        out.append(lax.ppermute(values, axis, pairs))
    return out


def shards(
    source_points,
    source_logmass,
    target_points,
    target_logmass,
    target_potential,
    tile_slot,
    tile_counts,
    fetch_ids,
):
    peers = lax.axis_size("src")
    blocks = tile_counts.shape[0]
    halves = blocks // 2
    per_peer = fetch_ids.shape[1]
    owned = target_potential.shape[0] // BLOCK
    count = peers * per_peer
    place = lax.axis_index("src")
    half = lax.axis_index("grp") % 2

    def swap(values):
        return ring(values, "grp", 2, 1)[1]

    tiles = jnp.concatenate([tile_slot.T, tile_counts.T], axis=0)
    ids = ring(fetch_ids, "src", peers)
    packed = pack(
        place,
        ids,
        target_points.T,
        target_potential.reshape(owned, BLOCK),
        target_logmass.reshape(owned, BLOCK),
    )
    ids = jnp.stack(ids)
    col_pairs, row_pairs = plan(half, tiles, swap(tiles))
    fetched = lax.all_to_all(packed, "src", split_axis=0, concat_axis=0, tiled=True)
    points_right, points_left, source_half = source(half, halves, source_points.T)
    targets_right, targets_left, potentials, slot_mass = unpack(1, swap(fetched), unpack(0, fetched, []))
    source_mass = LOG2E * lax.dynamic_slice(
        source_logmass.reshape(blocks, BLOCK), (half * halves, 0), (halves, BLOCK)
    )

    all_ids = jnp.stack([ids, swap(ids)])
    same = all_ids[:, :, :, None, :] == all_ids[:, :1, :, :, None]
    same = same[:, :, :, :, None, :] & jnp.eye(peers, dtype=bool)[:, None, :, None]
    same = same.reshape(2, peers, count, 1, count) & jnp.eye(peers, dtype=bool)[:, None, :, None]
    chosen = same.reshape(2, peers * count, peers * count).astype(jnp.bfloat16)

    for sweep_index in range(ITERS):
        if sweep_index == 0:
            rows, _ = log_sums(row_pairs, targets_left, points_right, start_bias, [potentials], [])
        else:
            rows, _ = log_sums(
                row_pairs, targets_left, points_right, potential_bias, [slot_mass, chosen], col_parts
            )
        rows = log_sum(ring(rows, "grp", 4, 2))
        row_parts = ring(rows, "grp", 4, 8)
        cols, field = log_sums(col_pairs, points_left, targets_right, field_bias, [source_mass], row_parts)
        if sweep_index < ITERS - 1:
            other = swap(cols)
            cols = log_sum([cols, jnp.concatenate([other[count:], other[:count]], axis=0)])
            col_parts = ring(cols, "src", peers)
    field = field * (1.0 / SCALE) + source_half
    other = swap(field)
    low = half == 0
    source_field = jnp.concatenate([jnp.where(low, field, other), jnp.where(low, other, field)], axis=0)

    cols = log_sum([cols[:count], swap(cols[count:])]).reshape(peers, per_peer, BLOCK)
    back, requested = [], []
    for d in range(peers):
        wanted = lax.dynamic_slice(cols, ((place + d) % peers, 0, 0), (1, per_peer, BLOCK))[0]
        pairs = [(i, (i + d) % peers) for i in range(peers)]
        back.append(wanted if d == 0 else lax.ppermute(wanted, "src", pairs))
        requested.append(lax.dynamic_slice(ids, (d, place, 0), (1, 1, per_peer))[0, 0])
    blocks_here = jnp.arange(owned, dtype=jnp.int32)[:, None]
    parts = [
        jnp.max(jnp.where((blocks_here == wants[None])[..., None], sums[None], LOWEST), axis=1)
        for wants, sums in zip(requested, back)
    ]
    owned_pot = LOG2E * target_logmass.reshape(owned, BLOCK) - log_sum(parts)
    target_half = 0.5 * jnp.sum(jnp.square(target_points.astype(jnp.float32)), -1)
    target_field = owned_pot.reshape(-1) * (1.0 / SCALE) + target_half
    return (source_field.reshape(-1), target_field)


def solution(mesh):
    return jax.shard_map(
        shards,
        mesh=mesh,
        in_specs=(
            P("src", None),
            P("src"),
            P(("src", "grp"), None),
            P(("src", "grp")),
            P(("src", "grp")),
            P("src", "grp"),
            P("src", "grp"),
            P("src", "grp"),
        ),
        out_specs=(P("src"), P(("src", "grp"))),
        check_vma=False,
    )
```

```python
import functools

import jax
import jax.numpy as jnp
from jax import lax
from jax.experimental import pallas as pl
from jax.experimental.pallas import tpu as pltpu
from jax.sharding import PartitionSpec as P

D = 64
BLOCK = 128
KG = 8
ITERS = 3
EPSILON = 0.25
LOWEST = -1e30
LOG2E = 1.4426950408889634
SCALE = LOG2E / EPSILON
PAIRS = 32
TAIL = 16
COPIES = 2
GROUP = 32
EXTRA = 16
LEFT, RIGHT = 0, 1
HEAD = 8
STRIDE = 64


SMEM = pl.BlockSpec(memory_space=pltpu.SMEM)
VMEM = pl.BlockSpec(memory_space=pltpu.VMEM)
HBM = pl.BlockSpec(memory_space=pltpu.HBM)
MIB = 1024 * 1024
PREPARE = pltpu.CompilerParams(vmem_limit_bytes=64 * MIB)
PASS = pltpu.CompilerParams(vmem_limit_bytes=53 * MIB)


def shape(dims, dtype=jnp.float32):
    return jax.ShapeDtypeStruct(dims, dtype)


def start_copies(pairs, sems):
    copies = [pltpu.make_async_copy(src, dst, sems.at[k]) for k, (src, dst) in enumerate(pairs)]
    for copy in copies:
        copy.start()
    return copies


def plan_kernel(half_ref, near_ref, far_ref, col_ref, row_ref, lists, sizes):
    halves = near_ref.shape[1] // 2
    slots = 2 * GROUP
    first = half_ref[0] * halves
    col_right = HEAD + (col_ref.shape[0] - HEAD) // 3
    row_right = HEAD + (row_ref.shape[0] - HEAD) // 3

    def clear(q, carry):
        sizes[q] = 0
        return carry

    lax.fori_loop(0, slots + 1, clear, 0, unroll=8)

    def one_block(b, position):
        at = col_right + 2 * position
        tiles = jnp.int32(0)
        for group, ref in enumerate((near_ref, far_ref)):
            count = ref[KG, first + b]
            named = [ref[k, first + b] + group * GROUP for k in range(KG)]
            for k in range(KG):
                col_ref[at + tiles + k] = named[k]
            named = [slot if k < 2 else jnp.where(k < count, slot, slots) for k, slot in enumerate(named)]
            known = [sizes[slot] for slot in named]
            for slot, size in zip(named, known):
                lists[slot * STRIDE + size] = b
            for slot, size in zip(named, known):
                sizes[slot] = size + 1
            tiles = tiles + count
        col_ref[at + tiles] = slots
        for k in range(KG):
            col_ref[HEAD + position + k] = b
        return position + (tiles + 1) // 2

    def finish(ref, right, pairs, none):
        tails = (pairs + TAIL - 1) // TAIL
        ref[0] = tails // (PAIRS // TAIL)
        ref[1] = tails % (PAIRS // TAIL)

        def pad(k, carry):
            ref[HEAD + pairs + k] = 0
            ref[right + 2 * (pairs + k)] = none
            ref[right + 2 * (pairs + k) + 1] = none
            return carry

        lax.fori_loop(0, tails * TAIL - pairs, pad, 0)

    finish(col_ref, col_right, lax.fori_loop(0, halves, one_block, jnp.int32(0)), slots)

    def one_slot(q, position):
        size = sizes[q]
        lists[q * STRIDE + size] = halves
        pairs = (size + 1) // 2

        def one_pair(k, carry):
            row_ref[HEAD + position + k] = q
            for j in range(2):
                row_ref[row_right + 2 * (position + k) + j] = lists[q * STRIDE + 2 * k + j]
            return carry

        for k in range(4):
            one_pair(k, 0)
        lax.fori_loop(4, pairs, one_pair, 0)
        return position + pairs

    finish(row_ref, row_right, lax.fori_loop(0, slots, one_slot, jnp.int32(0)), halves)


def plan(half, near, far):
    halves = near.shape[1] // 2
    room = halves * KG + 2 * GROUP + PAIRS + KG
    return pl.pallas_call(
        plan_kernel,
        out_shape=[shape((HEAD + 3 * room,), jnp.int32)] * 2,
        in_specs=[SMEM] * 3,
        out_specs=[SMEM] * 2,
        scratch_shapes=[
            pltpu.SMEM(((2 * GROUP + 1) * STRIDE,), jnp.int32),
            pltpu.SMEM((2 * GROUP + 1,), jnp.int32),
        ],
    )(half.reshape(1), near, far)


def split3(values):
    high = values.astype(jnp.bfloat16)
    rest = values - high.astype(jnp.float32)
    middle = rest.astype(jnp.bfloat16)
    low = (rest - middle.astype(jnp.float32)).astype(jnp.bfloat16)
    return high, middle, low


def log_sum(values):
    top = functools.reduce(jnp.maximum, values)
    return top + jnp.log2(sum(jnp.exp2(value - top) for value in values))


def pack_kernel(place_ref, *refs):
    *ids_refs, points_hbm, potential_hbm, logmass_hbm, out_ref, points, potential, logmass, sems = refs
    copies = start_copies(
        [(potential_hbm, potential), (logmass_hbm, logmass), (points_hbm, points)], sems
    )
    place = place_ref[0]
    peers, per_peer = ids_refs[0].shape
    for copy in copies:
        copy.wait()
    for d, ids_ref in enumerate(ids_refs):
        other = lax.rem(place - d + peers, peers)

        def one_block(c, carry, ids_ref=ids_ref, other=other):
            t = ids_ref[place, c]
            block = points[:, pl.ds(pl.multiple_of(t * BLOCK, BLOCK), BLOCK)]
            wide = block.astype(jnp.float32)
            norm = jnp.sum(wide * wide, axis=0, keepdims=True)
            start = SCALE * (potential[pl.ds(t, 1), :] - 0.5 * norm)
            mass = LOG2E * logmass[pl.ds(t, 1), :]
            rows = [part.astype(jnp.float32) for part in split3(start) + split3(mass)]
            rows.append(jnp.zeros((EXTRA - len(rows), BLOCK), jnp.float32))
            out_ref[other * per_peer + c, :D, :] = block
            out_ref[other * per_peer + c, D:, :] = jnp.concatenate(rows, axis=0).astype(jnp.bfloat16)
            return carry

        lax.fori_loop(0, per_peer, one_block, 0, unroll=8)


def pack(place, ids, points, potential, logmass):
    count = ids[0].size
    return pl.pallas_call(
        pack_kernel,
        out_shape=shape((count, D + EXTRA, BLOCK), jnp.bfloat16),
        in_specs=[SMEM] * (1 + len(ids)) + [HBM] * 3,
        out_specs=VMEM,
        scratch_shapes=[
            pltpu.VMEM(points.shape, points.dtype),
            pltpu.VMEM(potential.shape, potential.dtype),
            pltpu.VMEM(logmass.shape, logmass.dtype),
            pltpu.SemaphoreType.DMA((3,)),
        ],
        compiler_params=PREPARE,
    )(place.reshape(1), *ids, points, potential, logmass)


def unpack_kernel(group, in_ref, *refs):
    outs, (blocks, start, mass, sems) = refs[-7:-4], refs[-4:]

    def one_block(q, carry):
        block = in_ref[q, :D, :]
        both = jnp.concatenate([block, block], axis=0)
        blocks[RIGHT, q] = both
        blocks[LEFT, q] = both.T
        rows = in_ref[q, D:, :].astype(jnp.float32)
        start[pl.ds(q, 1), :] = rows[0:1] + rows[1:2] + rows[2:3]
        mass[pl.ds(q, 1), :] = rows[3:4] + rows[4:5] + rows[5:6]
        return carry

    lax.fori_loop(0, GROUP, one_block, 0, unroll=8)
    own = pl.ds(group * GROUP, GROUP)
    pairs = [(blocks, outs[0].at[:, own]), (start, outs[1].at[own]), (mass, outs[2].at[own])]
    for copy in start_copies(pairs, sems):
        copy.wait()


def unpack(group, fetched, before):
    return pl.pallas_call(
        functools.partial(unpack_kernel, group),
        out_shape=[shape((2, 2 * GROUP, BLOCK, BLOCK), jnp.bfloat16)]
        + [shape((2 * GROUP, BLOCK))] * 2,
        in_specs=[VMEM] + [HBM] * len(before),
        out_specs=[HBM] * 3,
        scratch_shapes=[
            pltpu.VMEM((2, GROUP, BLOCK, BLOCK), jnp.bfloat16),
            pltpu.VMEM((GROUP, BLOCK), jnp.float32),
            pltpu.VMEM((GROUP, BLOCK), jnp.float32),
            pltpu.SemaphoreType.DMA((3,)),
        ],
        input_output_aliases={1 + k: k for k in range(len(before))},
        compiler_params=PREPARE,
    )(fetched, *before)


def source_kernel(half_ref, points_hbm, blocks_hbm, norm_ref, points, blocks, sems):
    halves = blocks.shape[1]
    at = pl.multiple_of(half_ref[0] * (halves * BLOCK), halves * BLOCK)
    copy = pltpu.make_async_copy(points_hbm.at[:, pl.ds(at, halves * BLOCK)], points, sems.at[0])
    copy.start()
    copy.wait()

    def one_block(b, carry):
        wide = points[:, pl.ds(pl.multiple_of(b * BLOCK, BLOCK), BLOCK)].astype(jnp.float32)
        norm_ref[pl.ds(b, 1), :] = 0.5 * jnp.sum(wide * wide, axis=0, keepdims=True)
        scaled = SCALE * wide
        high = scaled.astype(jnp.bfloat16)
        low = (scaled - high.astype(jnp.float32)).astype(jnp.bfloat16)
        both = jnp.concatenate([high, low], axis=0)
        blocks[RIGHT, b] = both
        blocks[LEFT, b] = both.T
        return carry

    lax.fori_loop(0, halves, one_block, 0, unroll=4)
    copy = pltpu.make_async_copy(blocks, blocks_hbm, sems.at[1])
    copy.start()
    copy.wait()


def source(half, halves, points):
    blocks = (2, halves, BLOCK, BLOCK)
    return pl.pallas_call(
        source_kernel,
        out_shape=[shape(blocks, jnp.bfloat16), shape((halves, BLOCK))],
        in_specs=[SMEM, HBM],
        out_specs=[HBM, VMEM],
        scratch_shapes=[
            pltpu.VMEM((D, halves * BLOCK), jnp.bfloat16),
            pltpu.VMEM(blocks, jnp.bfloat16),
            pltpu.SemaphoreType.DMA((2,)),
        ],
        compiler_params=PREPARE,
    )(half.reshape(1), points)


def start_bias(start_ref):
    return start_ref[...]


def field_bias(mass_ref, parts_ref):
    return mass_ref[...] - log_sum([parts_ref[k] for k in range(parts_ref.shape[0])])


def potential_bias(mass_ref, chosen_ref, *refs):
    dot = functools.partial(jnp.dot, preferred_element_type=jnp.float32)
    out = []
    for group in range(2):
        own = slice(group * GROUP, (group + 1) * GROUP)
        chosen = chosen_ref[group]
        sums = jnp.concatenate([ref[own, :] for ref in refs], axis=0)
        parts = sum(dot(chosen, part) for part in split3(sums))
        known = dot(chosen, jnp.ones_like(chosen)) > 0.5
        parts = jnp.where(known, parts, LOWEST)
        merged = log_sum([parts[k * GROUP : (k + 1) * GROUP] for k in range(len(refs))])
        out.append(mass_ref[own, :] - merged)
    return jnp.concatenate(out, axis=0)


def pass_kernel(bias_of, fixed_count, parts_count, *refs):
    remote_count = 3 + fixed_count
    remotes, refs = refs[:remote_count], refs[remote_count:]
    bias_parts, refs = refs[:parts_count], refs[parts_count:]
    out_ref, bias_ref, columns, peaks, masses, sems = refs[:6]
    locals_ = refs[6:]
    list_ref, left_ref, right_ref, *fixed = locals_
    sources = [remotes[0], remotes[1].at[LEFT], remotes[2].at[RIGHT], *remotes[3:]]
    copies = start_copies(list(zip(sources, locals_))[::-1], sems)
    lefts, rights = left_ref.shape[0], right_ref.shape[0]
    square = (BLOCK, BLOCK)
    lane = lax.broadcasted_iota(jnp.int32, square, 1)
    eye = jnp.where(lane == lax.broadcasted_iota(jnp.int32, square, 0), 1.0, 0.0).astype(jnp.bfloat16)
    lane = jnp.where(lane < 3 * GROUP, lane % GROUP, -1)
    peaks[...] = jnp.full_like(peaks, LOWEST)
    masses[...] = jnp.zeros_like(masses)
    for copy in copies[:fixed_count]:
        copy.wait()
    bias_ref[...] = bias_of(*fixed, *bias_parts)
    for group in range(lefts // GROUP):
        high, middle, low = split3(bias_ref[group * GROUP : (group + 1) * GROUP, :])
        parts = jnp.concatenate([high, middle, low, jnp.zeros_like(high)], axis=0)
        turned = lax.dot_general(
            eye, parts, (((1,), (1,)), ((), ())), preferred_element_type=jnp.float32
        )

        def fill(k, carry, group=group, turned=turned):
            columns[group * GROUP + k] = jnp.where(lane == k, turned, 0.0).astype(jnp.bfloat16)
            return carry

        lax.fori_loop(0, GROUP, fill, 0, unroll=4)
    for copy in copies[fixed_count:]:
        copy.wait()
    rights_at = HEAD + (list_ref.shape[0] - HEAD) // 3
    ones = jnp.ones((BLOCK, 2 * BLOCK), jnp.bfloat16)

    def fold(copy, r, scores):
        scores = scores.reshape(BLOCK // 8, 8, BLOCK)
        old = peaks[copy, r]
        top = jnp.maximum(old, jnp.max(scores, axis=0))
        mass = jnp.sum(jnp.exp2(scores - top[None]), axis=0)
        masses[copy, r] = masses[copy, r] * jnp.exp2(old - top) + mass
        peaks[copy, r] = top

    def right_block(r):
        return right_ref[jnp.minimum(r, rights - 1)]

    def step(start, count, t, carry):
        for u in range(count):
            i = start + t * count + u
            l = list_ref[HEAD + i]
            first, second = list_ref[rights_at + 2 * i], list_ref[rights_at + 2 * i + 1]
            left = jnp.concatenate([left_ref[l], columns[l]], axis=1)
            right = jnp.concatenate([right_block(first), right_block(second)], axis=1)
            scores = jnp.dot(
                left, jnp.concatenate([right, ones], axis=0), preferred_element_type=jnp.float32
            )
            fold((2 * u) % COPIES, first, scores[:, :BLOCK])
            fold((2 * u + 1) % COPIES, second, scores[:, BLOCK:])
        return carry

    lax.fori_loop(0, list_ref[0], functools.partial(step, 0, PAIRS), 0)
    lax.fori_loop(0, list_ref[1], functools.partial(step, list_ref[0] * PAIRS, TAIL), 0)

    def finish(octet, carry):
        rows = []
        for k in range(8):
            r = octet * 8 + k
            tops = [peaks[copy, r] for copy in range(COPIES)]
            top = jnp.max(functools.reduce(jnp.maximum, tops), axis=0, keepdims=True)
            mass = sum(masses[copy, r] * jnp.exp2(tops[copy] - top) for copy in range(COPIES))
            rows.append(top + jnp.log2(jnp.sum(mass, axis=0, keepdims=True)))
        out_ref[0, pl.ds(pl.multiple_of(octet * 8, 8), 8), :] = jnp.concatenate(rows, axis=0)
        return carry

    lax.fori_loop(0, rights // 8, finish, 0)
    for k in range(1, out_ref.shape[0]):
        out_ref[k] = out_ref[0]


def log_sums(pairs, left, right, bias_of, fixed, parts, copies):
    lefts, rights = left.shape[1], right.shape[1]
    remotes = [pairs, left, right, *fixed]
    return pl.pallas_call(
        functools.partial(pass_kernel, bias_of, len(fixed), len(parts)),
        out_shape=[shape((copies, rights, BLOCK)), shape((lefts, BLOCK))],
        in_specs=[HBM] * len(remotes) + [VMEM] * len(parts),
        out_specs=[VMEM, VMEM],
        scratch_shapes=[
            pltpu.VMEM((lefts, BLOCK, BLOCK), jnp.bfloat16),
            pltpu.VMEM((COPIES, rights + 1, 8, BLOCK), jnp.float32),
            pltpu.VMEM((COPIES, rights + 1, 8, BLOCK), jnp.float32),
            pltpu.SemaphoreType.DMA((len(remotes),)),
            pltpu.SMEM(pairs.shape, pairs.dtype),
            pltpu.VMEM(left.shape[1:], left.dtype),
            pltpu.VMEM(right.shape[1:], right.dtype),
        ]
        + [pltpu.VMEM(value.shape, value.dtype) for value in fixed],
        compiler_params=PASS,
    )(*remotes, *parts)


def ring(values, axis, size, stride=1):
    places = lax.axis_size(axis)
    out = [values]
    for d in range(1, size):
        pairs = []
        for i in range(places):
            place = i // stride % size
            pairs.append((i, i + ((place + d) % size - place) * stride))
        out.append(lax.ppermute(values, axis, pairs))
    return out


def shards(
    source_points,
    source_logmass,
    target_points,
    target_logmass,
    target_potential,
    tile_slot,
    tile_counts,
    fetch_ids,
):
    peers = lax.axis_size("src")
    blocks = tile_counts.shape[0]
    halves = blocks // 2
    per_peer = fetch_ids.shape[1]
    owned = target_potential.shape[0] // BLOCK
    count = peers * per_peer
    place = lax.axis_index("src")
    half = lax.axis_index("grp") % 2

    def swap(values):
        return ring(values, "grp", 2, 1)[1]

    tiles = jnp.concatenate([tile_slot.T, tile_counts.T], axis=0)
    ids = ring(fetch_ids, "src", peers)
    packed = pack(
        place,
        ids,
        target_points.T,
        target_potential.reshape(owned, BLOCK),
        target_logmass.reshape(owned, BLOCK),
    )
    ids = jnp.stack(ids)
    col_pairs, row_pairs = plan(half, tiles, swap(tiles))
    fetched = lax.all_to_all(packed, "src", split_axis=0, concat_axis=0, tiled=True)
    points, source_half = source(half, halves, source_points.T)
    fetched, points, col_pairs, row_pairs = lax.optimization_barrier((fetched, points, col_pairs, row_pairs))
    targets, potentials, slot_mass = unpack(1, swap(fetched), unpack(0, fetched, []))
    source_mass = LOG2E * lax.dynamic_slice(
        source_logmass.reshape(blocks, BLOCK), (half * halves, 0), (halves, BLOCK)
    )

    all_ids = jnp.stack([ids, swap(ids)])
    same = all_ids[:, :, :, None, :] == all_ids[:, :1, :, :, None]
    same = same[:, :, :, :, None, :] & jnp.eye(peers, dtype=bool)[:, None, :, None]
    same = same.reshape(2, peers, count, 1, count) & jnp.eye(peers, dtype=bool)[:, None, :, None]
    chosen = same.reshape(2, peers * count, peers * count).astype(jnp.bfloat16)

    groups = lax.axis_size("grp")
    same_core = [list(range(core, groups, 2)) for core in range(2)]
    for sweep_index in range(ITERS):
        if sweep_index == 0:
            bias_of, fixed, parts = start_bias, [potentials], []
        else:
            bias_of, fixed, parts = potential_bias, [slot_mass, chosen], col_parts
        rows, _ = log_sums(row_pairs, targets, points, bias_of, fixed, parts, groups // 2)
        rows = lax.all_to_all(
            rows, "grp", split_axis=0, concat_axis=0, tiled=True, axis_index_groups=same_core
        )
        cols, field = log_sums(col_pairs, points, targets, field_bias, [source_mass], [rows], 1)
        cols = cols[0]
        if sweep_index < ITERS - 1:
            other = swap(cols)
            cols = log_sum([cols, jnp.concatenate([other[count:], other[:count]], axis=0)])
            col_parts = ring(cols, "src", peers)
    field = field * (1.0 / SCALE) + source_half
    other = swap(field)
    low = half == 0
    source_field = jnp.concatenate([jnp.where(low, field, other), jnp.where(low, other, field)], axis=0)

    cols = log_sum([cols[:count], swap(cols[count:])]).reshape(peers, per_peer, BLOCK)
    back, requested = [], []
    for d in range(peers):
        wanted = lax.dynamic_slice(cols, ((place + d) % peers, 0, 0), (1, per_peer, BLOCK))[0]
        pairs = [(i, (i + d) % peers) for i in range(peers)]
        back.append(wanted if d == 0 else lax.ppermute(wanted, "src", pairs))
        requested.append(lax.dynamic_slice(ids, (d, place, 0), (1, 1, per_peer))[0, 0])
    blocks_here = jnp.arange(owned, dtype=jnp.int32)[:, None]
    parts = [
        jnp.max(jnp.where((blocks_here == wants[None])[..., None], sums[None], LOWEST), axis=1)
        for wants, sums in zip(requested, back)
    ]
    owned_pot = LOG2E * target_logmass.reshape(owned, BLOCK) - log_sum(parts)
    target_half = 0.5 * jnp.sum(jnp.square(target_points.astype(jnp.float32)), -1)
    target_field = owned_pot.reshape(-1) * (1.0 / SCALE) + target_half
    return (source_field.reshape(-1), target_field)


def solution(mesh):
    return jax.shard_map(
        shards,
        mesh=mesh,
        in_specs=(
            P("src", None),
            P("src"),
            P(("src", "grp"), None),
            P(("src", "grp")),
            P(("src", "grp")),
            P("src", "grp"),
            P("src", "grp"),
            P("src", "grp"),
        ),
        out_specs=(P("src"), P(("src", "grp"))),
        check_vma=False,
    )
```

```python
import functools

import jax
import jax.numpy as jnp
from jax import lax
from jax.experimental import pallas as pl
from jax.experimental.pallas import tpu as pltpu
from jax.sharding import PartitionSpec as P

D = 64
BLOCK = 128
KG = 8
ITERS = 3
EPSILON = 0.25
LOWEST = -1e30
LOG2E = 1.4426950408889634
SCALE = LOG2E / EPSILON
PAIRS = 32
TAIL = 16
COPIES = 2
GROUP = 32
EXTRA = 16
LEFT, RIGHT = 0, 1
FIRST, ROWS, COLUMNS = 0, 1, 2
PARTS = 4
LONG = 1024 * 1024
HEAD = 8
STRIDE = 64


SMEM = pl.BlockSpec(memory_space=pltpu.SMEM)
VMEM = pl.BlockSpec(memory_space=pltpu.VMEM)
HBM = pl.BlockSpec(memory_space=pltpu.HBM)
MIB = 1024 * 1024
PREPARE = pltpu.CompilerParams(vmem_limit_bytes=64 * MIB)
PASS = pltpu.CompilerParams(vmem_limit_bytes=53 * MIB)


def shape(dims, dtype=jnp.float32):
    return jax.ShapeDtypeStruct(dims, dtype)


def start_copies(pairs, sems):
    copies = [pltpu.make_async_copy(src, dst, sems.at[k]) for k, (src, dst) in enumerate(pairs)]
    for copy in copies:
        copy.start()
    return copies


def plan_kernel(half_ref, near_ref, far_ref, col_hbm, row_hbm, col_ref, row_ref, lists, sizes, sems):
    halves = near_ref.shape[1] // 2
    slots = 2 * GROUP
    first = half_ref[0] * halves
    col_right = HEAD + (col_ref.shape[0] - HEAD) // 3
    row_right = HEAD + (row_ref.shape[0] - HEAD) // 3

    def clear(q, carry):
        sizes[q] = 0
        return carry

    lax.fori_loop(0, slots + 1, clear, 0, unroll=8)

    def one_block(b, position):
        at = col_right + 2 * position
        tiles = jnp.int32(0)
        for group, ref in enumerate((near_ref, far_ref)):
            count = ref[KG, first + b]

            def some(start, stop, ref=ref, group=group, tiles=tiles, count=count):
                named = [ref[k, first + b] + group * GROUP for k in range(start, stop)]
                for k, slot in enumerate(named, start):
                    col_ref[at + tiles + k] = slot
                if start >= 2:
                    named = [jnp.where(k < count, slot, slots) for k, slot in enumerate(named, start)]
                known = [sizes[slot] for slot in named]
                for slot, size in zip(named, known):
                    lists[slot * STRIDE + size] = b
                for slot, size in zip(named, known):
                    sizes[slot] = size + 1

            some(0, 2)
            pl.when(count > 2)(functools.partial(some, 2, KG))
            tiles = tiles + count
        col_ref[at + tiles] = slots
        for k in range(KG):
            col_ref[HEAD + position + k] = b
        return position + (tiles + 1) // 2

    def finish(ref, right, pairs, last, none):
        tails = (pairs + TAIL - 1) // TAIL
        ref[0] = tails // (PAIRS // TAIL)
        ref[1] = tails % (PAIRS // TAIL)

        def pad(k, carry):
            ref[HEAD + pairs + k] = last
            ref[right + 2 * (pairs + k)] = none
            ref[right + 2 * (pairs + k) + 1] = none
            return carry

        lax.fori_loop(0, tails * TAIL - pairs, pad, 0)

    finish(col_ref, col_right, lax.fori_loop(0, halves, one_block, jnp.int32(0)), halves - 1, slots)

    def one_slot(q, position):
        size = sizes[q]
        lists[q * STRIDE + size] = halves
        pairs = (size + 1) // 2

        def one_pair(k, carry):
            row_ref[HEAD + position + k] = q
            for j in range(2):
                row_ref[row_right + 2 * (position + k) + j] = lists[q * STRIDE + 2 * k + j]
            return carry

        def more():
            for k in range(1, 4):
                one_pair(k, 0)
            lax.fori_loop(4, pairs, one_pair, 0)

        one_pair(0, 0)
        pl.when(pairs > 1)(more)
        return position + pairs

    finish(row_ref, row_right, lax.fori_loop(0, slots, one_slot, jnp.int32(0)), slots - 1, halves)
    pairs = [(ref, hbm.at[pl.ds(0, ref.shape[0])]) for ref, hbm in ((col_ref, col_hbm), (row_ref, row_hbm))]
    for copy in start_copies(pairs, sems):
        copy.wait()


def list_shape(halves):
    room = HEAD + 3 * (halves * KG + 2 * GROUP + PAIRS + KG)
    return ((room + 1023) // 1024 * 1024,)


def plan(half, near, far):
    dims = list_shape(near.shape[1] // 2)
    return pl.pallas_call(
        plan_kernel,
        out_shape=[shape((LONG,), jnp.int32)] * 2,
        in_specs=[SMEM] * 3,
        out_specs=[HBM] * 2,
        scratch_shapes=[
            pltpu.SMEM(dims, jnp.int32),
            pltpu.SMEM(dims, jnp.int32),
            pltpu.SMEM(((2 * GROUP + 1) * STRIDE,), jnp.int32),
            pltpu.SMEM((2 * GROUP + 1,), jnp.int32),
            pltpu.SemaphoreType.DMA((2,)),
        ],
        compiler_params=PREPARE,
    )(half.reshape(1), near, far)


def split3(values):
    high = values.astype(jnp.bfloat16)
    rest = values - high.astype(jnp.float32)
    middle = rest.astype(jnp.bfloat16)
    low = (rest - middle.astype(jnp.float32)).astype(jnp.bfloat16)
    return high, middle, low


def whole(parts):
    high, middle, low = [part.astype(jnp.float32) for part in parts]
    return high + middle + low


def log_sum(values):
    top = functools.reduce(jnp.maximum, values)
    return top + jnp.log2(sum(jnp.exp2(value - top) for value in values))


def pack_kernel(place_ref, *refs):
    count = (len(refs) - 2) // 2
    remotes, (out_ref, *locals_, sems) = refs[:count], refs[count:]
    *ids_refs, points, potential, logmass = locals_
    copies = start_copies(list(zip(remotes, locals_)), sems)
    place = place_ref[0]
    peers, per_peer = ids_refs[0].shape
    for copy in copies:
        copy.wait()
    for d, ids_ref in enumerate(ids_refs):
        other = lax.rem(place - d + peers, peers)

        def one_block(c, carry, ids_ref=ids_ref, other=other):
            t = ids_ref[place, c]
            block = points[:, pl.ds(pl.multiple_of(t * BLOCK, BLOCK), BLOCK)]
            wide = block.astype(jnp.float32)
            norm = jnp.sum(wide * wide, axis=0, keepdims=True)
            start = SCALE * (potential[pl.ds(t, 1), :] - 0.5 * norm)
            mass = LOG2E * logmass[pl.ds(t, 1), :]
            rows = [part.astype(jnp.float32) for part in split3(start) + split3(mass)]
            rows.append(jnp.zeros((EXTRA - len(rows), BLOCK), jnp.float32))
            out_ref[other * per_peer + c, :D, :] = block
            out_ref[other * per_peer + c, D:, :] = jnp.concatenate(rows, axis=0).astype(jnp.bfloat16)
            return carry

        lax.fori_loop(0, per_peer, one_block, 0, unroll=8)


def pack(place, ids, *values):
    remotes = [*ids, *values]
    return pl.pallas_call(
        pack_kernel,
        out_shape=shape((ids[0].size, D + EXTRA, BLOCK), jnp.bfloat16),
        in_specs=[SMEM] + [HBM] * len(remotes),
        out_specs=VMEM,
        scratch_shapes=[pltpu.SMEM(value.shape, value.dtype) for value in ids]
        + [pltpu.VMEM(value.shape, value.dtype) for value in values]
        + [pltpu.SemaphoreType.DMA((len(remotes),))],
        compiler_params=PREPARE,
    )(place.reshape(1), *remotes)


def source_kernel(half_ref, points_hbm, logmass_hbm, blocks_hbm, norm_ref, points, logmass, blocks, sems):
    halves = blocks.shape[1] - 1
    rows = pl.ds(pl.multiple_of(half_ref[0] * halves, halves), halves)
    at = pl.multiple_of(half_ref[0] * (halves * BLOCK), halves * BLOCK)
    pairs = [(points_hbm.at[:, pl.ds(at, halves * BLOCK)], points), (logmass_hbm.at[rows], logmass)]
    for copy in start_copies(pairs, sems):
        copy.wait()
    parts = split3(LOG2E * logmass[...])
    blocks[LEFT, halves] = jnp.concatenate([*parts, jnp.zeros_like(parts[0])], axis=0)
    blocks[RIGHT, halves] = jnp.zeros((BLOCK, BLOCK), jnp.bfloat16)

    def one_block(b, carry):
        wide = points[:, pl.ds(pl.multiple_of(b * BLOCK, BLOCK), BLOCK)].astype(jnp.float32)
        norm_ref[pl.ds(b, 1), :] = 0.5 * jnp.sum(wide * wide, axis=0, keepdims=True)
        scaled = SCALE * wide
        high = scaled.astype(jnp.bfloat16)
        low = (scaled - high.astype(jnp.float32)).astype(jnp.bfloat16)
        both = jnp.concatenate([high, low], axis=0)
        blocks[RIGHT, b] = both
        blocks[LEFT, b] = both.T
        return carry

    lax.fori_loop(0, halves, one_block, 0, unroll=4)
    copy = pltpu.make_async_copy(blocks, blocks_hbm, sems.at[0])
    copy.start()
    copy.wait()


def source(half, halves, points, logmass):
    blocks = (2, halves + 1, BLOCK, BLOCK)
    return pl.pallas_call(
        source_kernel,
        out_shape=[shape(blocks, jnp.bfloat16), shape((halves, BLOCK))],
        in_specs=[SMEM, HBM, HBM],
        out_specs=[HBM, VMEM],
        scratch_shapes=[
            pltpu.VMEM((D, halves * BLOCK), jnp.bfloat16),
            pltpu.VMEM((halves, BLOCK), jnp.float32),
            pltpu.VMEM(blocks, jnp.bfloat16),
            pltpu.SemaphoreType.DMA((2,)),
        ],
        compiler_params=PREPARE,
    )(half.reshape(1), points, logmass)


def field_bias(mass_ref, parts_ref):
    rows = parts_ref.shape[1]
    mass = whole([mass_ref[k * rows : (k + 1) * rows, :] for k in range(3)])
    return mass - log_sum([parts_ref[k] for k in range(parts_ref.shape[0])])


def potential_bias(mass_ref, chosen_ref, *refs):
    dot = functools.partial(jnp.dot, preferred_element_type=jnp.float32)
    mass = whole([mass_ref[0, : 2 * GROUP, :], mass_ref[0, 2 * GROUP :, :], mass_ref[1, : 2 * GROUP, :]])
    out = []
    for group in range(2):
        own = slice(group * GROUP, (group + 1) * GROUP)
        chosen = chosen_ref[group]
        sums = jnp.concatenate([ref[own, :] for ref in refs], axis=0)
        parts = sum(dot(chosen, part) for part in split3(sums))
        known = dot(chosen, jnp.ones_like(chosen)) > 0.5
        parts = jnp.where(known, parts, LOWEST)
        merged = log_sum([parts[k * GROUP : (k + 1) * GROUP] for k in range(len(refs))])
        out.append(mass[own, :] - merged)
    return jnp.concatenate(out, axis=0)


def unpack(raw, left, start_ref, mass_ref):
    def one_block(q, carry):
        block = raw[q, :D, :]
        left[q] = jnp.concatenate([block, block], axis=0).T
        rows = raw[q, D:, :].astype(jnp.float32)
        start_ref[pl.ds(q, 1), :] = rows[0:1] + rows[1:2] + rows[2:3]
        mass_ref[pl.ds(q, 1), :] = rows[3:4] + rows[4:5] + rows[5:6]
        return carry

    return lambda group: lax.fori_loop(group * GROUP, (group + 1) * GROUP, one_block, 0, unroll=8)


def pass_kernel(kind, *refs):
    columns, peaks, masses, list_ref, left_ref, right_ref, sems = refs[-7:]
    lefts, rights = columns.shape[0], right_ref.shape[0]
    part = lefts // PARTS
    left_parts = []
    if kind == FIRST:
        list_hbm, near_hbm, far_hbm, points_hbm, out_ref, left_hbm, mass_ref, bias_ref, raw = refs[:-7]
        early = [(near_hbm, raw.at[pl.ds(0, GROUP)]), (far_hbm, raw.at[pl.ds(GROUP, GROUP)])]
        late = [(points_hbm.at[RIGHT, pl.ds(0, rights)], right_ref)]
    elif kind == ROWS:
        list_hbm, left_hbm, points_hbm, chosen_hbm = refs[:4]
        *col_parts, out_ref, bias_ref, mass, chosen = refs[4:-7]
        early = [(left_hbm.at[pl.ds(lefts, 2)], mass), (chosen_hbm, chosen)]
        late = [(points_hbm.at[RIGHT, pl.ds(0, rights)], right_ref)]
        left_parts = [left_hbm.at[pl.ds(k * part, part)] for k in range(PARTS)]
    else:
        list_hbm, near_hbm, far_hbm, points_hbm, rows_ref, out_ref, bias_ref, mass = refs[:-7]
        early = [(points_hbm.at[LEFT, lefts], mass)]
        late = [(near_hbm, right_ref.at[pl.ds(0, GROUP)]), (far_hbm, right_ref.at[pl.ds(GROUP, GROUP)])]
        left_parts = [points_hbm.at[LEFT, pl.ds(k * part, part)] for k in range(PARTS)]
    late.append((list_hbm.at[pl.ds(0, list_ref.shape[0])], list_ref))
    pairs = early + late + [(ref, left_ref.at[pl.ds(k * part, part)]) for k, ref in enumerate(left_parts)]
    copies = start_copies(pairs, sems)
    peaks[...] = jnp.full_like(peaks, LOWEST)
    masses[...] = jnp.zeros_like(masses)
    for copy in copies[: len(early)]:
        copy.wait()
    if kind == FIRST:
        unpack_group = unpack(raw, left_ref, bias_ref, mass_ref)
        for group in range(2):
            unpack_group(group)
        high, middle, low = split3(mass_ref[...])
        left_ref[lefts] = jnp.concatenate([high, middle], axis=0)
        left_ref[lefts + 1] = jnp.concatenate([low, jnp.zeros_like(low)], axis=0)
        hand_on = pltpu.make_async_copy(left_ref, left_hbm, sems.at[len(pairs)])
        hand_on.start()
    elif kind == ROWS:
        bias_ref[...] = potential_bias(mass, chosen, *col_parts)
    else:
        bias_ref[...] = field_bias(mass, rows_ref)
    square = (BLOCK, BLOCK)
    lane = lax.broadcasted_iota(jnp.int32, square, 1)
    eye = jnp.where(lane == lax.broadcasted_iota(jnp.int32, square, 0), 1.0, 0.0).astype(jnp.bfloat16)
    lane = jnp.where(lane < 3 * GROUP, lane % GROUP, -1)
    for group in range(lefts // GROUP):
        high, middle, low = split3(bias_ref[group * GROUP : (group + 1) * GROUP, :])
        parts = jnp.concatenate([high, middle, low, jnp.zeros_like(high)], axis=0)
        turned = lax.dot_general(
            eye, parts, (((1,), (1,)), ((), ())), preferred_element_type=jnp.float32
        )

        def fill(k, carry, group=group, turned=turned):
            columns[group * GROUP + k] = jnp.where(lane == k, turned, 0.0).astype(jnp.bfloat16)
            return carry

        lax.fori_loop(0, GROUP, fill, 0, unroll=4)
    for copy in copies[len(early) : len(early) + len(late)]:
        copy.wait()
    rights_at = HEAD + (list_ref.shape[0] - HEAD) // 3
    ones = jnp.ones((BLOCK, 2 * BLOCK), jnp.bfloat16)

    def fold(copy, r, scores):
        scores = scores.reshape(BLOCK // 8, 8, BLOCK)
        old = peaks[copy, r]
        top = jnp.maximum(old, jnp.max(scores, axis=0))
        mass = jnp.sum(jnp.exp2(scores - top[None]), axis=0)
        masses[copy, r] = masses[copy, r] * jnp.exp2(old - top) + mass
        peaks[copy, r] = top

    def right_block(r):
        r = jnp.minimum(r, rights - 1)
        if kind != COLUMNS:
            return right_ref[r]
        block = right_ref[r, :D, :]
        return jnp.concatenate([block, block], axis=0)

    def wait_for(known, needed):
        if not left_parts:
            return known

        def wait(k, carry):
            at = pl.ds(k * part, part)
            source = left_hbm.at[at] if kind == ROWS else points_hbm.at[LEFT, at]
            pltpu.make_async_copy(source, left_ref.at[at], sems.at[len(early) + len(late) + k]).wait()
            return carry

        lax.fori_loop(known, needed, wait, 0)
        return jnp.maximum(known, needed)

    def step(start, count, t, known):
        known = wait_for(known, list_ref[HEAD + start + t * count + count - 1] // part + 1)
        for u in range(count):
            i = start + t * count + u
            l = list_ref[HEAD + i]
            first, second = list_ref[rights_at + 2 * i], list_ref[rights_at + 2 * i + 1]
            left = jnp.concatenate([left_ref[l], columns[l]], axis=1)
            right = jnp.concatenate([right_block(first), right_block(second)], axis=1)
            scores = jnp.dot(
                left, jnp.concatenate([right, ones], axis=0), preferred_element_type=jnp.float32
            )
            fold((2 * u) % COPIES, first, scores[:, :BLOCK])
            fold((2 * u + 1) % COPIES, second, scores[:, BLOCK:])
        return known

    known = lax.fori_loop(0, list_ref[0], functools.partial(step, 0, PAIRS), jnp.int32(0))
    known = lax.fori_loop(0, list_ref[1], functools.partial(step, list_ref[0] * PAIRS, TAIL), known)
    wait_for(known, PARTS)

    def finish(octet, carry):
        rows = []
        for k in range(8):
            r = octet * 8 + k
            tops = [peaks[copy, r] for copy in range(COPIES)]
            top = jnp.max(functools.reduce(jnp.maximum, tops), axis=0, keepdims=True)
            mass = sum(masses[copy, r] * jnp.exp2(tops[copy] - top) for copy in range(COPIES))
            rows.append(top + jnp.log2(jnp.sum(mass, axis=0, keepdims=True)))
        out_ref[0, pl.ds(pl.multiple_of(octet * 8, 8), 8), :] = jnp.concatenate(rows, axis=0)
        return carry

    lax.fori_loop(0, rights // 8, finish, 0)
    for k in range(1, out_ref.shape[0]):
        out_ref[k] = out_ref[0]
    if kind == FIRST:
        hand_on.wait()


def log_sums(kind, pairs, halves, remotes, parts, copies):
    slots = 2 * GROUP
    lefts, rights = (halves, slots) if kind == COLUMNS else (slots, halves)
    rows = D + EXTRA if kind == COLUMNS else BLOCK
    held = lefts
    outs, bias = [shape((copies, rights, BLOCK))], pltpu.VMEM((lefts, BLOCK), jnp.float32)
    if kind == FIRST:
        held = lefts + 2
        outs.append(shape((held, BLOCK, BLOCK), jnp.bfloat16))
        scratch = [bias, bias, pltpu.VMEM((slots, D + EXTRA, BLOCK), jnp.bfloat16)]
    elif kind == ROWS:
        scratch = [bias, pltpu.VMEM((2, BLOCK, BLOCK), jnp.bfloat16), pltpu.VMEM(remotes[-1].shape, jnp.bfloat16)]
    else:
        outs.append(shape((lefts, BLOCK)))
        scratch = [pltpu.VMEM((BLOCK, BLOCK), jnp.bfloat16)]
    return pl.pallas_call(
        functools.partial(pass_kernel, kind),
        out_shape=outs,
        in_specs=[HBM] * (1 + len(remotes)) + [VMEM] * len(parts),
        out_specs=[VMEM, HBM] if kind == FIRST else [VMEM] * len(outs),
        scratch_shapes=scratch
        + [
            pltpu.VMEM((lefts, BLOCK, BLOCK), jnp.bfloat16),
            pltpu.VMEM((COPIES, rights + 1, 8, BLOCK), jnp.float32),
            pltpu.VMEM((COPIES, rights + 1, 8, BLOCK), jnp.float32),
            pltpu.SMEM(list_shape(halves), jnp.int32),
            pltpu.VMEM((held, BLOCK, BLOCK), jnp.bfloat16),
            pltpu.VMEM((rights, rows, BLOCK), jnp.bfloat16),
            pltpu.SemaphoreType.DMA((5 + PARTS,)),
        ],
        compiler_params=PREPARE if kind == FIRST else PASS,
    )(pairs, *remotes, *parts)


def ring(values, axis, size, stride=1):
    places = lax.axis_size(axis)
    out = [values]
    for d in range(1, size):
        pairs = []
        for i in range(places):
            place = i // stride % size
            pairs.append((i, i + ((place + d) % size - place) * stride))
        out.append(lax.ppermute(values, axis, pairs))
    return out


def shards(
    source_points,
    source_logmass,
    target_points,
    target_logmass,
    target_potential,
    tile_slot,
    tile_counts,
    fetch_ids,
):
    peers = lax.axis_size("src")
    blocks = tile_counts.shape[0]
    halves = blocks // 2
    per_peer = fetch_ids.shape[1]
    owned = target_potential.shape[0] // BLOCK
    count = peers * per_peer
    place = lax.axis_index("src")
    half = lax.axis_index("grp") % 2

    def swap(values):
        return ring(values, "grp", 2, 1)[1]

    tiles = jnp.concatenate([tile_slot.T, tile_counts.T], axis=0)
    ids = ring(fetch_ids, "src", peers)
    packed = pack(
        place,
        ids,
        target_points.T,
        target_potential.reshape(owned, BLOCK),
        target_logmass.reshape(owned, BLOCK),
    )
    ids = jnp.stack(ids)
    col_pairs, row_pairs = plan(half, tiles, swap(tiles))
    fetched = lax.all_to_all(packed, "src", split_axis=0, concat_axis=0, tiled=True)
    points, source_half = source(
        half, halves, source_points.T, source_logmass.reshape(blocks, BLOCK)
    )
    fetched, points, col_pairs, row_pairs = lax.optimization_barrier((fetched, points, col_pairs, row_pairs))
    both = [fetched, swap(fetched)]
    all_ids = jnp.stack([ids, swap(ids)])
    same = all_ids[:, :, :, None, :] == all_ids[:, :1, :, :, None]
    same = same[:, :, :, :, None, :] & jnp.eye(peers, dtype=bool)[:, None, :, None]
    same = same.reshape(2, peers, count, 1, count) & jnp.eye(peers, dtype=bool)[:, None, :, None]
    chosen = same.reshape(2, peers * count, peers * count).astype(jnp.bfloat16)

    groups = lax.axis_size("grp")
    same_core = [list(range(core, groups, 2)) for core in range(2)]
    for sweep_index in range(ITERS):
        if sweep_index == 0:
            rows, targets = log_sums(FIRST, row_pairs, halves, [*both, points], [], groups // 2)
        else:
            remotes = [targets, points, chosen]
            (rows,) = log_sums(ROWS, row_pairs, halves, remotes, col_parts, groups // 2)
        rows = lax.all_to_all(
            rows, "grp", split_axis=0, concat_axis=0, tiled=True, axis_index_groups=same_core
        )
        cols, field = log_sums(COLUMNS, col_pairs, halves, [*both, points], [rows], 1)
        cols = cols[0]
        if sweep_index < ITERS - 1:
            other = swap(cols)
            cols = log_sum([cols, jnp.concatenate([other[count:], other[:count]], axis=0)])
            col_parts = ring(cols, "src", peers)
    field = field * (1.0 / SCALE) + source_half
    other = swap(field)
    low = half == 0
    source_field = jnp.concatenate([jnp.where(low, field, other), jnp.where(low, other, field)], axis=0)

    cols = log_sum([cols[:count], swap(cols[count:])]).reshape(peers, per_peer, BLOCK)
    back, requested = [], []
    for d in range(peers):
        wanted = lax.dynamic_slice(cols, ((place + d) % peers, 0, 0), (1, per_peer, BLOCK))[0]
        pairs = [(i, (i + d) % peers) for i in range(peers)]
        back.append(wanted if d == 0 else lax.ppermute(wanted, "src", pairs))
        requested.append(lax.dynamic_slice(ids, (d, place, 0), (1, 1, per_peer))[0, 0])
    blocks_here = jnp.arange(owned, dtype=jnp.int32)[:, None]
    parts = [
        jnp.max(jnp.where((blocks_here == wants[None])[..., None], sums[None], LOWEST), axis=1)
        for wants, sums in zip(requested, back)
    ]
    owned_pot = LOG2E * target_logmass.reshape(owned, BLOCK) - log_sum(parts)
    target_half = 0.5 * jnp.sum(jnp.square(target_points.astype(jnp.float32)), -1)
    target_field = owned_pot.reshape(-1) * (1.0 / SCALE) + target_half
    return (source_field.reshape(-1), target_field)


def solution(mesh):
    return jax.shard_map(
        shards,
        mesh=mesh,
        in_specs=(
            P("src", None),
            P("src"),
            P(("src", "grp"), None),
            P(("src", "grp")),
            P(("src", "grp")),
            P("src", "grp"),
            P("src", "grp"),
            P("src", "grp"),
        ),
        out_specs=(P("src"), P(("src", "grp"))),
        check_vma=False,
    )
```

```python
import functools

import jax
import jax.numpy as jnp
import numpy as np
from jax import lax
from jax.experimental import pallas as pl
from jax.experimental.pallas import tpu as pltpu
from jax.sharding import PartitionSpec as P

D = 64
BLOCK = 128
KG = 8
ITERS = 3
EPSILON = 0.25
LOWEST = -1e30
LOG2E = 1.4426950408889634
SCALE = LOG2E / EPSILON
PAIRS = 32
TAIL = 16
COPIES = 2
GROUP = 32
EXTRA = 16
LEFT, RIGHT = 0, 1
FIRST, ROWS, COLUMNS = 0, 1, 2
PARTS = 4
LONG = 1024 * 1024
HEAD = 8
STRIDE = 64


SMEM = pl.BlockSpec(memory_space=pltpu.SMEM)
VMEM = pl.BlockSpec(memory_space=pltpu.VMEM)
HBM = pl.BlockSpec(memory_space=pltpu.HBM)
MIB = 1024 * 1024
PREPARE = pltpu.CompilerParams(vmem_limit_bytes=64 * MIB)
PASS = pltpu.CompilerParams(vmem_limit_bytes=53 * MIB)


def shape(dims, dtype=jnp.float32):
    return jax.ShapeDtypeStruct(dims, dtype)


def start_copies(pairs, sems):
    copies = [pltpu.make_async_copy(src, dst, sems.at[k]) for k, (src, dst) in enumerate(pairs)]
    for copy in copies:
        copy.start()
    return copies


def close_list(ref, hbm, pairs, last, none, sems):
    right = HEAD + (ref.shape[0] - HEAD) // 3
    tails = (pairs + TAIL - 1) // TAIL
    ref[0] = tails // (PAIRS // TAIL)
    ref[1] = tails % (PAIRS // TAIL)

    def pad(k, carry):
        ref[HEAD + pairs + k] = last
        ref[right + 2 * (pairs + k)] = none
        ref[right + 2 * (pairs + k) + 1] = none
        return carry

    lax.fori_loop(0, tails * TAIL - pairs, pad, 0)
    copy = pltpu.make_async_copy(ref, hbm.at[pl.ds(0, ref.shape[0])], sems.at[0])
    copy.start()
    copy.wait()


def columns_kernel(half_ref, near_ref, far_ref, hbm, ref, sems):
    halves = near_ref.shape[1] // 2
    first = half_ref[0] * halves
    right = HEAD + (ref.shape[0] - HEAD) // 3

    def one_block(b, position):
        at = right + 2 * position
        tiles = jnp.int32(0)
        for group, slots_ref in enumerate((near_ref, far_ref)):
            for k in range(KG):
                ref[at + tiles + k] = slots_ref[k, first + b] + group * GROUP
            tiles = tiles + slots_ref[KG, first + b]
        ref[at + tiles] = 2 * GROUP
        for k in range(KG):
            ref[HEAD + position + k] = b
        return position + (tiles + 1) // 2

    close_list(ref, hbm, lax.fori_loop(0, halves, one_block, jnp.int32(0)), halves - 1, 2 * GROUP, sems)


def rows_kernel(half_ref, near_ref, far_ref, hbm, ref, lists, sizes, sems):
    halves = near_ref.shape[1] // 2
    slots = 2 * GROUP
    first = half_ref[0] * halves
    right = HEAD + (ref.shape[0] - HEAD) // 3

    def clear(q, carry):
        sizes[q] = 0
        return carry

    lax.fori_loop(0, slots + 1, clear, 0, unroll=8)

    def one_block(b, carry):
        for group, slots_ref in enumerate((near_ref, far_ref)):
            count = slots_ref[KG, first + b]

            def some(start, stop, slots_ref=slots_ref, group=group, count=count):
                named = [slots_ref[k, first + b] + group * GROUP for k in range(start, stop)]
                if start >= 2:
                    named = [jnp.where(k < count, slot, slots) for k, slot in enumerate(named, start)]
                known = [sizes[slot] for slot in named]
                for slot, size in zip(named, known):
                    lists[slot * STRIDE + size] = b
                for slot, size in zip(named, known):
                    sizes[slot] = size + 1

            some(0, 2)
            pl.when(count > 2)(functools.partial(some, 2, KG))
        return carry

    lax.fori_loop(0, halves, one_block, 0)

    def one_slot(q, position):
        size = sizes[q]
        lists[q * STRIDE + size] = halves
        pairs = (size + 1) // 2

        def one_pair(k, carry):
            ref[HEAD + position + k] = q
            for j in range(2):
                ref[right + 2 * (position + k) + j] = lists[q * STRIDE + 2 * k + j]
            return carry

        def more():
            for k in range(1, 4):
                one_pair(k, 0)
            lax.fori_loop(4, pairs, one_pair, 0)

        one_pair(0, 0)
        pl.when(pairs > 1)(more)
        return position + pairs

    close_list(ref, hbm, lax.fori_loop(0, slots, one_slot, jnp.int32(0)), slots - 1, halves, sems)


def list_shape(halves):
    room = HEAD + 3 * (halves * KG + 2 * GROUP + PAIRS + KG)
    return ((room + 1023) // 1024 * 1024,)


def make_list(kernel, half, near, far):
    own = []
    if kernel is rows_kernel:
        own = [
            pltpu.SMEM(((2 * GROUP + 1) * STRIDE,), jnp.int32),
            pltpu.SMEM((2 * GROUP + 1,), jnp.int32),
        ]
    return pl.pallas_call(
        kernel,
        out_shape=shape((LONG,), jnp.int32),
        in_specs=[SMEM] * 3,
        out_specs=HBM,
        scratch_shapes=[
            pltpu.SMEM(list_shape(near.shape[1] // 2), jnp.int32),
            *own,
            pltpu.SemaphoreType.DMA((1,)),
        ],
        compiler_params=PREPARE,
    )(half.reshape(1), near, far)


def split3(values):
    high = values.astype(jnp.bfloat16)
    rest = values - high.astype(jnp.float32)
    middle = rest.astype(jnp.bfloat16)
    low = (rest - middle.astype(jnp.float32)).astype(jnp.bfloat16)
    return high, middle, low


def whole(parts):
    high, middle, low = [part.astype(jnp.float32) for part in parts]
    return high + middle + low


def log_sum(values):
    top = functools.reduce(jnp.maximum, values)
    return top + jnp.log2(sum(jnp.exp2(value - top) for value in values))


def pack_kernel(place_ref, *refs):
    count = (len(refs) - 2) // 2
    remotes, (out_ref, *locals_, sems) = refs[:count], refs[count:]
    *ids_refs, points, potential, logmass = locals_
    copies = start_copies(list(zip(remotes, locals_)), sems)
    place = place_ref[0]
    peers, per_peer = ids_refs[0].shape
    for copy in copies:
        copy.wait()
    for d, ids_ref in enumerate(ids_refs):
        other = lax.rem(place - d + peers, peers)

        def one_block(c, carry, ids_ref=ids_ref, other=other):
            t = ids_ref[place, c]
            block = points[:, pl.ds(pl.multiple_of(t * BLOCK, BLOCK), BLOCK)]
            wide = block.astype(jnp.float32)
            norm = jnp.sum(wide * wide, axis=0, keepdims=True)
            start = SCALE * (potential[pl.ds(t, 1), :] - 0.5 * norm)
            mass = LOG2E * logmass[pl.ds(t, 1), :]
            rows = [part.astype(jnp.float32) for part in split3(start) + split3(mass)]
            rows.append(jnp.zeros((EXTRA - len(rows), BLOCK), jnp.float32))
            out_ref[other * per_peer + c, :D, :] = block
            out_ref[other * per_peer + c, D:, :] = jnp.concatenate(rows, axis=0).astype(jnp.bfloat16)
            return carry

        lax.fori_loop(0, per_peer, one_block, 0, unroll=8)


def pack(place, ids, *values):
    remotes = [*ids, *values]
    return pl.pallas_call(
        pack_kernel,
        out_shape=shape((ids[0].size, D + EXTRA, BLOCK), jnp.bfloat16),
        in_specs=[SMEM] + [HBM] * len(remotes),
        out_specs=VMEM,
        scratch_shapes=[pltpu.SMEM(value.shape, value.dtype) for value in ids]
        + [pltpu.VMEM(value.shape, value.dtype) for value in values]
        + [pltpu.SemaphoreType.DMA((len(remotes),))],
        compiler_params=PREPARE,
    )(place.reshape(1), *remotes)


def scaled_block(points, b):
    wide = points[:, pl.ds(pl.multiple_of(b * BLOCK, BLOCK), BLOCK)].astype(jnp.float32)
    scaled = SCALE * wide
    high = scaled.astype(jnp.bfloat16)
    low = (scaled - high.astype(jnp.float32)).astype(jnp.bfloat16)
    return wide, jnp.concatenate([high, low], axis=0)


def source_kernel(half_ref, points_hbm, logmass_hbm, blocks_hbm, norm_ref, points, logmass, blocks, sems):
    halves = blocks.shape[1] - 1
    rows = pl.ds(pl.multiple_of(half_ref[0] * halves, halves), halves)
    at = pl.multiple_of(half_ref[0] * (halves * BLOCK), halves * BLOCK)
    pairs = [(points_hbm.at[:, pl.ds(at, halves * BLOCK)], points), (logmass_hbm.at[rows], logmass)]
    for copy in start_copies(pairs, sems):
        copy.wait()
    parts = split3(LOG2E * logmass[...])
    blocks[LEFT, halves] = jnp.concatenate([*parts, jnp.zeros_like(parts[0])], axis=0)
    blocks[RIGHT, halves] = jnp.zeros((BLOCK, BLOCK), jnp.bfloat16)

    part = halves // PARTS

    def one_block(b, carry):
        wide, both = scaled_block(points, b)
        norm_ref[pl.ds(b, 1), :] = 0.5 * jnp.sum(wide * wide, axis=0, keepdims=True)
        blocks[RIGHT, b] = both
        blocks[LEFT, b] = both.T
        return carry

    copies = []
    for k in range(PARTS):
        lax.fori_loop(k * part, (k + 1) * part, one_block, 0, unroll=4)
        own = (slice(None), pl.ds(k * part, part + (k == PARTS - 1)))
        copies.append(pltpu.make_async_copy(blocks.at[own], blocks_hbm.at[own], sems.at[2 + k]))
        copies[-1].start()
    for copy in copies:
        copy.wait()


def source(half, halves, points, logmass):
    blocks = (2, halves + 1, BLOCK, BLOCK)
    return pl.pallas_call(
        source_kernel,
        out_shape=[shape(blocks, jnp.bfloat16), shape((halves, BLOCK))],
        in_specs=[SMEM, HBM, HBM],
        out_specs=[HBM, VMEM],
        scratch_shapes=[
            pltpu.VMEM((D, halves * BLOCK), jnp.bfloat16),
            pltpu.VMEM((halves, BLOCK), jnp.float32),
            pltpu.VMEM(blocks, jnp.bfloat16),
            pltpu.SemaphoreType.DMA((2 + PARTS,)),
        ],
        compiler_params=PREPARE,
    )(half.reshape(1), points, logmass)


def field_bias(mass_ref, parts_ref):
    rows = parts_ref.shape[1]
    mass = whole([mass_ref[k * rows : (k + 1) * rows, :] for k in range(3)])
    return mass - log_sum([parts_ref[k] for k in range(parts_ref.shape[0])])


def potential_bias(mass_ref, chosen_ref, *refs):
    dot = functools.partial(jnp.dot, preferred_element_type=jnp.float32)
    mass = whole([mass_ref[0, : 2 * GROUP, :], mass_ref[0, 2 * GROUP :, :], mass_ref[1, : 2 * GROUP, :]])
    out = []
    for group in range(2):
        own = slice(group * GROUP, (group + 1) * GROUP)
        chosen = chosen_ref[group]
        sums = jnp.concatenate([ref[own, :] for ref in refs], axis=0)
        parts = sum(dot(chosen, part) for part in split3(sums))
        known = dot(chosen, jnp.ones_like(chosen)) > 0.5
        parts = jnp.where(known, parts, LOWEST)
        merged = log_sum([parts[k * GROUP : (k + 1) * GROUP] for k in range(len(refs))])
        out.append(mass[own, :] - merged)
    return jnp.concatenate(out, axis=0)


def unpack(raw, left, start_ref, mass_ref):
    def one_block(q, carry):
        block = raw[q, :D, :]
        left[q] = jnp.concatenate([block, block], axis=0).T
        rows = raw[q, D:, :].astype(jnp.float32)
        start_ref[pl.ds(q, 1), :] = rows[0:1] + rows[1:2] + rows[2:3]
        mass_ref[pl.ds(q, 1), :] = rows[3:4] + rows[4:5] + rows[5:6]
        return carry

    return lambda group: lax.fori_loop(group * GROUP, (group + 1) * GROUP, one_block, 0, unroll=8)


def pass_kernel(kind, *refs):
    columns, peaks, masses, list_ref, left_ref, right_ref, sems = refs[-7:]
    lefts, rights = columns.shape[0], right_ref.shape[0]
    part = lefts // PARTS
    left_parts = []
    if kind == FIRST:
        list_hbm, near_hbm, far_hbm, points_hbm, half_ref = refs[:5]
        out_ref, left_hbm, mass_ref, bias_ref, raw, points = refs[5:-7]
        own = rights * BLOCK
        at = pl.multiple_of(half_ref[0] * own, own)
        early = [(near_hbm, raw.at[pl.ds(0, GROUP)]), (far_hbm, raw.at[pl.ds(GROUP, GROUP)])]
        early.insert(0, (points_hbm.at[:, pl.ds(at, own)], points))
        late = []
    elif kind == ROWS:
        list_hbm, left_hbm, points_hbm, chosen_hbm = refs[:4]
        *col_parts, out_ref, bias_ref, mass, chosen = refs[4:-7]
        early = [(left_hbm.at[pl.ds(lefts, 2)], mass), (chosen_hbm, chosen)]
        late = [(points_hbm.at[RIGHT, pl.ds(0, rights)], right_ref)]
        left_parts = [left_hbm.at[pl.ds(k * part, part)] for k in range(PARTS)]
    else:
        list_hbm, near_hbm, far_hbm, points_hbm, rows_ref, out_ref, bias_ref, mass = refs[:-7]
        early = [(points_hbm.at[LEFT, lefts], mass)]
        late = [(near_hbm, right_ref.at[pl.ds(0, GROUP)]), (far_hbm, right_ref.at[pl.ds(GROUP, GROUP)])]
        left_parts = [points_hbm.at[LEFT, pl.ds(k * part, part)] for k in range(PARTS)]
    late.append((list_hbm.at[pl.ds(0, list_ref.shape[0])], list_ref))
    pairs = early + late + [(ref, left_ref.at[pl.ds(k * part, part)]) for k, ref in enumerate(left_parts)]
    copies = start_copies(pairs, sems)
    peaks[...] = jnp.full_like(peaks, LOWEST)
    masses[...] = jnp.zeros_like(masses)
    for copy in copies[: len(early)]:
        copy.wait()
    if kind == FIRST:

        def scale(b, carry):
            right_ref[b] = scaled_block(points, b)[1]
            return carry

        lax.fori_loop(0, rights, scale, 0, unroll=8)
        unpack_group = unpack(raw, left_ref, bias_ref, mass_ref)
        for group in range(2):
            unpack_group(group)
        high, middle, low = split3(mass_ref[...])
        left_ref[lefts] = jnp.concatenate([high, middle], axis=0)
        left_ref[lefts + 1] = jnp.concatenate([low, jnp.zeros_like(low)], axis=0)
        hand_on = pltpu.make_async_copy(left_ref, left_hbm, sems.at[len(pairs)])
        hand_on.start()
    elif kind == ROWS:
        bias_ref[...] = potential_bias(mass, chosen, *col_parts)
    else:
        bias_ref[...] = field_bias(mass, rows_ref)
    square = (BLOCK, BLOCK)
    lane = lax.broadcasted_iota(jnp.int32, square, 1)
    eye = jnp.where(lane == lax.broadcasted_iota(jnp.int32, square, 0), 1.0, 0.0).astype(jnp.bfloat16)
    lane = jnp.where(lane < 3 * GROUP, lane % GROUP, -1)
    for group in range(lefts // GROUP):
        high, middle, low = split3(bias_ref[group * GROUP : (group + 1) * GROUP, :])
        parts = jnp.concatenate([high, middle, low, jnp.zeros_like(high)], axis=0)
        turned = lax.dot_general(
            eye, parts, (((1,), (1,)), ((), ())), preferred_element_type=jnp.float32
        )

        def fill(k, carry, group=group, turned=turned):
            columns[group * GROUP + k] = jnp.where(lane == k, turned, 0.0).astype(jnp.bfloat16)
            return carry

        lax.fori_loop(0, GROUP, fill, 0, unroll=4)
    for copy in copies[len(early) : len(early) + len(late)]:
        copy.wait()
    rights_at = HEAD + (list_ref.shape[0] - HEAD) // 3
    ones = jnp.ones((BLOCK, 2 * BLOCK), jnp.bfloat16)

    def fold(copy, r, scores):
        scores = scores.reshape(BLOCK // 8, 8, BLOCK)
        old = peaks[copy, r]
        top = jnp.maximum(old, jnp.max(scores, axis=0))
        mass = jnp.sum(jnp.exp2(scores - top[None]), axis=0)
        masses[copy, r] = masses[copy, r] * jnp.exp2(old - top) + mass
        peaks[copy, r] = top

    def right_block(r):
        r = jnp.minimum(r, rights - 1)
        if kind != COLUMNS:
            return right_ref[r]
        block = right_ref[r, :D, :]
        return jnp.concatenate([block, block], axis=0)

    def wait_for(known, needed):
        if not left_parts:
            return known

        def wait(k, carry):
            at = pl.ds(k * part, part)
            source = left_hbm.at[at] if kind == ROWS else points_hbm.at[LEFT, at]
            pltpu.make_async_copy(source, left_ref.at[at], sems.at[len(early) + len(late) + k]).wait()
            return carry

        lax.fori_loop(known, needed, wait, 0)
        return jnp.maximum(known, needed)

    def step(start, count, t, known):
        known = wait_for(known, list_ref[HEAD + start + t * count + count - 1] // part + 1)
        for u in range(count):
            i = start + t * count + u
            l = list_ref[HEAD + i]
            first, second = list_ref[rights_at + 2 * i], list_ref[rights_at + 2 * i + 1]
            left = jnp.concatenate([left_ref[l], columns[l]], axis=1)
            right = jnp.concatenate([right_block(first), right_block(second)], axis=1)
            scores = jnp.dot(
                left, jnp.concatenate([right, ones], axis=0), preferred_element_type=jnp.float32
            )
            fold((2 * u) % COPIES, first, scores[:, :BLOCK])
            fold((2 * u + 1) % COPIES, second, scores[:, BLOCK:])
        return known

    known = lax.fori_loop(0, list_ref[0], functools.partial(step, 0, PAIRS), jnp.int32(0))
    known = lax.fori_loop(0, list_ref[1], functools.partial(step, list_ref[0] * PAIRS, TAIL), known)
    wait_for(known, PARTS)

    def finish(octet, carry):
        rows = []
        for k in range(8):
            r = octet * 8 + k
            tops = [peaks[copy, r] for copy in range(COPIES)]
            top = jnp.max(functools.reduce(jnp.maximum, tops), axis=0, keepdims=True)
            mass = sum(masses[copy, r] * jnp.exp2(tops[copy] - top) for copy in range(COPIES))
            rows.append(top + jnp.log2(jnp.sum(mass, axis=0, keepdims=True)))
        out_ref[0, pl.ds(pl.multiple_of(octet * 8, 8), 8), :] = jnp.concatenate(rows, axis=0)
        return carry

    lax.fori_loop(0, rights // 8, finish, 0)
    for k in range(1, out_ref.shape[0]):
        out_ref[k] = out_ref[0]
    if kind == FIRST:
        hand_on.wait()


def log_sums(kind, pairs, halves, remotes, parts, copies):
    slots = 2 * GROUP
    lefts, rights = (halves, slots) if kind == COLUMNS else (slots, halves)
    rows = D + EXTRA if kind == COLUMNS else BLOCK
    held = lefts
    outs, bias = [shape((copies, rights, BLOCK))], pltpu.VMEM((lefts, BLOCK), jnp.float32)
    if kind == FIRST:
        held = lefts + 2
        outs.append(shape((held, BLOCK, BLOCK), jnp.bfloat16))
        scratch = [bias, bias, pltpu.VMEM((slots, D + EXTRA, BLOCK), jnp.bfloat16)]
        scratch.append(pltpu.VMEM((D, halves * BLOCK), jnp.bfloat16))
    elif kind == ROWS:
        scratch = [bias, pltpu.VMEM((2, BLOCK, BLOCK), jnp.bfloat16), pltpu.VMEM(remotes[-1].shape, jnp.bfloat16)]
    else:
        outs.append(shape((lefts, BLOCK)))
        scratch = [pltpu.VMEM((BLOCK, BLOCK), jnp.bfloat16)]
    return pl.pallas_call(
        functools.partial(pass_kernel, kind),
        out_shape=outs,
        in_specs=[HBM] * (1 + len(remotes)) + [SMEM if kind == FIRST else VMEM] * len(parts),
        out_specs=[VMEM, HBM] if kind == FIRST else [VMEM] * len(outs),
        scratch_shapes=scratch
        + [
            pltpu.VMEM((lefts, BLOCK, BLOCK), jnp.bfloat16),
            pltpu.VMEM((COPIES, rights + 1, 8, BLOCK), jnp.float32),
            pltpu.VMEM((COPIES, rights + 1, 8, BLOCK), jnp.float32),
            pltpu.SMEM(list_shape(halves), jnp.int32),
            pltpu.VMEM((held, BLOCK, BLOCK), jnp.bfloat16),
            pltpu.VMEM((rights, rows, BLOCK), jnp.bfloat16),
            pltpu.SemaphoreType.DMA((5 + PARTS,)),
        ],
        compiler_params=PREPARE if kind == FIRST else PASS,
    )(pairs, *remotes, *parts)


def ring(values, axis, size, stride=1):
    places = lax.axis_size(axis)
    out = [values]
    for d in range(1, size):
        pairs = []
        for i in range(places):
            place = i // stride % size
            pairs.append((i, i + ((place + d) % size - place) * stride))
        out.append(lax.ppermute(values, axis, pairs))
    return out


def same_targets(ids):
    groups, peers, _, per_peer = ids.shape
    count = peers * per_peer
    alike = np.kron(np.eye(peers * peers), np.ones((per_peer, per_peer))) > 0
    rows = jnp.tile(ids[:, 0].reshape(groups, count), (1, peers))
    same = rows[:, :, None] == ids.reshape(groups, peers * count)[:, None, :]
    return (same & alike).astype(jnp.bfloat16)


def shards(
    source_points,
    source_logmass,
    target_points,
    target_logmass,
    target_potential,
    tile_slot,
    tile_counts,
    fetch_ids,
):
    peers = lax.axis_size("src")
    blocks = tile_counts.shape[0]
    halves = blocks // 2
    per_peer = fetch_ids.shape[1]
    owned = target_potential.shape[0] // BLOCK
    count = peers * per_peer
    place = lax.axis_index("src")
    half = lax.axis_index("grp") % 2

    def swap(values):
        return ring(values, "grp", 2, 1)[1]

    tiles = jnp.concatenate([tile_slot.T, tile_counts.T], axis=0)
    ids = ring(fetch_ids, "src", peers)
    packed = pack(
        place,
        ids,
        target_points.T,
        target_potential.reshape(owned, BLOCK),
        target_logmass.reshape(owned, BLOCK),
    )
    ids = jnp.stack(ids)
    far_tiles = swap(tiles)
    row_pairs = make_list(rows_kernel, half, tiles, far_tiles)
    fetched = lax.all_to_all(packed, "src", split_axis=0, concat_axis=0, tiled=True)
    fetched, row_pairs, tiles, far_tiles = lax.optimization_barrier((fetched, row_pairs, tiles, far_tiles))
    col_pairs = make_list(columns_kernel, half, tiles, far_tiles)
    all_ids = jnp.stack([ids, swap(ids)])
    *both, col_pairs, chosen = lax.optimization_barrier(
        (fetched, swap(fetched), col_pairs, same_targets(all_ids))
    )

    groups = lax.axis_size("grp")
    same_core = [list(range(core, groups, 2)) for core in range(2)]
    for sweep_index in range(ITERS):
        if sweep_index == 0:
            turned = source_points.T
            rows, targets = log_sums(FIRST, row_pairs, halves, [*both, turned], [half.reshape(1)], groups // 2)
            rows, turned, logmass = lax.optimization_barrier((rows, turned, source_logmass))
            points, source_half = source(half, halves, turned, logmass.reshape(blocks, BLOCK))
        else:
            remotes = [targets, points, chosen]
            (rows,) = log_sums(ROWS, row_pairs, halves, remotes, col_parts, groups // 2)
        rows = lax.all_to_all(
            rows, "grp", split_axis=0, concat_axis=0, tiled=True, axis_index_groups=same_core
        )
        cols, field = log_sums(COLUMNS, col_pairs, halves, [*both, points], [rows], 1)
        cols = cols[0]
        if sweep_index < ITERS - 1:
            other = swap(cols)
            cols = log_sum([cols, jnp.concatenate([other[count:], other[:count]], axis=0)])
            col_parts = ring(cols, "src", peers)
    field = field * (1.0 / SCALE) + source_half
    other = swap(field)
    low = half == 0
    source_field = jnp.concatenate([jnp.where(low, field, other), jnp.where(low, other, field)], axis=0)

    cols = log_sum([cols[:count], swap(cols[count:])]).reshape(peers, per_peer, BLOCK)
    back, requested = [], []
    for d in range(peers):
        wanted = lax.dynamic_slice(cols, ((place + d) % peers, 0, 0), (1, per_peer, BLOCK))[0]
        pairs = [(i, (i + d) % peers) for i in range(peers)]
        back.append(wanted if d == 0 else lax.ppermute(wanted, "src", pairs))
        requested.append(lax.dynamic_slice(ids, (d, place, 0), (1, 1, per_peer))[0, 0])
    blocks_here = jnp.arange(owned, dtype=jnp.int32)[:, None]
    parts = [
        jnp.max(jnp.where((blocks_here == wants[None])[..., None], sums[None], LOWEST), axis=1)
        for wants, sums in zip(requested, back)
    ]
    owned_pot = LOG2E * target_logmass.reshape(owned, BLOCK) - log_sum(parts)
    target_half = 0.5 * jnp.sum(jnp.square(target_points.astype(jnp.float32)), -1)
    target_field = owned_pot.reshape(-1) * (1.0 / SCALE) + target_half
    return (source_field.reshape(-1), target_field)


def solution(mesh):
    return jax.shard_map(
        shards,
        mesh=mesh,
        in_specs=(
            P("src", None),
            P("src"),
            P(("src", "grp"), None),
            P(("src", "grp")),
            P(("src", "grp")),
            P("src", "grp"),
            P("src", "grp"),
            P("src", "grp"),
        ),
        out_specs=(P("src"), P(("src", "grp"))),
        check_vma=False,
    )
```

```python
import functools

import jax
import jax.numpy as jnp
from jax import lax
from jax.experimental import pallas as pl
from jax.experimental.pallas import tpu as pltpu
from jax.sharding import PartitionSpec as P

D = 64
BLOCK = 128
KG = 8
ITERS = 3
EPSILON = 0.25
LOWEST = -1e30
LOG2E = 1.4426950408889634
SCALE = LOG2E / EPSILON
PAIRS = 32
TAIL = 16
COPIES = 2
GROUP = 32
EXTRA = 16
LEFT, RIGHT = 0, 1
FIRST, ROWS, COLUMNS = 0, 1, 2
PARTS = 4
LONG = 1024 * 1024
HEAD = 8
STRIDE = 64


SMEM = pl.BlockSpec(memory_space=pltpu.SMEM)
VMEM = pl.BlockSpec(memory_space=pltpu.VMEM)
HBM = pl.BlockSpec(memory_space=pltpu.HBM)
MIB = 1024 * 1024
PREPARE = pltpu.CompilerParams(vmem_limit_bytes=64 * MIB)
PASS = pltpu.CompilerParams(vmem_limit_bytes=53 * MIB)


def shape(dims, dtype=jnp.float32):
    return jax.ShapeDtypeStruct(dims, dtype)


def start_copies(pairs, sems):
    copies = [pltpu.make_async_copy(src, dst, sems.at[k]) for k, (src, dst) in enumerate(pairs)]
    for copy in copies:
        copy.start()
    return copies


def close_list(ref, hbm, pairs, last, none, sems):
    right = HEAD + (ref.shape[0] - HEAD) // 3
    tails = (pairs + TAIL - 1) // TAIL
    ref[0] = tails // (PAIRS // TAIL)
    ref[1] = tails % (PAIRS // TAIL)

    def pad(k, carry):
        ref[HEAD + pairs + k] = last
        ref[right + 2 * (pairs + k)] = none
        ref[right + 2 * (pairs + k) + 1] = none
        return carry

    lax.fori_loop(0, tails * TAIL - pairs, pad, 0)
    copy = pltpu.make_async_copy(ref, hbm.at[pl.ds(0, ref.shape[0])], sems.at[0])
    copy.start()
    return copy


def columns_kernel(half_ref, *refs):
    remotes, (hbm, same_ref), locals_ = refs[:8], refs[8:10], refs[10:]
    *tables, ref, rows, sems = locals_
    copies = start_copies(list(zip(remotes, tables)), sems)
    for copy in copies:
        copy.wait()
    groups, ids = (tables[0:2], tables[2:4]), tables[4:]
    halves = tables[0].shape[1] // 2
    first = half_ref[0] * halves
    right = HEAD + (ref.shape[0] - HEAD) // 3

    def one_block(b, position):
        at = right + 2 * position
        tiles = jnp.int32(0)
        for group, (slots_ref, counts_ref) in enumerate(groups):
            for k in range(KG):
                ref[at + tiles + k] = slots_ref[k, first + b] + group * GROUP
            tiles = tiles + counts_ref[0, first + b]
        ref[at + tiles] = 2 * GROUP
        for k in range(KG):
            ref[HEAD + position + k] = b
        return position + (tiles + 1) // 2

    copy = close_list(ref, hbm, lax.fori_loop(0, halves, one_block, jnp.int32(0)), halves - 1, 2 * GROUP, sems)
    peers, per_peer = ids[0].shape
    lane = lax.broadcasted_iota(jnp.int32, (1, BLOCK), 1)
    known = jnp.zeros((1, BLOCK), jnp.int32)
    for d in range(peers):
        for p in range(peers):
            for c in range(per_peer):
                known = jnp.where(lane == (d * peers + p) * per_peer + c, ids[d][p, c], known)
    for p in range(peers):
        for c in range(per_peer):
            q = p * per_peer + c
            same = jnp.logical_and(known == ids[0][p, c], lane // per_peer % peers == p)
            for d in range(peers):
                own = jnp.logical_and(same, lane // GROUP == d)
                rows[pl.ds(d * GROUP + q, 1), :] = jnp.where(own, 1.0, 0.0)
    same_ref[...] = rows[...].astype(jnp.bfloat16)
    copy.wait()


def rows_kernel(half_ref, *refs):
    remotes, hbm, locals_ = refs[:4], refs[4], refs[5:]
    *tables, ref, lists, sizes, sems = locals_
    copies = start_copies(list(zip(remotes, tables)), sems)
    groups = (tables[0:2], tables[2:4])
    halves = tables[0].shape[1] // 2
    slots = 2 * GROUP
    first = half_ref[0] * halves
    right = HEAD + (ref.shape[0] - HEAD) // 3

    def clear(q, carry):
        sizes[q] = 0
        return carry

    lax.fori_loop(0, slots + 1, clear, 0, unroll=13)
    for copy in copies:
        copy.wait()

    def one_block(b, carry):
        def append(named):
            known = [sizes[slot] for slot in named]
            for slot, size in zip(named, known):
                lists[slot * STRIDE + size] = b
            for slot, size in zip(named, known):
                sizes[slot] = size + 1

        append([table[k, first + b] + group * GROUP for group, (table, _) in enumerate(groups) for k in range(2)])
        for group, (table, counts_ref) in enumerate(groups):
            count = counts_ref[0, first + b]

            def more(table=table, group=group, count=count):
                append(
                    [jnp.where(k < count, table[k, first + b] + group * GROUP, slots) for k in range(2, KG)]
                )

            pl.when(count > 2)(more)
        return carry

    lax.fori_loop(0, halves, one_block, 0)
    batch = 4

    def one_pair(q, position, k):
        ref[HEAD + position + k] = q
        for j in range(2):
            ref[right + 2 * (position + k) + j] = lists[q * STRIDE + 2 * k + j]

    def some_slots(t, position):
        counted = [sizes[t * batch + j] for j in range(batch)]
        for j, size in enumerate(counted):
            lists[(t * batch + j) * STRIDE + size] = halves
        counted = [(size + 1) // 2 for size in counted]
        places = [position]
        for pairs in counted:
            places.append(places[-1] + pairs)
        for j in range(batch):
            for k in range(3):
                one_pair(t * batch + j, places[j], k)

        def rest():
            for j in range(batch):

                def another(k, carry, j=j):
                    one_pair(t * batch + j, places[j], k)
                    return carry

                lax.fori_loop(3, counted[j], another, 0)

        pl.when(functools.reduce(jnp.maximum, counted) > 3)(rest)
        return places[-1]

    pairs = lax.fori_loop(0, slots // batch, some_slots, jnp.int32(0))
    close_list(ref, hbm, pairs, slots - 1, halves, sems).wait()


def list_shape(halves):
    room = HEAD + 3 * (halves * KG + 2 * GROUP + PAIRS + KG)
    return ((room + 1023) // 1024 * 1024,)


def make_list(kernel, half, remotes):
    own = [pltpu.SMEM(value.shape, value.dtype) for value in remotes]
    own.append(pltpu.SMEM(list_shape(remotes[0].shape[1] // 2), jnp.int32))
    outs, specs = [shape((LONG,), jnp.int32)], [HBM]
    if kernel is rows_kernel:
        own.append(pltpu.SMEM(((2 * GROUP + 1) * STRIDE,), jnp.int32))
        own.append(pltpu.SMEM((2 * GROUP + 1,), jnp.int32))
    else:
        own.append(pltpu.VMEM((BLOCK, BLOCK), jnp.float32))
        outs.append(shape((BLOCK, BLOCK), jnp.bfloat16))
        specs.append(VMEM)
    return pl.pallas_call(
        kernel,
        out_shape=outs,
        in_specs=[SMEM] + [HBM] * len(remotes),
        out_specs=specs,
        scratch_shapes=[*own, pltpu.SemaphoreType.DMA((len(remotes),))],
        compiler_params=PREPARE,
    )(half.reshape(1), *remotes)


def split3(values):
    high = values.astype(jnp.bfloat16)
    rest = values - high.astype(jnp.float32)
    middle = rest.astype(jnp.bfloat16)
    low = (rest - middle.astype(jnp.float32)).astype(jnp.bfloat16)
    return high, middle, low


def whole(parts):
    high, middle, low = [part.astype(jnp.float32) for part in parts]
    return high + middle + low


def log_sum(values):
    top = functools.reduce(jnp.maximum, values)
    return top + jnp.log2(sum(jnp.exp2(value - top) for value in values))


def pack_kernel(place_ref, *refs):
    count = (len(refs) - 2) // 2
    remotes, (out_ref, *locals_, sems) = refs[:count], refs[count:]
    *ids_refs, points, potential, logmass = locals_
    copies = start_copies(list(zip(remotes, locals_)), sems)
    place = place_ref[0]
    peers, per_peer = ids_refs[0].shape
    for copy in copies:
        copy.wait()
    for d, ids_ref in enumerate(ids_refs):
        other = lax.rem(place - d + peers, peers)

        def one_block(c, carry, ids_ref=ids_ref, other=other):
            t = ids_ref[place, c]
            block = points[:, pl.ds(pl.multiple_of(t * BLOCK, BLOCK), BLOCK)]
            wide = block.astype(jnp.float32)
            norm = jnp.sum(wide * wide, axis=0, keepdims=True)
            start = SCALE * (potential[pl.ds(t, 1), :] - 0.5 * norm)
            mass = LOG2E * logmass[pl.ds(t, 1), :]
            rows = [part.astype(jnp.float32) for part in split3(start) + split3(mass)]
            rows.append(jnp.zeros((EXTRA - len(rows), BLOCK), jnp.float32))
            out_ref[other * per_peer + c, :D, :] = block
            out_ref[other * per_peer + c, D:, :] = jnp.concatenate(rows, axis=0).astype(jnp.bfloat16)
            return carry

        lax.fori_loop(0, per_peer, one_block, 0, unroll=8)


def pack(place, ids, *values):
    remotes = [*ids, *values]
    return pl.pallas_call(
        pack_kernel,
        out_shape=shape((ids[0].size, D + EXTRA, BLOCK), jnp.bfloat16),
        in_specs=[SMEM] + [HBM] * len(remotes),
        out_specs=VMEM,
        scratch_shapes=[pltpu.SMEM(value.shape, value.dtype) for value in ids]
        + [pltpu.VMEM(value.shape, value.dtype) for value in values]
        + [pltpu.SemaphoreType.DMA((len(remotes),))],
        compiler_params=PREPARE,
    )(place.reshape(1), *remotes)


def scaled_block(points, b):
    wide = points[:, pl.ds(pl.multiple_of(b * BLOCK, BLOCK), BLOCK)].astype(jnp.float32)
    scaled = SCALE * wide
    high = scaled.astype(jnp.bfloat16)
    low = (scaled - high.astype(jnp.float32)).astype(jnp.bfloat16)
    return wide, jnp.concatenate([high, low], axis=0)


def source_kernel(half_ref, points_hbm, logmass_hbm, blocks_hbm, norm_ref, points, logmass, blocks, sems):
    halves = blocks.shape[1] - 1
    rows = pl.ds(pl.multiple_of(half_ref[0] * halves, halves), halves)
    at = pl.multiple_of(half_ref[0] * (halves * BLOCK), halves * BLOCK)
    pairs = [(points_hbm.at[:, pl.ds(at, halves * BLOCK)], points), (logmass_hbm.at[rows], logmass)]
    for copy in start_copies(pairs, sems):
        copy.wait()
    parts = split3(LOG2E * logmass[...])
    blocks[LEFT, halves] = jnp.concatenate([*parts, jnp.zeros_like(parts[0])], axis=0)
    blocks[RIGHT, halves] = jnp.zeros((BLOCK, BLOCK), jnp.bfloat16)

    part = halves // PARTS

    def one_block(b, carry):
        wide, both = scaled_block(points, b)
        norm_ref[pl.ds(b, 1), :] = 0.5 * jnp.sum(wide * wide, axis=0, keepdims=True)
        blocks[RIGHT, b] = both
        blocks[LEFT, b] = both.T
        return carry

    copies = []
    for k in range(PARTS):
        lax.fori_loop(k * part, (k + 1) * part, one_block, 0, unroll=4)
        own = (slice(None), pl.ds(k * part, part + (k == PARTS - 1)))
        copies.append(pltpu.make_async_copy(blocks.at[own], blocks_hbm.at[own], sems.at[2 + k]))
        copies[-1].start()
    for copy in copies:
        copy.wait()


def source(half, halves, points, logmass):
    blocks = (2, halves + 1, BLOCK, BLOCK)
    return pl.pallas_call(
        source_kernel,
        out_shape=[shape(blocks, jnp.bfloat16), shape((halves, BLOCK))],
        in_specs=[SMEM, HBM, HBM],
        out_specs=[HBM, VMEM],
        scratch_shapes=[
            pltpu.VMEM((D, halves * BLOCK), jnp.bfloat16),
            pltpu.VMEM((halves, BLOCK), jnp.float32),
            pltpu.VMEM(blocks, jnp.bfloat16),
            pltpu.SemaphoreType.DMA((2 + PARTS,)),
        ],
        compiler_params=PASS,
    )(half.reshape(1), points, logmass)


def field_bias(mass_ref, parts_ref):
    rows = parts_ref.shape[1]
    mass = whole([mass_ref[k * rows : (k + 1) * rows, :] for k in range(3)])
    return mass - log_sum([parts_ref[k] for k in range(parts_ref.shape[0])])


def potential_bias(mass_ref, chosen_refs, *refs):
    dot = functools.partial(jnp.dot, preferred_element_type=jnp.float32)
    mass = whole([mass_ref[0, : 2 * GROUP, :], mass_ref[0, 2 * GROUP :, :], mass_ref[1, : 2 * GROUP, :]])
    out = []
    for group in range(2):
        own = slice(group * GROUP, (group + 1) * GROUP)
        chosen = chosen_refs[group][...]
        sums = jnp.concatenate([ref[own, :] for ref in refs], axis=0)
        parts = sum(dot(chosen, part) for part in split3(sums))
        known = dot(chosen, jnp.ones_like(chosen)) > 0.5
        parts = jnp.where(known, parts, LOWEST)
        merged = log_sum([parts[k * GROUP : (k + 1) * GROUP] for k in range(len(refs))])
        out.append(mass[own, :] - merged)
    return jnp.concatenate(out, axis=0)


def unpack(raw, left, start_ref, mass_ref):
    def one_block(q, carry):
        block = raw[q, :D, :]
        left[q] = jnp.concatenate([block, block], axis=0).T
        rows = raw[q, D:, :].astype(jnp.float32)
        start_ref[pl.ds(q, 1), :] = rows[0:1] + rows[1:2] + rows[2:3]
        mass_ref[pl.ds(q, 1), :] = rows[3:4] + rows[4:5] + rows[5:6]
        return carry

    return lambda group: lax.fori_loop(group * GROUP, (group + 1) * GROUP, one_block, 0, unroll=8)


def pass_kernel(kind, *refs):
    columns, peaks, masses, list_ref, left_ref, right_ref, sems = refs[-7:]
    lefts, rights = columns.shape[0], right_ref.shape[0]
    part = lefts // PARTS
    left_parts = []
    if kind == FIRST:
        list_hbm, near_hbm, far_hbm, points_hbm, half_ref = refs[:5]
        out_ref, left_hbm, mass_ref, bias_ref, raw, points = refs[5:-7]
        own = rights * BLOCK
        at = pl.multiple_of(half_ref[0] * own, own)
        early = [(near_hbm, raw.at[pl.ds(0, GROUP)]), (far_hbm, raw.at[pl.ds(GROUP, GROUP)])]
        early.insert(0, (points_hbm.at[:, pl.ds(at, own)], points))
        late = []
    elif kind == ROWS:
        list_hbm, left_hbm, points_hbm = refs[:3]
        *col_parts, near_same, far_same, out_ref, bias_ref, mass = refs[3:-7]
        early = [(left_hbm.at[pl.ds(lefts, 2)], mass)]
        late = [(points_hbm.at[RIGHT, pl.ds(0, rights)], right_ref)]
        left_parts = [left_hbm.at[pl.ds(k * part, part)] for k in range(PARTS)]
    else:
        list_hbm, near_hbm, far_hbm, points_hbm, rows_ref, out_ref, bias_ref, mass = refs[:-7]
        early = [(points_hbm.at[LEFT, lefts], mass)]
        late = [(near_hbm, right_ref.at[pl.ds(0, GROUP)]), (far_hbm, right_ref.at[pl.ds(GROUP, GROUP)])]
        left_parts = [points_hbm.at[LEFT, pl.ds(k * part, part)] for k in range(PARTS)]
    late.append((list_hbm.at[pl.ds(0, list_ref.shape[0])], list_ref))
    pairs = early + late + [(ref, left_ref.at[pl.ds(k * part, part)]) for k, ref in enumerate(left_parts)]
    copies = start_copies(pairs, sems)
    peaks[...] = jnp.full_like(peaks, LOWEST)
    masses[...] = jnp.zeros_like(masses)
    for copy in copies[: len(early)]:
        copy.wait()
    if kind == FIRST:

        def scale(b, carry):
            right_ref[b] = scaled_block(points, b)[1]
            return carry

        lax.fori_loop(0, rights, scale, 0, unroll=8)
        unpack_group = unpack(raw, left_ref, bias_ref, mass_ref)
        for group in range(2):
            unpack_group(group)
        high, middle, low = split3(mass_ref[...])
        left_ref[lefts] = jnp.concatenate([high, middle], axis=0)
        left_ref[lefts + 1] = jnp.concatenate([low, jnp.zeros_like(low)], axis=0)
        hand_on = pltpu.make_async_copy(left_ref, left_hbm, sems.at[len(pairs)])
        hand_on.start()
    elif kind == ROWS:
        bias_ref[...] = potential_bias(mass, (near_same, far_same), *col_parts)
    else:
        bias_ref[...] = field_bias(mass, rows_ref)
    square = (BLOCK, BLOCK)
    lane = lax.broadcasted_iota(jnp.int32, square, 1)
    eye = jnp.where(lane == lax.broadcasted_iota(jnp.int32, square, 0), 1.0, 0.0).astype(jnp.bfloat16)
    lane = jnp.where(lane < 3 * GROUP, lane % GROUP, -1)
    for group in range(lefts // GROUP):
        high, middle, low = split3(bias_ref[group * GROUP : (group + 1) * GROUP, :])
        parts = jnp.concatenate([high, middle, low, jnp.zeros_like(high)], axis=0)
        turned = lax.dot_general(
            eye, parts, (((1,), (1,)), ((), ())), preferred_element_type=jnp.float32
        )

        def fill(k, carry, group=group, turned=turned):
            columns[group * GROUP + k] = jnp.where(lane == k, turned, 0.0).astype(jnp.bfloat16)
            return carry

        lax.fori_loop(0, GROUP, fill, 0, unroll=4)
    for copy in copies[len(early) : len(early) + len(late)]:
        copy.wait()
    rights_at = HEAD + (list_ref.shape[0] - HEAD) // 3
    ones = jnp.ones((BLOCK, 2 * BLOCK), jnp.bfloat16)

    def fold(copy, r, scores):
        scores = scores.reshape(BLOCK // 8, 8, BLOCK)
        old = peaks[copy, r]
        top = jnp.maximum(old, jnp.max(scores, axis=0))
        mass = jnp.sum(jnp.exp2(scores - top[None]), axis=0)
        masses[copy, r] = masses[copy, r] * jnp.exp2(old - top) + mass
        peaks[copy, r] = top

    def right_block(r):
        r = jnp.minimum(r, rights - 1)
        if kind != COLUMNS:
            return right_ref[r]
        block = right_ref[r, :D, :]
        return jnp.concatenate([block, block], axis=0)

    def wait_for(known, needed):
        if not left_parts:
            return known

        def wait(k, carry):
            at = pl.ds(k * part, part)
            source = left_hbm.at[at] if kind == ROWS else points_hbm.at[LEFT, at]
            pltpu.make_async_copy(source, left_ref.at[at], sems.at[len(early) + len(late) + k]).wait()
            return carry

        lax.fori_loop(known, needed, wait, 0)
        return jnp.maximum(known, needed)

    def step(start, count, t, known):
        known = wait_for(known, list_ref[HEAD + start + t * count + count - 1] // part + 1)
        for u in range(count):
            i = start + t * count + u
            l = list_ref[HEAD + i]
            first, second = list_ref[rights_at + 2 * i], list_ref[rights_at + 2 * i + 1]
            left = jnp.concatenate([left_ref[l], columns[l]], axis=1)
            right = jnp.concatenate([right_block(first), right_block(second)], axis=1)
            scores = jnp.dot(
                left, jnp.concatenate([right, ones], axis=0), preferred_element_type=jnp.float32
            )
            fold((2 * u) % COPIES, first, scores[:, :BLOCK])
            fold((2 * u + 1) % COPIES, second, scores[:, BLOCK:])
        return known

    known = lax.fori_loop(0, list_ref[0], functools.partial(step, 0, PAIRS), jnp.int32(0))
    known = lax.fori_loop(0, list_ref[1], functools.partial(step, list_ref[0] * PAIRS, TAIL), known)
    wait_for(known, PARTS)

    def finish(octet, carry):
        rows = []
        for k in range(8):
            r = octet * 8 + k
            tops = [peaks[copy, r] for copy in range(COPIES)]
            top = jnp.max(functools.reduce(jnp.maximum, tops), axis=0, keepdims=True)
            mass = sum(masses[copy, r] * jnp.exp2(tops[copy] - top) for copy in range(COPIES))
            rows.append(top + jnp.log2(jnp.sum(mass, axis=0, keepdims=True)))
        out_ref[0, pl.ds(pl.multiple_of(octet * 8, 8), 8), :] = jnp.concatenate(rows, axis=0)
        return carry

    lax.fori_loop(0, rights // 8, finish, 0)
    for k in range(1, out_ref.shape[0]):
        out_ref[k] = out_ref[0]
    if kind == FIRST:
        hand_on.wait()


def log_sums(kind, pairs, halves, remotes, parts, copies):
    slots = 2 * GROUP
    lefts, rights = (halves, slots) if kind == COLUMNS else (slots, halves)
    rows = D + EXTRA if kind == COLUMNS else BLOCK
    held = lefts
    outs, bias = [shape((copies, rights, BLOCK))], pltpu.VMEM((lefts, BLOCK), jnp.float32)
    if kind == FIRST:
        held = lefts + 2
        outs.append(shape((held, BLOCK, BLOCK), jnp.bfloat16))
        scratch = [bias, bias, pltpu.VMEM((slots, D + EXTRA, BLOCK), jnp.bfloat16)]
        scratch.append(pltpu.VMEM((D, halves * BLOCK), jnp.bfloat16))
    elif kind == ROWS:
        scratch = [bias, pltpu.VMEM((2, BLOCK, BLOCK), jnp.bfloat16)]
    else:
        outs.append(shape((lefts, BLOCK)))
        scratch = [pltpu.VMEM((BLOCK, BLOCK), jnp.bfloat16)]
    return pl.pallas_call(
        functools.partial(pass_kernel, kind),
        out_shape=outs,
        in_specs=[HBM] * (1 + len(remotes)) + [SMEM if kind == FIRST else VMEM] * len(parts),
        out_specs=[VMEM, HBM] if kind == FIRST else [VMEM] * len(outs),
        scratch_shapes=scratch
        + [
            pltpu.VMEM((lefts, BLOCK, BLOCK), jnp.bfloat16),
            pltpu.VMEM((COPIES, rights + 1, 8, BLOCK), jnp.float32),
            pltpu.VMEM((COPIES, rights + 1, 8, BLOCK), jnp.float32),
            pltpu.SMEM(list_shape(halves), jnp.int32),
            pltpu.VMEM((held, BLOCK, BLOCK), jnp.bfloat16),
            pltpu.VMEM((rights, rows, BLOCK), jnp.bfloat16),
            pltpu.SemaphoreType.DMA((5 + PARTS,)),
        ],
        compiler_params=PREPARE if kind == FIRST else PASS,
    )(pairs, *remotes, *parts)


def ring(values, axis, size, stride=1):
    places = lax.axis_size(axis)
    out = [values]
    for d in range(1, size):
        pairs = []
        for i in range(places):
            place = i // stride % size
            pairs.append((i, i + ((place + d) % size - place) * stride))
        out.append(lax.ppermute(values, axis, pairs))
    return out


def shards(
    source_points,
    source_logmass,
    target_points,
    target_logmass,
    target_potential,
    tile_slot,
    tile_counts,
    fetch_ids,
):
    peers = lax.axis_size("src")
    blocks = tile_counts.shape[0]
    halves = blocks // 2
    per_peer = fetch_ids.shape[1]
    owned = target_potential.shape[0] // BLOCK
    count = peers * per_peer
    place = lax.axis_index("src")
    half = lax.axis_index("grp") % 2

    def swap(values):
        return ring(values, "grp", 2, 1)[1]

    tiles = [tile_slot.T, tile_counts.T]
    ids = ring(fetch_ids, "src", peers)
    ids, tiles = lax.optimization_barrier((ids, tiles + [swap(part) for part in tiles]))
    packed = pack(
        place,
        ids,
        target_points.T,
        target_potential.reshape(owned, BLOCK),
        target_logmass.reshape(owned, BLOCK),
    )
    (row_pairs,) = make_list(rows_kernel, half, tiles)
    fetched = lax.all_to_all(packed, "src", split_axis=0, concat_axis=0, tiled=True)
    fetched, row_pairs, ids, tiles = lax.optimization_barrier((fetched, row_pairs, ids, tiles))
    col_pairs, same = make_list(columns_kernel, half, tiles + ids)
    *both, col_pairs, same = lax.optimization_barrier((fetched, swap(fetched), col_pairs, same))
    same = [same, swap(same)]
    ids = jnp.stack(ids)

    groups = lax.axis_size("grp")
    same_core = [list(range(core, groups, 2)) for core in range(2)]
    for sweep_index in range(ITERS):
        if sweep_index == 0:
            turned = source_points.T
            rows, targets = log_sums(FIRST, row_pairs, halves, [*both, turned], [half.reshape(1)], groups // 2)
            rows, turned, logmass = lax.optimization_barrier((rows, turned, source_logmass))
            points, source_half = source(half, halves, turned, logmass.reshape(blocks, BLOCK))
        else:
            (rows,) = log_sums(ROWS, row_pairs, halves, [targets, points], col_parts + same, groups // 2)
        rows = lax.all_to_all(
            rows, "grp", split_axis=0, concat_axis=0, tiled=True, axis_index_groups=same_core
        )
        cols, field = log_sums(COLUMNS, col_pairs, halves, [*both, points], [rows], 1)
        cols = cols[0]
        if sweep_index < ITERS - 1:
            other = swap(cols)
            cols = log_sum([cols, jnp.concatenate([other[count:], other[:count]], axis=0)])
            col_parts = ring(cols, "src", peers)
    field = field * (1.0 / SCALE) + source_half
    other = swap(field)
    low = half == 0
    source_field = jnp.concatenate([jnp.where(low, field, other), jnp.where(low, other, field)], axis=0)

    cols = log_sum([cols[:count], swap(cols[count:])]).reshape(peers, per_peer, BLOCK)
    back, requested = [], []
    for d in range(peers):
        wanted = lax.dynamic_slice(cols, ((place + d) % peers, 0, 0), (1, per_peer, BLOCK))[0]
        pairs = [(i, (i + d) % peers) for i in range(peers)]
        back.append(wanted if d == 0 else lax.ppermute(wanted, "src", pairs))
        requested.append(lax.dynamic_slice(ids, (d, place, 0), (1, 1, per_peer))[0, 0])
    blocks_here = jnp.arange(owned, dtype=jnp.int32)[:, None]
    parts = [
        jnp.max(jnp.where((blocks_here == wants[None])[..., None], sums[None], LOWEST), axis=1)
        for wants, sums in zip(requested, back)
    ]
    owned_pot = LOG2E * target_logmass.reshape(owned, BLOCK) - log_sum(parts)
    target_half = 0.5 * jnp.sum(jnp.square(target_points.astype(jnp.float32)), -1)
    target_field = owned_pot.reshape(-1) * (1.0 / SCALE) + target_half
    return (source_field.reshape(-1), target_field)


def solution(mesh):
    return jax.shard_map(
        shards,
        mesh=mesh,
        in_specs=(
            P("src", None),
            P("src"),
            P(("src", "grp"), None),
            P(("src", "grp")),
            P(("src", "grp")),
            P("src", "grp"),
            P("src", "grp"),
            P("src", "grp"),
        ),
        out_specs=(P("src"), P(("src", "grp"))),
        check_vma=False,
    )
```

```python
import functools

import jax
import jax.numpy as jnp
from jax import lax
from jax.experimental import pallas as pl
from jax.experimental.pallas import tpu as pltpu
from jax.sharding import PartitionSpec as P

D = 64
BLOCK = 128
KG = 8
ITERS = 3
EPSILON = 0.25
LOWEST = -1e30
LOG2E = 1.4426950408889634
SCALE = LOG2E / EPSILON
PAIRS = 64
TAIL = 16
COPIES = 2
GROUP = 32
EXTRA = 16
LEFT, RIGHT = 0, 1
FIRST, ROWS, COLUMNS = 0, 1, 2
PARTS = 4
LONG = 1024 * 1024
HEAD = 8
STRIDE = 64


SMEM = pl.BlockSpec(memory_space=pltpu.SMEM)
VMEM = pl.BlockSpec(memory_space=pltpu.VMEM)
HBM = pl.BlockSpec(memory_space=pltpu.HBM)
MIB = 1024 * 1024
PREPARE = pltpu.CompilerParams(vmem_limit_bytes=64 * MIB)
PASS = pltpu.CompilerParams(vmem_limit_bytes=53 * MIB)


def shape(dims, dtype=jnp.float32):
    return jax.ShapeDtypeStruct(dims, dtype)


def start_copies(pairs, sems):
    copies = [pltpu.make_async_copy(src, dst, sems.at[k]) for k, (src, dst) in enumerate(pairs)]
    for copy in copies:
        copy.start()
    return copies


def close_list(ref, hbm, pairs, last, none, sems):
    right = HEAD + (ref.shape[0] - HEAD) // 3
    tails = (pairs + TAIL - 1) // TAIL
    ref[0] = tails // (PAIRS // TAIL)
    ref[1] = tails % (PAIRS // TAIL)

    def pad(k, carry):
        ref[HEAD + pairs + k] = last
        ref[right + 2 * (pairs + k)] = none
        ref[right + 2 * (pairs + k) + 1] = none
        return carry

    lax.fori_loop(0, tails * TAIL - pairs, pad, 0)
    copy = pltpu.make_async_copy(ref, hbm.at[pl.ds(0, ref.shape[0])], sems.at[0])
    copy.start()
    return copy


def columns_kernel(half_ref, *refs):
    remotes, (hbm, same_ref), locals_ = refs[:8], refs[8:10], refs[10:]
    *tables, ref, rows, sems = locals_
    copies = start_copies(list(zip(remotes, tables)), sems)
    for copy in copies:
        copy.wait()
    groups, ids = (tables[0:2], tables[2:4]), tables[4:]
    halves = tables[0].shape[1] // 2
    first = half_ref[0] * halves
    right = HEAD + (ref.shape[0] - HEAD) // 3

    def one_block(b, position):
        at = right + 2 * position
        tiles = jnp.int32(0)
        for group, (slots_ref, counts_ref) in enumerate(groups):
            for k in range(KG):
                ref[at + tiles + k] = slots_ref[k, first + b] + group * GROUP
            tiles = tiles + counts_ref[0, first + b]
        ref[at + tiles] = 2 * GROUP
        for k in range(KG):
            ref[HEAD + position + k] = b
        return position + (tiles + 1) // 2

    copy = close_list(ref, hbm, lax.fori_loop(0, halves, one_block, jnp.int32(0)), halves - 1, 2 * GROUP, sems)
    peers, per_peer = ids[0].shape
    lane = lax.broadcasted_iota(jnp.int32, (1, BLOCK), 1)
    known = jnp.zeros((1, BLOCK), jnp.int32)
    for d in range(peers):
        for p in range(peers):
            for c in range(per_peer):
                known = jnp.where(lane == (d * peers + p) * per_peer + c, ids[d][p, c], known)
    for p in range(peers):
        for c in range(per_peer):
            q = p * per_peer + c
            same = jnp.logical_and(known == ids[0][p, c], lane // per_peer % peers == p)
            for d in range(peers):
                own = jnp.logical_and(same, lane // GROUP == d)
                rows[pl.ds(d * GROUP + q, 1), :] = jnp.where(own, 1.0, 0.0)
    same_ref[...] = rows[...].astype(jnp.bfloat16)
    copy.wait()


def rows_kernel(half_ref, *refs):
    remotes, hbm, locals_ = refs[:4], refs[4], refs[5:]
    *tables, ref, lists, sizes, sems = locals_
    copies = start_copies(list(zip(remotes, tables)), sems)
    groups = (tables[0:2], tables[2:4])
    halves = tables[0].shape[1] // 2
    slots = 2 * GROUP
    first = half_ref[0] * halves
    right = HEAD + (ref.shape[0] - HEAD) // 3

    def clear(q, carry):
        sizes[q] = 0
        return carry

    lax.fori_loop(0, slots + 1, clear, 0, unroll=13)
    for copy in copies:
        copy.wait()

    def one_block(b, carry):
        def append(named):
            known = [sizes[slot] for slot in named]
            for slot, size in zip(named, known):
                lists[slot * STRIDE + size] = b
            for slot, size in zip(named, known):
                sizes[slot] = size + 1

        append([table[k, first + b] + group * GROUP for group, (table, _) in enumerate(groups) for k in range(2)])
        for group, (table, counts_ref) in enumerate(groups):
            count = counts_ref[0, first + b]

            def more(table=table, group=group, count=count):
                append(
                    [jnp.where(k < count, table[k, first + b] + group * GROUP, slots) for k in range(2, KG)]
                )

            pl.when(count > 2)(more)
        return carry

    lax.fori_loop(0, halves, one_block, 0)
    batch = 4

    def one_pair(q, position, k):
        ref[HEAD + position + k] = q
        for j in range(2):
            ref[right + 2 * (position + k) + j] = lists[q * STRIDE + 2 * k + j]

    def some_slots(t, position):
        counted = [sizes[t * batch + j] for j in range(batch)]
        for j, size in enumerate(counted):
            lists[(t * batch + j) * STRIDE + size] = halves
        counted = [(size + 1) // 2 for size in counted]
        places = [position]
        for pairs in counted:
            places.append(places[-1] + pairs)
        for j in range(batch):
            for k in range(3):
                one_pair(t * batch + j, places[j], k)

        def rest():
            for j in range(batch):

                def another(k, carry, j=j):
                    one_pair(t * batch + j, places[j], k)
                    return carry

                lax.fori_loop(3, counted[j], another, 0)

        pl.when(functools.reduce(jnp.maximum, counted) > 3)(rest)
        return places[-1]

    pairs = lax.fori_loop(0, slots // batch, some_slots, jnp.int32(0))
    close_list(ref, hbm, pairs, slots - 1, halves, sems).wait()


def list_shape(halves):
    room = HEAD + 3 * (halves * KG + 2 * GROUP + PAIRS + KG)
    return ((room + 1023) // 1024 * 1024,)


def make_list(kernel, half, remotes):
    own = [pltpu.SMEM(value.shape, value.dtype) for value in remotes]
    own.append(pltpu.SMEM(list_shape(remotes[0].shape[1] // 2), jnp.int32))
    outs, specs = [shape((LONG,), jnp.int32)], [HBM]
    if kernel is rows_kernel:
        own.append(pltpu.SMEM(((2 * GROUP + 1) * STRIDE,), jnp.int32))
        own.append(pltpu.SMEM((2 * GROUP + 1,), jnp.int32))
    else:
        own.append(pltpu.VMEM((BLOCK, BLOCK), jnp.float32))
        outs.append(shape((BLOCK, BLOCK), jnp.bfloat16))
        specs.append(VMEM)
    return pl.pallas_call(
        kernel,
        out_shape=outs,
        in_specs=[SMEM] + [HBM] * len(remotes),
        out_specs=specs,
        scratch_shapes=[*own, pltpu.SemaphoreType.DMA((len(remotes),))],
        compiler_params=PREPARE,
    )(half.reshape(1), *remotes)


def split3(values):
    high = values.astype(jnp.bfloat16)
    rest = values - high.astype(jnp.float32)
    middle = rest.astype(jnp.bfloat16)
    low = (rest - middle.astype(jnp.float32)).astype(jnp.bfloat16)
    return high, middle, low


def whole(parts):
    high, middle, low = [part.astype(jnp.float32) for part in parts]
    return high + middle + low


def log_sum(values):
    top = functools.reduce(jnp.maximum, values)
    return top + jnp.log2(sum(jnp.exp2(value - top) for value in values))


def pack_kernel(place_ref, *refs):
    count = (len(refs) - 3) // 2
    remotes, (out_ref, norm_ref, *locals_, sems) = refs[:count], refs[count:]
    *ids_refs, points, potential, logmass = locals_
    copies = start_copies(list(zip(remotes, locals_)), sems)
    place = place_ref[0]
    peers, per_peer = ids_refs[0].shape
    for copy in copies:
        copy.wait()

    def one_norm(t, carry):
        wide = points[:, pl.ds(pl.multiple_of(t * BLOCK, BLOCK), BLOCK)].astype(jnp.float32)
        norm_ref[pl.ds(t, 1), :] = 0.5 * jnp.sum(wide * wide, axis=0, keepdims=True)
        return carry

    lax.fori_loop(0, norm_ref.shape[0], one_norm, 0, unroll=8)
    for d, ids_ref in enumerate(ids_refs):
        other = lax.rem(place - d + peers, peers)

        def one_block(c, carry, ids_ref=ids_ref, other=other):
            t = ids_ref[place, c]
            block = points[:, pl.ds(pl.multiple_of(t * BLOCK, BLOCK), BLOCK)]
            start = SCALE * (potential[pl.ds(t, 1), :] - norm_ref[pl.ds(t, 1), :])
            mass = LOG2E * logmass[pl.ds(t, 1), :]
            rows = [part.astype(jnp.float32) for part in split3(start) + split3(mass)]
            rows.append(jnp.zeros((EXTRA - len(rows), BLOCK), jnp.float32))
            out_ref[other * per_peer + c, :D, :] = block
            out_ref[other * per_peer + c, D:, :] = jnp.concatenate(rows, axis=0).astype(jnp.bfloat16)
            return carry

        lax.fori_loop(0, per_peer, one_block, 0, unroll=8)


def pack(place, ids, *values):
    remotes = [*ids, *values]
    return pl.pallas_call(
        pack_kernel,
        out_shape=[shape((ids[0].size, D + EXTRA, BLOCK), jnp.bfloat16), shape(values[1].shape)],
        in_specs=[SMEM] + [HBM] * len(remotes),
        out_specs=[VMEM, VMEM],
        scratch_shapes=[pltpu.SMEM(value.shape, value.dtype) for value in ids]
        + [pltpu.VMEM(value.shape, value.dtype) for value in values]
        + [pltpu.SemaphoreType.DMA((len(remotes),))],
        compiler_params=PREPARE,
    )(place.reshape(1), *remotes)


def merge_kernel(peers, place_ref, *refs):
    sums, ids, (logmass_ref, norm_ref, out_ref, parts) = refs[:peers], refs[peers : 2 * peers], refs[2 * peers :]
    place = place_ref[0]
    parts[...] = jnp.full_like(parts, LOWEST)
    for d in range(peers):
        for c in range(sums[d].shape[0]):
            parts[d, pl.ds(ids[d][place, c], 1), :] = sums[d][c : c + 1, :]
    merged = log_sum([parts[d] for d in range(peers)])
    out_ref[...] = (LOG2E * logmass_ref[...] - merged) * (1.0 / SCALE) + norm_ref[...]


def merge(place, sums, ids, logmass, norm):
    peers = len(ids)
    return pl.pallas_call(
        functools.partial(merge_kernel, peers),
        out_shape=shape(norm.shape),
        in_specs=[SMEM] + [VMEM] * peers + [SMEM] * peers + [VMEM] * 2,
        out_specs=VMEM,
        scratch_shapes=[pltpu.VMEM((peers, *norm.shape), jnp.float32)],
        compiler_params=PASS,
    )(place.reshape(1), *sums, *ids, logmass, norm)


def scaled_block(points, b):
    wide = points[:, pl.ds(pl.multiple_of(b * BLOCK, BLOCK), BLOCK)].astype(jnp.float32)
    scaled = SCALE * wide
    high = scaled.astype(jnp.bfloat16)
    low = (scaled - high.astype(jnp.float32)).astype(jnp.bfloat16)
    return wide, jnp.concatenate([high, low], axis=0)


def source_kernel(half_ref, points_hbm, logmass_hbm, blocks_hbm, norm_ref, points, logmass, blocks, sems):
    halves = blocks.shape[1] - 1
    rows = pl.ds(pl.multiple_of(half_ref[0] * halves, halves), halves)
    at = pl.multiple_of(half_ref[0] * (halves * BLOCK), halves * BLOCK)
    pairs = [(points_hbm.at[:, pl.ds(at, halves * BLOCK)], points), (logmass_hbm.at[rows], logmass)]
    for copy in start_copies(pairs, sems):
        copy.wait()
    parts = split3(LOG2E * logmass[...])
    blocks[LEFT, halves] = jnp.concatenate([*parts, jnp.zeros_like(parts[0])], axis=0)
    blocks[RIGHT, halves] = jnp.zeros((BLOCK, BLOCK), jnp.bfloat16)

    part = halves // PARTS

    def one_block(b, carry):
        wide, both = scaled_block(points, b)
        norm_ref[pl.ds(b, 1), :] = 0.5 * jnp.sum(wide * wide, axis=0, keepdims=True)
        blocks[RIGHT, b] = both
        blocks[LEFT, b] = both.T
        return carry

    copies = []
    for k in range(PARTS):
        lax.fori_loop(k * part, (k + 1) * part, one_block, 0, unroll=4)
        own = (slice(None), pl.ds(k * part, part + (k == PARTS - 1)))
        copies.append(pltpu.make_async_copy(blocks.at[own], blocks_hbm.at[own], sems.at[2 + k]))
        copies[-1].start()
    for copy in copies:
        copy.wait()


def source(half, halves, points, logmass):
    blocks = (2, halves + 1, BLOCK, BLOCK)
    return pl.pallas_call(
        source_kernel,
        out_shape=[shape(blocks, jnp.bfloat16), shape((halves, BLOCK))],
        in_specs=[SMEM, HBM, HBM],
        out_specs=[HBM, VMEM],
        scratch_shapes=[
            pltpu.VMEM((D, halves * BLOCK), jnp.bfloat16),
            pltpu.VMEM((halves, BLOCK), jnp.float32),
            pltpu.VMEM(blocks, jnp.bfloat16),
            pltpu.SemaphoreType.DMA((2 + PARTS,)),
        ],
        compiler_params=PASS,
    )(half.reshape(1), points, logmass)


def field_bias(mass_ref, parts_ref):
    rows = parts_ref.shape[1]
    mass = whole([mass_ref[k * rows : (k + 1) * rows, :] for k in range(3)])
    return mass - log_sum([parts_ref[k] for k in range(parts_ref.shape[0])])


def potential_bias(mass_ref, chosen_refs, *refs):
    dot = functools.partial(jnp.dot, preferred_element_type=jnp.float32)
    mass = whole([mass_ref[0, : 2 * GROUP, :], mass_ref[0, 2 * GROUP :, :], mass_ref[1, : 2 * GROUP, :]])
    out = []
    for group in range(2):
        own = slice(group * GROUP, (group + 1) * GROUP)
        chosen = chosen_refs[group][...]
        sums = jnp.concatenate([ref[own, :] for ref in refs], axis=0)
        parts = sum(dot(chosen, part) for part in split3(sums))
        known = dot(chosen, jnp.ones_like(chosen)) > 0.5
        parts = jnp.where(known, parts, LOWEST)
        merged = log_sum([parts[k * GROUP : (k + 1) * GROUP] for k in range(len(refs))])
        out.append(mass[own, :] - merged)
    return jnp.concatenate(out, axis=0)


def unpack(raw, left, start_ref, mass_ref):
    def one_block(q, carry):
        block = raw[q, :D, :]
        left[q] = jnp.concatenate([block, block], axis=0).T
        rows = raw[q, D:, :].astype(jnp.float32)
        start_ref[pl.ds(q, 1), :] = rows[0:1] + rows[1:2] + rows[2:3]
        mass_ref[pl.ds(q, 1), :] = rows[3:4] + rows[4:5] + rows[5:6]
        return carry

    return lambda group: lax.fori_loop(group * GROUP, (group + 1) * GROUP, one_block, 0, unroll=8)


def pass_kernel(kind, *refs):
    columns, peaks, masses, list_ref, left_ref, right_ref, sems = refs[-7:]
    lefts, rights = columns.shape[0], right_ref.shape[0]
    part = lefts // PARTS
    left_parts = []
    if kind == FIRST:
        list_hbm, near_hbm, far_hbm, points_hbm, half_ref = refs[:5]
        out_ref, left_hbm, mass_ref, bias_ref, raw, points = refs[5:-7]
        own = rights * BLOCK
        at = pl.multiple_of(half_ref[0] * own, own)
        early = [(near_hbm, raw.at[pl.ds(0, GROUP)]), (far_hbm, raw.at[pl.ds(GROUP, GROUP)])]
        early.insert(0, (points_hbm.at[:, pl.ds(at, own)], points))
        late = []
    elif kind == ROWS:
        list_hbm, left_hbm, points_hbm = refs[:3]
        *col_parts, near_same, far_same, out_ref, bias_ref, mass = refs[3:-7]
        early = [(left_hbm.at[pl.ds(lefts, 2)], mass)]
        late = [(points_hbm.at[RIGHT, pl.ds(0, rights)], right_ref)]
        left_parts = [left_hbm.at[pl.ds(k * part, part)] for k in range(PARTS)]
    else:
        list_hbm, near_hbm, far_hbm, points_hbm, rows_ref, out_ref, bias_ref, mass = refs[:-7]
        early = [(points_hbm.at[LEFT, lefts], mass)]
        late = [(near_hbm, right_ref.at[pl.ds(0, GROUP)]), (far_hbm, right_ref.at[pl.ds(GROUP, GROUP)])]
        left_parts = [points_hbm.at[LEFT, pl.ds(k * part, part)] for k in range(PARTS)]
    late.append((list_hbm.at[pl.ds(0, list_ref.shape[0])], list_ref))
    pairs = early + late + [(ref, left_ref.at[pl.ds(k * part, part)]) for k, ref in enumerate(left_parts)]
    copies = start_copies(pairs, sems)
    peaks[...] = jnp.full_like(peaks, LOWEST)
    masses[...] = jnp.zeros_like(masses)
    for copy in copies[: len(early)]:
        copy.wait()
    if kind == FIRST:

        def scale(b, carry):
            right_ref[b] = scaled_block(points, b)[1]
            return carry

        lax.fori_loop(0, rights, scale, 0, unroll=8)
        unpack_group = unpack(raw, left_ref, bias_ref, mass_ref)
        for group in range(2):
            unpack_group(group)
        high, middle, low = split3(mass_ref[...])
        left_ref[lefts] = jnp.concatenate([high, middle], axis=0)
        left_ref[lefts + 1] = jnp.concatenate([low, jnp.zeros_like(low)], axis=0)
        hand_on = pltpu.make_async_copy(left_ref, left_hbm, sems.at[len(pairs)])
        hand_on.start()
    elif kind == ROWS:
        bias_ref[...] = potential_bias(mass, (near_same, far_same), *col_parts)
    else:
        bias_ref[...] = field_bias(mass, rows_ref)
    square = (BLOCK, BLOCK)
    lane = lax.broadcasted_iota(jnp.int32, square, 1)
    eye = jnp.where(lane == lax.broadcasted_iota(jnp.int32, square, 0), 1.0, 0.0).astype(jnp.bfloat16)
    lane = jnp.where(lane < 3 * GROUP, lane % GROUP, -1)
    for group in range(lefts // GROUP):
        high, middle, low = split3(bias_ref[group * GROUP : (group + 1) * GROUP, :])
        parts = jnp.concatenate([high, middle, low, jnp.zeros_like(high)], axis=0)
        turned = lax.dot_general(
            eye, parts, (((1,), (1,)), ((), ())), preferred_element_type=jnp.float32
        )

        def fill(k, carry, group=group, turned=turned):
            columns[group * GROUP + k] = jnp.where(lane == k, turned, 0.0).astype(jnp.bfloat16)
            return carry

        lax.fori_loop(0, GROUP, fill, 0, unroll=4)
    for copy in copies[len(early) : len(early) + len(late)]:
        copy.wait()
    rights_at = HEAD + (list_ref.shape[0] - HEAD) // 3
    ones = jnp.ones((BLOCK, 2 * BLOCK), jnp.bfloat16)

    def fold(copy, r, scores):
        scores = scores.reshape(BLOCK // 8, 8, BLOCK)
        old = peaks[copy, r]
        top = jnp.maximum(old, jnp.max(scores, axis=0))
        mass = jnp.sum(jnp.exp2(scores - top[None]), axis=0)
        masses[copy, r] = masses[copy, r] * jnp.exp2(old - top) + mass
        peaks[copy, r] = top

    def right_block(r):
        r = jnp.minimum(r, rights - 1)
        if kind != COLUMNS:
            return right_ref[r]
        block = right_ref[r, :D, :]
        return jnp.concatenate([block, block], axis=0)

    def wait_for(known, needed):
        if not left_parts:
            return known

        def wait(k, carry):
            at = pl.ds(k * part, part)
            source = left_hbm.at[at] if kind == ROWS else points_hbm.at[LEFT, at]
            pltpu.make_async_copy(source, left_ref.at[at], sems.at[len(early) + len(late) + k]).wait()
            return carry

        lax.fori_loop(known, needed, wait, 0)
        return jnp.maximum(known, needed)

    def step(start, count, t, known):
        known = wait_for(known, list_ref[HEAD + start + t * count + count - 1] // part + 1)
        for u in range(count):
            i = start + t * count + u
            l = list_ref[HEAD + i]
            first, second = list_ref[rights_at + 2 * i], list_ref[rights_at + 2 * i + 1]
            left = jnp.concatenate([left_ref[l], columns[l]], axis=1)
            right = jnp.concatenate([right_block(first), right_block(second)], axis=1)
            scores = jnp.dot(
                left, jnp.concatenate([right, ones], axis=0), preferred_element_type=jnp.float32
            )
            fold((2 * u) % COPIES, first, scores[:, :BLOCK])
            fold((2 * u + 1) % COPIES, second, scores[:, BLOCK:])
        return known

    known = lax.fori_loop(0, list_ref[0], functools.partial(step, 0, PAIRS), jnp.int32(0))
    known = lax.fori_loop(0, list_ref[1], functools.partial(step, list_ref[0] * PAIRS, TAIL), known)
    wait_for(known, PARTS)

    def finish(octet, carry):
        rows = []
        for k in range(8):
            r = octet * 8 + k
            tops = [peaks[copy, r] for copy in range(COPIES)]
            top = jnp.max(functools.reduce(jnp.maximum, tops), axis=0, keepdims=True)
            mass = sum(masses[copy, r] * jnp.exp2(tops[copy] - top) for copy in range(COPIES))
            rows.append(top + jnp.log2(jnp.sum(mass, axis=0, keepdims=True)))
        out_ref[0, pl.ds(pl.multiple_of(octet * 8, 8), 8), :] = jnp.concatenate(rows, axis=0)
        return carry

    lax.fori_loop(0, rights // 8, finish, 0)
    for k in range(1, out_ref.shape[0]):
        out_ref[k] = out_ref[0]
    if kind == FIRST:
        hand_on.wait()


def log_sums(kind, pairs, halves, remotes, parts, copies):
    slots = 2 * GROUP
    lefts, rights = (halves, slots) if kind == COLUMNS else (slots, halves)
    rows = D + EXTRA if kind == COLUMNS else BLOCK
    held = lefts
    outs, bias = [shape((copies, rights, BLOCK))], pltpu.VMEM((lefts, BLOCK), jnp.float32)
    if kind == FIRST:
        held = lefts + 2
        outs.append(shape((held, BLOCK, BLOCK), jnp.bfloat16))
        scratch = [bias, bias, pltpu.VMEM((slots, D + EXTRA, BLOCK), jnp.bfloat16)]
        scratch.append(pltpu.VMEM((D, halves * BLOCK), jnp.bfloat16))
    elif kind == ROWS:
        scratch = [bias, pltpu.VMEM((2, BLOCK, BLOCK), jnp.bfloat16)]
    else:
        outs.append(shape((lefts, BLOCK)))
        scratch = [pltpu.VMEM((BLOCK, BLOCK), jnp.bfloat16)]
    return pl.pallas_call(
        functools.partial(pass_kernel, kind),
        out_shape=outs,
        in_specs=[HBM] * (1 + len(remotes)) + [SMEM if kind == FIRST else VMEM] * len(parts),
        out_specs=[VMEM, HBM] if kind == FIRST else [VMEM] * len(outs),
        scratch_shapes=scratch
        + [
            pltpu.VMEM((lefts, BLOCK, BLOCK), jnp.bfloat16),
            pltpu.VMEM((COPIES, rights + 1, 8, BLOCK), jnp.float32),
            pltpu.VMEM((COPIES, rights + 1, 8, BLOCK), jnp.float32),
            pltpu.SMEM(list_shape(halves), jnp.int32),
            pltpu.VMEM((held, BLOCK, BLOCK), jnp.bfloat16),
            pltpu.VMEM((rights, rows, BLOCK), jnp.bfloat16),
            pltpu.SemaphoreType.DMA((5 + PARTS,)),
        ],
        compiler_params=PREPARE if kind == FIRST else PASS,
    )(pairs, *remotes, *parts)


def ring(values, axis, size, stride=1):
    places = lax.axis_size(axis)
    out = [values]
    for d in range(1, size):
        pairs = []
        for i in range(places):
            place = i // stride % size
            pairs.append((i, i + ((place + d) % size - place) * stride))
        out.append(lax.ppermute(values, axis, pairs))
    return out


def shards(
    source_points,
    source_logmass,
    target_points,
    target_logmass,
    target_potential,
    tile_slot,
    tile_counts,
    fetch_ids,
):
    peers = lax.axis_size("src")
    blocks = tile_counts.shape[0]
    halves = blocks // 2
    per_peer = fetch_ids.shape[1]
    owned = target_potential.shape[0] // BLOCK
    count = peers * per_peer
    place = lax.axis_index("src")
    half = lax.axis_index("grp") % 2

    def swap(values):
        return ring(values, "grp", 2, 1)[1]

    tiles = [tile_slot.T, tile_counts.T]
    ids = ring(fetch_ids, "src", peers)
    ids, tiles = lax.optimization_barrier((ids, tiles + [swap(part) for part in tiles]))
    packed, target_half = pack(
        place,
        ids,
        target_points.T,
        target_potential.reshape(owned, BLOCK),
        target_logmass.reshape(owned, BLOCK),
    )
    (row_pairs,) = make_list(rows_kernel, half, tiles)
    fetched = lax.all_to_all(packed, "src", split_axis=0, concat_axis=0, tiled=True)
    fetched, row_pairs, ids, tiles = lax.optimization_barrier((fetched, row_pairs, ids, tiles))
    col_pairs, same = make_list(columns_kernel, half, tiles + ids)
    *both, col_pairs, same = lax.optimization_barrier((fetched, swap(fetched), col_pairs, same))
    same = [same, swap(same)]

    groups = lax.axis_size("grp")
    same_core = [list(range(core, groups, 2)) for core in range(2)]
    for sweep_index in range(ITERS):
        if sweep_index == 0:
            turned = source_points.T
            rows, targets = log_sums(FIRST, row_pairs, halves, [*both, turned], [half.reshape(1)], groups // 2)
            rows, turned, logmass = lax.optimization_barrier((rows, turned, source_logmass))
            points, source_half = source(half, halves, turned, logmass.reshape(blocks, BLOCK))
        else:
            (rows,) = log_sums(ROWS, row_pairs, halves, [targets, points], col_parts + same, groups // 2)
        rows = lax.all_to_all(
            rows, "grp", split_axis=0, concat_axis=0, tiled=True, axis_index_groups=same_core
        )
        cols, field = log_sums(COLUMNS, col_pairs, halves, [*both, points], [rows], 1)
        cols = cols[0]
        if sweep_index < ITERS - 1:
            other = swap(cols)
            cols = log_sum([cols, jnp.concatenate([other[count:], other[:count]], axis=0)])
            col_parts = ring(cols, "src", peers)
    field = field * (1.0 / SCALE) + source_half
    other = swap(field)
    low = half == 0
    source_field = jnp.concatenate([jnp.where(low, field, other), jnp.where(low, other, field)], axis=0)

    cols = log_sum([cols[:count], swap(cols[count:])]).reshape(peers, per_peer, BLOCK)
    cols, last_place, ids, target_half, target_logmass = lax.optimization_barrier(
        (cols, place, ids, target_half, target_logmass)
    )
    back = []
    for d in range(peers):
        wanted = lax.dynamic_slice(cols, ((last_place + d) % peers, 0, 0), (1, per_peer, BLOCK))[0]
        pairs = [(i, (i + d) % peers) for i in range(peers)]
        back.append(wanted if d == 0 else lax.ppermute(wanted, "src", pairs))
    target_field = merge(last_place, back, ids, target_logmass.reshape(owned, BLOCK), target_half).reshape(-1)
    return (source_field.reshape(-1), target_field)


def solution(mesh):
    return jax.shard_map(
        shards,
        mesh=mesh,
        in_specs=(
            P("src", None),
            P("src"),
            P(("src", "grp"), None),
            P(("src", "grp")),
            P(("src", "grp")),
            P("src", "grp"),
            P("src", "grp"),
            P("src", "grp"),
        ),
        out_specs=(P("src"), P(("src", "grp"))),
        check_vma=False,
    )
```

```python
import functools

import jax
import jax.numpy as jnp
from jax import lax
from jax.experimental import pallas as pl
from jax.experimental.pallas import tpu as pltpu
from jax.sharding import PartitionSpec as P

D = 64
BLOCK = 128
KG = 8
ITERS = 3
EPSILON = 0.25
LOWEST = -1e30
LOG2E = 1.4426950408889634
SCALE = LOG2E / EPSILON
PAIRS = 64
TAIL = 16
COPIES = 2
GROUP = 32
CAP = 8
EXTRA = 6
LEFT, RIGHT = 0, 1
FIRST, ROWS, COLUMNS = 0, 1, 2
PARTS = 4
LONG = 1024 * 1024
HEAD = 8
STRIDE = 64


SMEM = pl.BlockSpec(memory_space=pltpu.SMEM)
VMEM = pl.BlockSpec(memory_space=pltpu.VMEM)
HBM = pl.BlockSpec(memory_space=pltpu.HBM)
MIB = 1024 * 1024
PREPARE = pltpu.CompilerParams(vmem_limit_bytes=64 * MIB)
PASS = pltpu.CompilerParams(vmem_limit_bytes=53 * MIB)


def shape(dims, dtype=jnp.float32):
    return jax.ShapeDtypeStruct(dims, dtype)


def start_copies(pairs, sems):
    copies = [pltpu.make_async_copy(src, dst, sems.at[k]) for k, (src, dst) in enumerate(pairs)]
    for copy in copies:
        copy.start()
    return copies


def close_list(ref, hbm, pairs, last, none, sems):
    right = HEAD + (ref.shape[0] - HEAD) // 3
    tails = (pairs + TAIL - 1) // TAIL
    ref[0] = tails // (PAIRS // TAIL)
    ref[1] = tails % (PAIRS // TAIL)

    def pad(k, carry):
        ref[HEAD + pairs + k] = last
        ref[right + 2 * (pairs + k)] = none
        ref[right + 2 * (pairs + k) + 1] = none
        return carry

    lax.fori_loop(0, tails * TAIL - pairs, pad, 0)
    copy = pltpu.make_async_copy(ref, hbm.at[pl.ds(0, ref.shape[0])], sems.at[0])
    copy.start()
    return copy


def columns_kernel(half_ref, *refs):
    remotes, (hbm, same_ref), locals_ = refs[:8], refs[8:10], refs[10:]
    *tables, ref, rows, sems = locals_
    copies = start_copies(list(zip(remotes, tables)), sems)
    for copy in copies:
        copy.wait()
    groups, ids = (tables[0:2], tables[2:4]), tables[4:]
    halves = tables[0].shape[1] // 2
    first = half_ref[0] * halves
    right = HEAD + (ref.shape[0] - HEAD) // 3

    def one_block(b, position):
        at = right + 2 * position
        tiles = jnp.int32(0)
        for group, (slots_ref, counts_ref) in enumerate(groups):
            for k in range(KG):
                ref[at + tiles + k] = slots_ref[k, first + b] + group * GROUP
            tiles = tiles + counts_ref[0, first + b]
        ref[at + tiles] = 2 * GROUP
        for k in range(KG):
            ref[HEAD + position + k] = b
        return position + (tiles + 1) // 2

    copy = close_list(ref, hbm, lax.fori_loop(0, halves, one_block, jnp.int32(0)), halves - 1, 2 * GROUP, sems)
    peers, per_peer = ids[0].shape
    lane = lax.broadcasted_iota(jnp.int32, (1, BLOCK), 1)
    known = jnp.zeros((1, BLOCK), jnp.int32)
    for d in range(peers):
        for p in range(peers):
            for c in range(per_peer):
                known = jnp.where(lane == (d * peers + p) * per_peer + c, ids[d][p, c], known)
    for p in range(peers):
        for c in range(per_peer):
            q = p * per_peer + c
            same = jnp.logical_and(known == ids[0][p, c], lane // per_peer % peers == p)
            for d in range(peers):
                own = jnp.logical_and(same, lane // GROUP == d)
                rows[pl.ds(d * GROUP + q, 1), :] = jnp.where(own, 1.0, 0.0)
    same_ref[...] = rows[...].astype(jnp.bfloat16)
    copy.wait()


def rows_kernel(half_ref, *refs):
    remotes, hbm, locals_ = refs[:4], refs[4], refs[5:]
    *tables, ref, lists, sizes, sems = locals_
    copies = start_copies(list(zip(remotes, tables)), sems)
    groups = (tables[0:2], tables[2:4])
    halves = tables[0].shape[1] // 2
    slots = 2 * GROUP
    first = half_ref[0] * halves
    right = HEAD + (ref.shape[0] - HEAD) // 3

    def clear(q, carry):
        sizes[q] = 0
        return carry

    lax.fori_loop(0, slots + 1, clear, 0, unroll=13)
    for copy in copies:
        copy.wait()

    def one_block(b, carry):
        def append(named):
            known = [sizes[slot] for slot in named]
            for slot, size in zip(named, known):
                lists[slot * STRIDE + size] = b
            for slot, size in zip(named, known):
                sizes[slot] = size + 1

        append([table[k, first + b] + group * GROUP for group, (table, _) in enumerate(groups) for k in range(2)])
        for group, (table, counts_ref) in enumerate(groups):
            count = counts_ref[0, first + b]

            def more(table=table, group=group, count=count):
                append(
                    [jnp.where(k < count, table[k, first + b] + group * GROUP, slots) for k in range(2, KG)]
                )

            pl.when(count > 2)(more)
        return carry

    lax.fori_loop(0, halves, one_block, 0)
    batch = 4

    def one_pair(q, position, k):
        ref[HEAD + position + k] = q
        for j in range(2):
            ref[right + 2 * (position + k) + j] = lists[q * STRIDE + 2 * k + j]

    def some_slots(t, position):
        counted = [sizes[t * batch + j] for j in range(batch)]
        for j, size in enumerate(counted):
            lists[(t * batch + j) * STRIDE + size] = halves
        counted = [(size + 1) // 2 for size in counted]
        places = [position]
        for pairs in counted:
            places.append(places[-1] + pairs)
        for j in range(batch):
            for k in range(3):
                one_pair(t * batch + j, places[j], k)

        def rest():
            for j in range(batch):

                def another(k, carry, j=j):
                    one_pair(t * batch + j, places[j], k)
                    return carry

                lax.fori_loop(3, counted[j], another, 0)

        pl.when(functools.reduce(jnp.maximum, counted) > 3)(rest)
        return places[-1]

    pairs = lax.fori_loop(0, slots // batch, some_slots, jnp.int32(0))
    close_list(ref, hbm, pairs, slots - 1, halves, sems).wait()


def list_shape(halves):
    room = HEAD + 3 * (halves * KG + 2 * GROUP + PAIRS + KG)
    return ((room + 1023) // 1024 * 1024,)


def make_list(kernel, half, remotes):
    own = [pltpu.SMEM(value.shape, value.dtype) for value in remotes]
    own.append(pltpu.SMEM(list_shape(remotes[0].shape[1] // 2), jnp.int32))
    outs, specs = [shape((LONG,), jnp.int32)], [HBM]
    if kernel is rows_kernel:
        own.append(pltpu.SMEM(((2 * GROUP + 1) * STRIDE,), jnp.int32))
        own.append(pltpu.SMEM((2 * GROUP + 1,), jnp.int32))
    else:
        own.append(pltpu.VMEM((BLOCK, BLOCK), jnp.float32))
        outs.append(shape((BLOCK, BLOCK), jnp.bfloat16))
        specs.append(VMEM)
    return pl.pallas_call(
        kernel,
        out_shape=outs,
        in_specs=[SMEM] + [HBM] * len(remotes),
        out_specs=specs,
        scratch_shapes=[*own, pltpu.SemaphoreType.DMA((len(remotes),))],
        compiler_params=PREPARE,
    )(half.reshape(1), *remotes)


def split3(values):
    high = values.astype(jnp.bfloat16)
    rest = values - high.astype(jnp.float32)
    middle = rest.astype(jnp.bfloat16)
    low = (rest - middle.astype(jnp.float32)).astype(jnp.bfloat16)
    return high, middle, low


def whole(parts):
    high, middle, low = [part.astype(jnp.float32) for part in parts]
    return high + middle + low


def log_sum(values):
    top = functools.reduce(jnp.maximum, values)
    return top + jnp.log2(sum(jnp.exp2(value - top) for value in values))


def pack_kernel(place_ref, *refs):
    count = (len(refs) - 3) // 2
    remotes, (out_ref, norm_ref, *locals_, sems) = refs[:count], refs[count:]
    *ids_refs, points, potential, logmass = locals_
    copies = start_copies(list(zip(remotes, locals_)), sems)
    place = place_ref[0]
    peers, per_peer = ids_refs[0].shape
    for copy in copies:
        copy.wait()

    def one_norm(t, carry):
        wide = points[:, pl.ds(pl.multiple_of(t * BLOCK, BLOCK), BLOCK)].astype(jnp.float32)
        norm_ref[pl.ds(t, 1), :] = 0.5 * jnp.sum(wide * wide, axis=0, keepdims=True)
        return carry

    lax.fori_loop(0, norm_ref.shape[0], one_norm, 0, unroll=8)
    for d, ids_ref in enumerate(ids_refs):
        other = lax.rem(place - d + peers, peers)
        rows = []
        for c in range(per_peer):
            t = ids_ref[place, c]
            block = points[:, pl.ds(pl.multiple_of(t * BLOCK, BLOCK), BLOCK)]
            start = SCALE * (potential[pl.ds(t, 1), :] - norm_ref[pl.ds(t, 1), :])
            mass = LOG2E * logmass[pl.ds(t, 1), :]
            rows += [part.astype(jnp.float32) for part in split3(start) + split3(mass)]
            out_ref[other, c * D : (c + 1) * D, :] = block
        out_ref[other, per_peer * D :, :] = jnp.concatenate(rows, axis=0).astype(jnp.bfloat16)


def pack(place, ids, *values):
    remotes = [*ids, *values]
    return pl.pallas_call(
        pack_kernel,
        out_shape=[shape((len(ids), CAP * (D + EXTRA), BLOCK), jnp.bfloat16), shape(values[1].shape)],
        in_specs=[SMEM] + [HBM] * len(remotes),
        out_specs=[VMEM, VMEM],
        scratch_shapes=[pltpu.SMEM(value.shape, value.dtype) for value in ids]
        + [pltpu.VMEM(value.shape, value.dtype) for value in values]
        + [pltpu.SemaphoreType.DMA((len(remotes),))],
        compiler_params=PREPARE,
    )(place.reshape(1), *remotes)


def merge_kernel(peers, place_ref, *refs):
    sums, ids, (logmass_ref, norm_ref, out_ref, parts) = refs[:peers], refs[peers : 2 * peers], refs[2 * peers :]
    place = place_ref[0]
    parts[...] = jnp.full_like(parts, LOWEST)
    for d in range(peers):
        for c in range(sums[d].shape[0]):
            parts[d, pl.ds(ids[d][place, c], 1), :] = sums[d][c : c + 1, :]
    merged = log_sum([parts[d] for d in range(peers)])
    out_ref[...] = (LOG2E * logmass_ref[...] - merged) * (1.0 / SCALE) + norm_ref[...]


def merge(place, sums, ids, logmass, norm):
    peers = len(ids)
    return pl.pallas_call(
        functools.partial(merge_kernel, peers),
        out_shape=shape(norm.shape),
        in_specs=[SMEM] + [VMEM] * peers + [SMEM] * peers + [VMEM] * 2,
        out_specs=VMEM,
        scratch_shapes=[pltpu.VMEM((peers, *norm.shape), jnp.float32)],
        compiler_params=PASS,
    )(place.reshape(1), *sums, *ids, logmass, norm)


def scaled_block(points, b):
    wide = points[:, pl.ds(pl.multiple_of(b * BLOCK, BLOCK), BLOCK)].astype(jnp.float32)
    scaled = SCALE * wide
    high = scaled.astype(jnp.bfloat16)
    low = (scaled - high.astype(jnp.float32)).astype(jnp.bfloat16)
    return wide, jnp.concatenate([high, low], axis=0)


def source_kernel(half_ref, points_hbm, logmass_hbm, blocks_hbm, norm_ref, points, logmass, blocks, sems):
    halves = blocks.shape[1] - 1
    rows = pl.ds(pl.multiple_of(half_ref[0] * halves, halves), halves)
    at = pl.multiple_of(half_ref[0] * (halves * BLOCK), halves * BLOCK)
    pairs = [(points_hbm.at[:, pl.ds(at, halves * BLOCK)], points), (logmass_hbm.at[rows], logmass)]
    for copy in start_copies(pairs, sems):
        copy.wait()
    parts = split3(LOG2E * logmass[...])
    blocks[LEFT, halves] = jnp.concatenate([*parts, jnp.zeros_like(parts[0])], axis=0)
    blocks[RIGHT, halves] = jnp.zeros((BLOCK, BLOCK), jnp.bfloat16)

    part = halves // PARTS

    def one_block(b, carry):
        wide, both = scaled_block(points, b)
        norm_ref[pl.ds(b, 1), :] = 0.5 * jnp.sum(wide * wide, axis=0, keepdims=True)
        blocks[RIGHT, b] = both
        blocks[LEFT, b] = both.T
        return carry

    copies = []
    for k in range(PARTS):
        lax.fori_loop(k * part, (k + 1) * part, one_block, 0, unroll=4)
        own = (slice(None), pl.ds(k * part, part + (k == PARTS - 1)))
        copies.append(pltpu.make_async_copy(blocks.at[own], blocks_hbm.at[own], sems.at[2 + k]))
        copies[-1].start()
    for copy in copies:
        copy.wait()


def source(half, halves, points, logmass):
    blocks = (2, halves + 1, BLOCK, BLOCK)
    return pl.pallas_call(
        source_kernel,
        out_shape=[shape(blocks, jnp.bfloat16), shape((halves, BLOCK))],
        in_specs=[SMEM, HBM, HBM],
        out_specs=[HBM, VMEM],
        scratch_shapes=[
            pltpu.VMEM((D, halves * BLOCK), jnp.bfloat16),
            pltpu.VMEM((halves, BLOCK), jnp.float32),
            pltpu.VMEM(blocks, jnp.bfloat16),
            pltpu.SemaphoreType.DMA((2 + PARTS,)),
        ],
        compiler_params=PASS,
    )(half.reshape(1), points, logmass)


def field_bias(mass_ref, parts_ref):
    rows = parts_ref.shape[1]
    mass = whole([mass_ref[k * rows : (k + 1) * rows, :] for k in range(3)])
    return mass - log_sum([parts_ref[k] for k in range(parts_ref.shape[0])])


def potential_bias(mass_ref, chosen_refs, *refs):
    dot = functools.partial(jnp.dot, preferred_element_type=jnp.float32)
    mass = whole([mass_ref[0, : 2 * GROUP, :], mass_ref[0, 2 * GROUP :, :], mass_ref[1, : 2 * GROUP, :]])
    out = []
    for group in range(2):
        own = slice(group * GROUP, (group + 1) * GROUP)
        chosen = chosen_refs[group][...]
        sums = jnp.concatenate([ref[own, :] for ref in refs], axis=0)
        parts = sum(dot(chosen, part) for part in split3(sums))
        known = dot(chosen, jnp.ones_like(chosen)) > 0.5
        parts = jnp.where(known, parts, LOWEST)
        merged = log_sum([parts[k * GROUP : (k + 1) * GROUP] for k in range(len(refs))])
        out.append(mass[own, :] - merged)
    return jnp.concatenate(out, axis=0)


def unpack(raw, left, start_ref, mass_ref):
    def one_peer(peer, carry):
        rows = raw[peer, CAP * D :, :].astype(jnp.float32)
        for c in range(CAP):
            q = peer * CAP + c
            block = raw[peer, c * D : (c + 1) * D, :]
            left[q] = jnp.concatenate([block, block], axis=0).T
            high, middle, low, *mass = [rows[EXTRA * c + k : EXTRA * c + k + 1] for k in range(EXTRA)]
            start_ref[pl.ds(q, 1), :] = high + middle + low
            mass_ref[pl.ds(q, 1), :] = mass[0] + mass[1] + mass[2]
        return carry

    lax.fori_loop(0, raw.shape[0], one_peer, 0)


def pass_kernel(kind, *refs):
    columns, peaks, masses, list_ref, left_ref, right_ref, sems = refs[-7:]
    lefts, rights = columns.shape[0], peaks.shape[1] - 1
    peers = GROUP // CAP
    part = lefts // PARTS
    left_parts = []
    if kind == FIRST:
        list_hbm, near_hbm, far_hbm, points_hbm, half_ref = refs[:5]
        out_ref, left_hbm, mass_ref, bias_ref, raw, points = refs[5:-7]
        own = rights * BLOCK
        at = pl.multiple_of(half_ref[0] * own, own)
        early = [(near_hbm, raw.at[pl.ds(0, peers)]), (far_hbm, raw.at[pl.ds(peers, peers)])]
        early.insert(0, (points_hbm.at[:, pl.ds(at, own)], points))
        late = []
    elif kind == ROWS:
        list_hbm, left_hbm, points_hbm = refs[:3]
        *col_parts, near_same, far_same, out_ref, bias_ref, mass = refs[3:-7]
        early = [(left_hbm.at[pl.ds(lefts, 2)], mass)]
        late = [(points_hbm.at[RIGHT, pl.ds(0, rights)], right_ref)]
        left_parts = [left_hbm.at[pl.ds(k * part, part)] for k in range(PARTS)]
    else:
        list_hbm, near_hbm, far_hbm, points_hbm, rows_ref, out_ref, bias_ref, mass = refs[:-7]
        early = [(points_hbm.at[LEFT, lefts], mass)]
        late = [
            (raw_hbm.at[:, pl.ds(0, CAP * D)], right_ref.at[pl.ds(group * peers, peers)])
            for group, raw_hbm in enumerate((near_hbm, far_hbm))
        ]
        left_parts = [points_hbm.at[LEFT, pl.ds(k * part, part)] for k in range(PARTS)]
    late.append((list_hbm.at[pl.ds(0, list_ref.shape[0])], list_ref))
    pairs = early + late + [(ref, left_ref.at[pl.ds(k * part, part)]) for k, ref in enumerate(left_parts)]
    copies = start_copies(pairs, sems)
    peaks[...] = jnp.full_like(peaks, LOWEST)
    masses[...] = jnp.zeros_like(masses)
    for copy in copies[: len(early)]:
        copy.wait()
    if kind == FIRST:

        def scale(b, carry):
            right_ref[b] = scaled_block(points, b)[1]
            return carry

        lax.fori_loop(0, rights, scale, 0, unroll=8)
        unpack(raw, left_ref, bias_ref, mass_ref)
        high, middle, low = split3(mass_ref[...])
        left_ref[lefts] = jnp.concatenate([high, middle], axis=0)
        left_ref[lefts + 1] = jnp.concatenate([low, jnp.zeros_like(low)], axis=0)
        hand_on = pltpu.make_async_copy(left_ref, left_hbm, sems.at[len(pairs)])
        hand_on.start()
    elif kind == ROWS:
        bias_ref[...] = potential_bias(mass, (near_same, far_same), *col_parts)
    else:
        bias_ref[...] = field_bias(mass, rows_ref)
    square = (BLOCK, BLOCK)
    lane = lax.broadcasted_iota(jnp.int32, square, 1)
    eye = jnp.where(lane == lax.broadcasted_iota(jnp.int32, square, 0), 1.0, 0.0).astype(jnp.bfloat16)
    lane = jnp.where(lane < 3 * GROUP, lane % GROUP, -1)
    for group in range(lefts // GROUP):
        high, middle, low = split3(bias_ref[group * GROUP : (group + 1) * GROUP, :])
        parts = jnp.concatenate([high, middle, low, jnp.zeros_like(high)], axis=0)
        turned = lax.dot_general(
            eye, parts, (((1,), (1,)), ((), ())), preferred_element_type=jnp.float32
        )

        def fill(k, carry, group=group, turned=turned):
            columns[group * GROUP + k] = jnp.where(lane == k, turned, 0.0).astype(jnp.bfloat16)
            return carry

        lax.fori_loop(0, GROUP, fill, 0, unroll=4)
    for copy in copies[len(early) : len(early) + len(late)]:
        copy.wait()
    rights_at = HEAD + (list_ref.shape[0] - HEAD) // 3
    ones = jnp.ones((BLOCK, 2 * BLOCK), jnp.bfloat16)

    def fold(copy, r, scores):
        scores = scores.reshape(BLOCK // 8, 8, BLOCK)
        old = peaks[copy, r]
        top = jnp.maximum(old, jnp.max(scores, axis=0))
        mass = jnp.sum(jnp.exp2(scores - top[None]), axis=0)
        masses[copy, r] = masses[copy, r] * jnp.exp2(old - top) + mass
        peaks[copy, r] = top

    def right_block(r):
        r = jnp.minimum(r, rights - 1)
        if kind != COLUMNS:
            return right_ref[r]
        block = right_ref[r // CAP, pl.ds(pl.multiple_of(r % CAP * D, D), D), :]
        return jnp.concatenate([block, block], axis=0)

    def wait_for(known, needed):
        if not left_parts:
            return known

        def wait(k, carry):
            at = pl.ds(k * part, part)
            source = left_hbm.at[at] if kind == ROWS else points_hbm.at[LEFT, at]
            pltpu.make_async_copy(source, left_ref.at[at], sems.at[len(early) + len(late) + k]).wait()
            return carry

        lax.fori_loop(known, needed, wait, 0)
        return jnp.maximum(known, needed)

    def step(start, count, t, known):
        known = wait_for(known, list_ref[HEAD + start + t * count + count - 1] // part + 1)
        for u in range(count):
            i = start + t * count + u
            l = list_ref[HEAD + i]
            first, second = list_ref[rights_at + 2 * i], list_ref[rights_at + 2 * i + 1]
            left = jnp.concatenate([left_ref[l], columns[l]], axis=1)
            right = jnp.concatenate([right_block(first), right_block(second)], axis=1)
            scores = jnp.dot(
                left, jnp.concatenate([right, ones], axis=0), preferred_element_type=jnp.float32
            )
            fold((2 * u) % COPIES, first, scores[:, :BLOCK])
            fold((2 * u + 1) % COPIES, second, scores[:, BLOCK:])
        return known

    known = lax.fori_loop(0, list_ref[0], functools.partial(step, 0, PAIRS), jnp.int32(0))
    known = lax.fori_loop(0, list_ref[1], functools.partial(step, list_ref[0] * PAIRS, TAIL), known)
    wait_for(known, PARTS)

    def finish(octet, carry):
        rows = []
        for k in range(8):
            r = octet * 8 + k
            tops = [peaks[copy, r] for copy in range(COPIES)]
            top = jnp.max(functools.reduce(jnp.maximum, tops), axis=0, keepdims=True)
            mass = sum(masses[copy, r] * jnp.exp2(tops[copy] - top) for copy in range(COPIES))
            rows.append(top + jnp.log2(jnp.sum(mass, axis=0, keepdims=True)))
        out_ref[0, pl.ds(pl.multiple_of(octet * 8, 8), 8), :] = jnp.concatenate(rows, axis=0)
        return carry

    lax.fori_loop(0, rights // 8, finish, 0)
    for k in range(1, out_ref.shape[0]):
        out_ref[k] = out_ref[0]
    if kind == FIRST:
        hand_on.wait()


def log_sums(kind, pairs, halves, remotes, parts, copies, keep=False):
    slots = 2 * GROUP
    lefts, rights = (halves, slots) if kind == COLUMNS else (slots, halves)
    form = (2 * GROUP // CAP, CAP * D, BLOCK) if kind == COLUMNS else (rights, BLOCK, BLOCK)
    held = lefts
    outs, bias = [shape((copies, rights, BLOCK))], pltpu.VMEM((lefts, BLOCK), jnp.float32)
    if kind == FIRST:
        held = lefts + 2
        outs.append(shape((held, BLOCK, BLOCK), jnp.bfloat16))
        scratch = [bias, bias, pltpu.VMEM((2 * GROUP // CAP, CAP * (D + EXTRA), BLOCK), jnp.bfloat16)]
        scratch.append(pltpu.VMEM((D, halves * BLOCK), jnp.bfloat16))
    elif kind == ROWS:
        scratch = [bias, pltpu.VMEM((2, BLOCK, BLOCK), jnp.bfloat16)]
    else:
        scratch = [pltpu.VMEM((BLOCK, BLOCK), jnp.bfloat16)]
        if keep:
            outs.append(shape((lefts, BLOCK)))
        else:
            scratch.insert(0, bias)
    return pl.pallas_call(
        functools.partial(pass_kernel, kind),
        out_shape=outs,
        in_specs=[HBM] * (1 + len(remotes)) + [SMEM if kind == FIRST else VMEM] * len(parts),
        out_specs=[VMEM, HBM] if kind == FIRST else [VMEM] * len(outs),
        scratch_shapes=scratch
        + [
            pltpu.VMEM((lefts, BLOCK, BLOCK), jnp.bfloat16),
            pltpu.VMEM((COPIES, rights + 1, 8, BLOCK), jnp.float32),
            pltpu.VMEM((COPIES, rights + 1, 8, BLOCK), jnp.float32),
            pltpu.SMEM(list_shape(halves), jnp.int32),
            pltpu.VMEM((held, BLOCK, BLOCK), jnp.bfloat16),
            pltpu.VMEM(form, jnp.bfloat16),
            pltpu.SemaphoreType.DMA((5 + PARTS,)),
        ],
        compiler_params=PREPARE if kind == FIRST else PASS,
    )(pairs, *remotes, *parts)


def ring(values, axis, size, stride=1):
    places = lax.axis_size(axis)
    out = [values]
    for d in range(1, size):
        pairs = []
        for i in range(places):
            place = i // stride % size
            pairs.append((i, i + ((place + d) % size - place) * stride))
        out.append(lax.ppermute(values, axis, pairs))
    return out


def shards(
    source_points,
    source_logmass,
    target_points,
    target_logmass,
    target_potential,
    tile_slot,
    tile_counts,
    fetch_ids,
):
    peers = lax.axis_size("src")
    blocks = tile_counts.shape[0]
    halves = blocks // 2
    per_peer = fetch_ids.shape[1]
    owned = target_potential.shape[0] // BLOCK
    count = peers * per_peer
    place = lax.axis_index("src")
    half = lax.axis_index("grp") % 2

    def swap(values):
        return ring(values, "grp", 2, 1)[1]

    tiles = [tile_slot.T, tile_counts.T]
    ids = ring(fetch_ids, "src", peers)
    ids, tiles = lax.optimization_barrier((ids, tiles + [swap(part) for part in tiles]))
    packed, target_half = pack(
        place,
        ids,
        target_points.T,
        target_potential.reshape(owned, BLOCK),
        target_logmass.reshape(owned, BLOCK),
    )
    (row_pairs,) = make_list(rows_kernel, half, tiles)
    fetched = lax.all_to_all(packed, "src", split_axis=0, concat_axis=0, tiled=True)
    fetched, row_pairs, ids, tiles = lax.optimization_barrier((fetched, row_pairs, ids, tiles))
    col_pairs, same = make_list(columns_kernel, half, tiles + ids)
    *both, col_pairs, same = lax.optimization_barrier((fetched, swap(fetched), col_pairs, same))
    same = [same, swap(same)]

    groups = lax.axis_size("grp")
    same_core = [list(range(core, groups, 2)) for core in range(2)]
    for sweep_index in range(ITERS):
        if sweep_index == 0:
            turned = source_points.T
            rows, targets = log_sums(FIRST, row_pairs, halves, [*both, turned], [half.reshape(1)], groups // 2)
            rows, turned, logmass = lax.optimization_barrier((rows, turned, source_logmass))
            points, source_half = source(half, halves, turned, logmass.reshape(blocks, BLOCK))
        else:
            (rows,) = log_sums(ROWS, row_pairs, halves, [targets, points], col_parts + same, groups // 2)
        rows = lax.all_to_all(
            rows, "grp", split_axis=0, concat_axis=0, tiled=True, axis_index_groups=same_core
        )
        last = sweep_index == ITERS - 1
        cols, *fields = log_sums(COLUMNS, col_pairs, halves, [*both, points], [rows], 1, keep=last)
        cols = cols[0]
        if sweep_index < ITERS - 1:
            other = swap(cols)
            cols = log_sum([cols, jnp.concatenate([other[count:], other[:count]], axis=0)])
            col_parts = ring(cols, "src", peers)
    field = fields[0] * (1.0 / SCALE) + source_half
    other = swap(field)
    low = half == 0
    source_field = jnp.concatenate([jnp.where(low, field, other), jnp.where(low, other, field)], axis=0)

    cols = log_sum([cols[:count], swap(cols[count:])]).reshape(peers, per_peer, BLOCK)
    cols, last_place, ids, target_half, target_logmass = lax.optimization_barrier(
        (cols, place, ids, target_half, target_logmass)
    )
    back = []
    for d in range(peers):
        wanted = lax.dynamic_slice(cols, ((last_place + d) % peers, 0, 0), (1, per_peer, BLOCK))[0]
        pairs = [(i, (i + d) % peers) for i in range(peers)]
        back.append(wanted if d == 0 else lax.ppermute(wanted, "src", pairs))
    target_field = merge(last_place, back, ids, target_logmass.reshape(owned, BLOCK), target_half).reshape(-1)
    return (source_field.reshape(-1), target_field)


def solution(mesh):
    return jax.shard_map(
        shards,
        mesh=mesh,
        in_specs=(
            P("src", None),
            P("src"),
            P(("src", "grp"), None),
            P(("src", "grp")),
            P(("src", "grp")),
            P("src", "grp"),
            P("src", "grp"),
            P("src", "grp"),
        ),
        out_specs=(P("src"), P(("src", "grp"))),
        check_vma=False,
    )
```

```python
import functools

import jax
import jax.numpy as jnp
from jax import lax
from jax.experimental import pallas as pl
from jax.experimental.pallas import tpu as pltpu
from jax.sharding import PartitionSpec as P

D = 64
BLOCK = 128
KG = 8
ITERS = 3
EPSILON = 0.25
LOWEST = -1e30
LOG2E = 1.4426950408889634
SCALE = LOG2E / EPSILON
PAIRS = 64
TAIL = 16
COPIES = 2
GROUP = 32
CAP = 8
EXTRA = 6
LEFT, RIGHT = 0, 1
FIRST, ROWS, COLUMNS = 0, 1, 2
PARTS = 4
LONG = 1024 * 1024
HEAD = 8
STRIDE = 64


SMEM = pl.BlockSpec(memory_space=pltpu.SMEM)
VMEM = pl.BlockSpec(memory_space=pltpu.VMEM)
HBM = pl.BlockSpec(memory_space=pltpu.HBM)
MIB = 1024 * 1024
PREPARE = pltpu.CompilerParams(vmem_limit_bytes=64 * MIB)
PASS = pltpu.CompilerParams(vmem_limit_bytes=53 * MIB)


def shape(dims, dtype=jnp.float32):
    return jax.ShapeDtypeStruct(dims, dtype)


def start_copies(pairs, sems):
    copies = [pltpu.make_async_copy(src, dst, sems.at[k]) for k, (src, dst) in enumerate(pairs)]
    for copy in copies:
        copy.start()
    return copies


def close_list(ref, hbm, pairs, last, none, sems):
    right = HEAD + (ref.shape[0] - HEAD) // 3
    tails = (pairs + TAIL - 1) // TAIL
    ref[0] = tails // (PAIRS // TAIL)
    ref[1] = tails % (PAIRS // TAIL)

    def pad(k, carry):
        ref[HEAD + pairs + k] = last
        ref[right + 2 * (pairs + k)] = none
        ref[right + 2 * (pairs + k) + 1] = none
        return carry

    lax.fori_loop(0, tails * TAIL - pairs, pad, 0)
    copy = pltpu.make_async_copy(ref, hbm.at[pl.ds(0, ref.shape[0])], sems.at[0])
    copy.start()
    return copy


def columns_kernel(half_ref, *refs):
    remotes, hbm, (*tables, ref, sems) = refs[:4], refs[4], refs[5:]
    for copy in start_copies(list(zip(remotes, tables)), sems):
        copy.wait()
    halves = tables[0].shape[1] // 2
    first = half_ref[0] * halves
    right = HEAD + (ref.shape[0] - HEAD) // 3

    def one_block(b, position):
        at = right + 2 * position
        tiles = jnp.int32(0)
        for group, (slots_ref, counts_ref) in enumerate((tables[0:2], tables[2:4])):
            for k in range(KG):
                ref[at + tiles + k] = slots_ref[k, first + b] + group * GROUP
            tiles = tiles + counts_ref[0, first + b]
        ref[at + tiles] = 2 * GROUP
        for k in range(KG):
            ref[HEAD + position + k] = b
        return position + (tiles + 1) // 2

    pairs = lax.fori_loop(0, halves, one_block, jnp.int32(0))
    close_list(ref, hbm, pairs, halves - 1, 2 * GROUP, sems).wait()


def same_targets(ids, rows, same_ref):
    peers, per_peer = ids[0].shape
    lane = lax.broadcasted_iota(jnp.int32, (1, BLOCK), 1)
    known = jnp.zeros((1, BLOCK), jnp.int32)
    for d in range(peers):
        for p in range(peers):
            for c in range(per_peer):
                known = jnp.where(lane == (d * peers + p) * per_peer + c, ids[d][p, c], known)
    for p in range(peers):
        for c in range(per_peer):
            q = p * per_peer + c
            same = jnp.logical_and(known == ids[0][p, c], lane // per_peer % peers == p)
            for d in range(peers):
                own = jnp.logical_and(same, lane // GROUP == d)
                rows[pl.ds(d * GROUP + q, 1), :] = jnp.where(own, 1.0, 0.0)
    same_ref[...] = rows[...].astype(jnp.bfloat16)


def rows_kernel(half_ref, *refs):
    remotes, hbm, locals_ = refs[:4], refs[4], refs[5:]
    *tables, ref, lists, sizes, sems = locals_
    copies = start_copies(list(zip(remotes, tables)), sems)
    groups = (tables[0:2], tables[2:4])
    halves = tables[0].shape[1] // 2
    slots = 2 * GROUP
    first = half_ref[0] * halves
    right = HEAD + (ref.shape[0] - HEAD) // 3

    def clear(q, carry):
        sizes[q] = 0
        return carry

    lax.fori_loop(0, slots + 1, clear, 0, unroll=13)
    for copy in copies:
        copy.wait()

    def one_block(b, carry):
        def append(named):
            known = [sizes[slot] for slot in named]
            for slot, size in zip(named, known):
                lists[slot * STRIDE + size] = b
            for slot, size in zip(named, known):
                sizes[slot] = size + 1

        append([table[k, first + b] + group * GROUP for group, (table, _) in enumerate(groups) for k in range(2)])
        for group, (table, counts_ref) in enumerate(groups):
            count = counts_ref[0, first + b]

            def more(table=table, group=group, count=count):
                append(
                    [jnp.where(k < count, table[k, first + b] + group * GROUP, slots) for k in range(2, KG)]
                )

            pl.when(count > 2)(more)
        return carry

    lax.fori_loop(0, halves, one_block, 0)
    batch = 4

    def one_pair(q, position, k):
        ref[HEAD + position + k] = q
        for j in range(2):
            ref[right + 2 * (position + k) + j] = lists[q * STRIDE + 2 * k + j]

    def some_slots(t, position):
        counted = [sizes[t * batch + j] for j in range(batch)]
        for j, size in enumerate(counted):
            lists[(t * batch + j) * STRIDE + size] = halves
        counted = [(size + 1) // 2 for size in counted]
        places = [position]
        for pairs in counted:
            places.append(places[-1] + pairs)
        for j in range(batch):
            for k in range(3):
                one_pair(t * batch + j, places[j], k)

        def rest():
            for j in range(batch):

                def another(k, carry, j=j):
                    one_pair(t * batch + j, places[j], k)
                    return carry

                lax.fori_loop(3, counted[j], another, 0)

        pl.when(functools.reduce(jnp.maximum, counted) > 3)(rest)
        return places[-1]

    pairs = lax.fori_loop(0, slots // batch, some_slots, jnp.int32(0))
    close_list(ref, hbm, pairs, slots - 1, halves, sems).wait()


def list_shape(halves):
    room = HEAD + 3 * (halves * KG + 2 * GROUP + PAIRS + KG)
    return ((room + 1023) // 1024 * 1024,)


def make_list(kernel, half, remotes):
    own = [pltpu.SMEM(value.shape, value.dtype) for value in remotes]
    own.append(pltpu.SMEM(list_shape(remotes[0].shape[1] // 2), jnp.int32))
    if kernel is rows_kernel:
        own.append(pltpu.SMEM(((2 * GROUP + 1) * STRIDE,), jnp.int32))
        own.append(pltpu.SMEM((2 * GROUP + 1,), jnp.int32))
    return pl.pallas_call(
        kernel,
        out_shape=shape((LONG,), jnp.int32),
        in_specs=[SMEM] + [HBM] * len(remotes),
        out_specs=HBM,
        scratch_shapes=[*own, pltpu.SemaphoreType.DMA((len(remotes),))],
        compiler_params=PREPARE,
    )(half.reshape(1), *remotes)


def split3(values):
    high = values.astype(jnp.bfloat16)
    rest = values - high.astype(jnp.float32)
    middle = rest.astype(jnp.bfloat16)
    low = (rest - middle.astype(jnp.float32)).astype(jnp.bfloat16)
    return high, middle, low


def whole(parts):
    high, middle, low = [part.astype(jnp.float32) for part in parts]
    return high + middle + low


def log_sum(values):
    top = functools.reduce(jnp.maximum, values)
    return top + jnp.log2(sum(jnp.exp2(value - top) for value in values))


def pack_kernel(place_ref, *refs):
    count = (len(refs) - 3) // 2
    remotes, (out_ref, norm_ref, *locals_, sems) = refs[:count], refs[count:]
    *ids_refs, points, potential, logmass = locals_
    copies = start_copies(list(zip(remotes, locals_)), sems)
    place = place_ref[0]
    peers, per_peer = ids_refs[0].shape
    for copy in copies:
        copy.wait()

    def one_norm(t, carry):
        wide = points[:, pl.ds(pl.multiple_of(t * BLOCK, BLOCK), BLOCK)].astype(jnp.float32)
        norm_ref[pl.ds(t, 1), :] = 0.5 * jnp.sum(wide * wide, axis=0, keepdims=True)
        return carry

    lax.fori_loop(0, norm_ref.shape[0], one_norm, 0, unroll=8)
    for d, ids_ref in enumerate(ids_refs):
        other = lax.rem(place - d + peers, peers)
        rows = []
        for c in range(per_peer):
            t = ids_ref[place, c]
            block = points[:, pl.ds(pl.multiple_of(t * BLOCK, BLOCK), BLOCK)]
            start = SCALE * (potential[pl.ds(t, 1), :] - norm_ref[pl.ds(t, 1), :])
            mass = LOG2E * logmass[pl.ds(t, 1), :]
            rows += [part.astype(jnp.float32) for part in split3(start) + split3(mass)]
            out_ref[other, c * D : (c + 1) * D, :] = block
        out_ref[other, per_peer * D :, :] = jnp.concatenate(rows, axis=0).astype(jnp.bfloat16)


def pack(place, ids, *values):
    remotes = [*ids, *values]
    return pl.pallas_call(
        pack_kernel,
        out_shape=[shape((len(ids), CAP * (D + EXTRA), BLOCK), jnp.bfloat16), shape(values[1].shape)],
        in_specs=[SMEM] + [HBM] * len(remotes),
        out_specs=[VMEM, VMEM],
        scratch_shapes=[pltpu.SMEM(value.shape, value.dtype) for value in ids]
        + [pltpu.VMEM(value.shape, value.dtype) for value in values]
        + [pltpu.SemaphoreType.DMA((len(remotes),))],
        compiler_params=PREPARE,
    )(place.reshape(1), *remotes)


def merge_kernel(peers, place_ref, *refs):
    sums, ids, (logmass_ref, norm_ref, out_ref, parts) = refs[:peers], refs[peers : 2 * peers], refs[2 * peers :]
    place = place_ref[0]
    parts[...] = jnp.full_like(parts, LOWEST)
    for d in range(peers):
        for c in range(sums[d].shape[0]):
            parts[d, pl.ds(ids[d][place, c], 1), :] = sums[d][c : c + 1, :]
    merged = log_sum([parts[d] for d in range(peers)])
    out_ref[...] = (LOG2E * logmass_ref[...] - merged) * (1.0 / SCALE) + norm_ref[...]


def merge(place, sums, ids, logmass, norm):
    peers = len(ids)
    return pl.pallas_call(
        functools.partial(merge_kernel, peers),
        out_shape=shape(norm.shape),
        in_specs=[SMEM] + [VMEM] * peers + [SMEM] * peers + [VMEM] * 2,
        out_specs=VMEM,
        scratch_shapes=[pltpu.VMEM((peers, *norm.shape), jnp.float32)],
        compiler_params=PASS,
    )(place.reshape(1), *sums, *ids, logmass, norm)


def scaled_block(points, b):
    wide = points[:, pl.ds(pl.multiple_of(b * BLOCK, BLOCK), BLOCK)].astype(jnp.float32)
    scaled = SCALE * wide
    high = scaled.astype(jnp.bfloat16)
    low = (scaled - high.astype(jnp.float32)).astype(jnp.bfloat16)
    return wide, jnp.concatenate([high, low], axis=0)


def source_kernel(half_ref, points_hbm, logmass_hbm, *refs):
    count = (len(refs) - 8) // 2
    ids_hbm, (blocks_hbm, norm_ref, same_ref, points, logmass, blocks, rows, *ids, sems) = refs[:count], refs[count:]
    halves = blocks.shape[1] - 1
    own = pl.ds(pl.multiple_of(half_ref[0] * halves, halves), halves)
    at = pl.multiple_of(half_ref[0] * (halves * BLOCK), halves * BLOCK)
    pairs = [(points_hbm.at[:, pl.ds(at, halves * BLOCK)], points), (logmass_hbm.at[own], logmass)]
    for copy in start_copies(pairs + list(zip(ids_hbm, ids)), sems):
        copy.wait()
    parts = split3(LOG2E * logmass[...])
    blocks[LEFT, halves] = jnp.concatenate([*parts, jnp.zeros_like(parts[0])], axis=0)
    blocks[RIGHT, halves] = jnp.zeros((BLOCK, BLOCK), jnp.bfloat16)

    part = halves // PARTS

    def one_block(b, carry):
        wide, both = scaled_block(points, b)
        norm_ref[pl.ds(b, 1), :] = 0.5 * jnp.sum(wide * wide, axis=0, keepdims=True)
        blocks[RIGHT, b] = both
        blocks[LEFT, b] = both.T
        return carry

    copies = []
    for k in range(PARTS):
        lax.fori_loop(k * part, (k + 1) * part, one_block, 0, unroll=4)
        own = (slice(None), pl.ds(k * part, part + (k == PARTS - 1)))
        copies.append(pltpu.make_async_copy(blocks.at[own], blocks_hbm.at[own], sems.at[2 + count + k]))
        copies[-1].start()
    same_targets(ids, rows, same_ref)
    for copy in copies:
        copy.wait()


def source(half, halves, points, logmass, ids):
    blocks = (2, halves + 1, BLOCK, BLOCK)
    return pl.pallas_call(
        source_kernel,
        out_shape=[
            shape(blocks, jnp.bfloat16),
            shape((halves, BLOCK)),
            shape((BLOCK, BLOCK), jnp.bfloat16),
        ],
        in_specs=[SMEM] + [HBM] * (2 + len(ids)),
        out_specs=[HBM, VMEM, VMEM],
        scratch_shapes=[
            pltpu.VMEM((D, halves * BLOCK), jnp.bfloat16),
            pltpu.VMEM((halves, BLOCK), jnp.float32),
            pltpu.VMEM(blocks, jnp.bfloat16),
            pltpu.VMEM((BLOCK, BLOCK), jnp.float32),
        ]
        + [pltpu.SMEM(value.shape, value.dtype) for value in ids]
        + [pltpu.SemaphoreType.DMA((2 + len(ids) + PARTS,))],
        compiler_params=PASS,
    )(half.reshape(1), points, logmass, *ids)


def field_bias(mass_ref, parts_ref):
    rows = parts_ref.shape[1]
    mass = whole([mass_ref[k * rows : (k + 1) * rows, :] for k in range(3)])
    return mass - log_sum([parts_ref[k] for k in range(parts_ref.shape[0])])


def potential_bias(mass_ref, chosen_refs, *refs):
    dot = functools.partial(jnp.dot, preferred_element_type=jnp.float32)
    mass = whole([mass_ref[0, : 2 * GROUP, :], mass_ref[0, 2 * GROUP :, :], mass_ref[1, : 2 * GROUP, :]])
    out = []
    for group in range(2):
        own = slice(group * GROUP, (group + 1) * GROUP)
        chosen = chosen_refs[group][...]
        sums = jnp.concatenate([ref[own, :] for ref in refs], axis=0)
        parts = sum(dot(chosen, part) for part in split3(sums))
        known = dot(chosen, jnp.ones_like(chosen)) > 0.5
        parts = jnp.where(known, parts, LOWEST)
        merged = log_sum([parts[k * GROUP : (k + 1) * GROUP] for k in range(len(refs))])
        out.append(mass[own, :] - merged)
    return jnp.concatenate(out, axis=0)


def unpack(raw, left, start_ref, mass_ref, first, stop):
    def one_peer(peer, carry):
        rows = raw[peer, CAP * D :, :].astype(jnp.float32)
        for c in range(CAP):
            q = peer * CAP + c
            block = raw[peer, c * D : (c + 1) * D, :]
            left[q] = jnp.concatenate([block, block], axis=0).T
            high, middle, low, *mass = [rows[EXTRA * c + k : EXTRA * c + k + 1] for k in range(EXTRA)]
            start_ref[pl.ds(q, 1), :] = high + middle + low
            mass_ref[pl.ds(q, 1), :] = mass[0] + mass[1] + mass[2]
        return carry

    lax.fori_loop(first, stop, one_peer, 0)


def pass_kernel(kind, *refs):
    columns, peaks, masses, list_ref, left_ref, right_ref, sems = refs[-7:]
    lefts, rights = columns.shape[0], peaks.shape[1] - 1
    peers = GROUP // CAP
    part = lefts // PARTS
    left_parts = []
    if kind == FIRST:
        list_hbm, near_hbm, far_hbm, points_hbm, half_ref = refs[:5]
        out_ref, left_hbm, mass_ref, bias_ref, raw, points = refs[5:-7]
        own = rights * BLOCK
        at = pl.multiple_of(half_ref[0] * own, own)
        early = [(near_hbm, raw.at[pl.ds(0, peers)]), (far_hbm, raw.at[pl.ds(peers, peers)])]
        early.insert(0, (points_hbm.at[:, pl.ds(at, own)], points))
        late = []
    elif kind == ROWS:
        list_hbm, left_hbm, points_hbm = refs[:3]
        *col_parts, near_same, far_same, out_ref, bias_ref, mass = refs[3:-7]
        early = [(left_hbm.at[pl.ds(lefts, 2)], mass)]
        late = [(points_hbm.at[RIGHT, pl.ds(0, rights)], right_ref)]
        left_parts = [left_hbm.at[pl.ds(k * part, part)] for k in range(PARTS)]
    else:
        list_hbm, near_hbm, far_hbm, points_hbm, rows_ref, out_ref, bias_ref, mass = refs[:-7]
        early = [(points_hbm.at[LEFT, lefts], mass)]
        late = [
            (raw_hbm.at[:, pl.ds(0, CAP * D)], right_ref.at[pl.ds(group * peers, peers)])
            for group, raw_hbm in enumerate((near_hbm, far_hbm))
        ]
        left_parts = [points_hbm.at[LEFT, pl.ds(k * part, part)] for k in range(PARTS)]
    late.append((list_hbm.at[pl.ds(0, list_ref.shape[0])], list_ref))
    pairs = early + late + [(ref, left_ref.at[pl.ds(k * part, part)]) for k, ref in enumerate(left_parts)]
    copies = start_copies(pairs, sems)
    peaks[...] = jnp.full_like(peaks, LOWEST)
    masses[...] = jnp.zeros_like(masses)
    if kind == FIRST:
        copies[0].wait()

        def scale(b, carry):
            right_ref[b] = scaled_block(points, b)[1]
            return carry

        lax.fori_loop(0, rights, scale, 0, unroll=8)
        for group in range(2):
            copies[1 + group].wait()
            unpack(raw, left_ref, bias_ref, mass_ref, group * peers, (group + 1) * peers)
        high, middle, low = split3(mass_ref[...])
        left_ref[lefts] = jnp.concatenate([high, middle], axis=0)
        left_ref[lefts + 1] = jnp.concatenate([low, jnp.zeros_like(low)], axis=0)
        hand_on = pltpu.make_async_copy(left_ref, left_hbm, sems.at[len(pairs)])
        hand_on.start()
    else:
        for copy in copies[: len(early)]:
            copy.wait()
    if kind == ROWS:
        bias_ref[...] = potential_bias(mass, (near_same, far_same), *col_parts)
    elif kind == COLUMNS:
        bias_ref[...] = field_bias(mass, rows_ref)
    square = (BLOCK, BLOCK)
    lane = lax.broadcasted_iota(jnp.int32, square, 1)
    eye = jnp.where(lane == lax.broadcasted_iota(jnp.int32, square, 0), 1.0, 0.0).astype(jnp.bfloat16)
    lane = jnp.where(lane < 3 * GROUP, lane % GROUP, -1)
    for group in range(lefts // GROUP):
        high, middle, low = split3(bias_ref[group * GROUP : (group + 1) * GROUP, :])
        parts = jnp.concatenate([high, middle, low, jnp.zeros_like(high)], axis=0)
        turned = lax.dot_general(
            eye, parts, (((1,), (1,)), ((), ())), preferred_element_type=jnp.float32
        )

        def fill(k, carry, group=group, turned=turned):
            columns[group * GROUP + k] = jnp.where(lane == k, turned, 0.0).astype(jnp.bfloat16)
            return carry

        lax.fori_loop(0, GROUP, fill, 0, unroll=4)
    for copy in copies[len(early) : len(early) + len(late)]:
        copy.wait()
    rights_at = HEAD + (list_ref.shape[0] - HEAD) // 3
    ones = jnp.ones((BLOCK, 2 * BLOCK), jnp.bfloat16)

    def fold(copy, r, scores):
        scores = scores.reshape(BLOCK // 8, 8, BLOCK)
        old = peaks[copy, r]
        top = jnp.maximum(old, jnp.max(scores, axis=0))
        mass = jnp.sum(jnp.exp2(scores - top[None]), axis=0)
        masses[copy, r] = masses[copy, r] * jnp.exp2(old - top) + mass
        peaks[copy, r] = top

    def right_block(r):
        r = jnp.minimum(r, rights - 1)
        if kind != COLUMNS:
            return right_ref[r]
        block = right_ref[r // CAP, pl.ds(pl.multiple_of(r % CAP * D, D), D), :]
        return jnp.concatenate([block, block], axis=0)

    def wait_for(known, needed):
        if not left_parts:
            return known

        def wait(k, carry):
            at = pl.ds(k * part, part)
            source = left_hbm.at[at] if kind == ROWS else points_hbm.at[LEFT, at]
            pltpu.make_async_copy(source, left_ref.at[at], sems.at[len(early) + len(late) + k]).wait()
            return carry

        lax.fori_loop(known, needed, wait, 0)
        return jnp.maximum(known, needed)

    def step(start, count, t, known):
        known = wait_for(known, list_ref[HEAD + start + t * count + count - 1] // part + 1)
        for u in range(count):
            i = start + t * count + u
            l = list_ref[HEAD + i]
            first, second = list_ref[rights_at + 2 * i], list_ref[rights_at + 2 * i + 1]
            left = jnp.concatenate([left_ref[l], columns[l]], axis=1)
            right = jnp.concatenate([right_block(first), right_block(second)], axis=1)
            scores = jnp.dot(
                left, jnp.concatenate([right, ones], axis=0), preferred_element_type=jnp.float32
            )
            fold((2 * u) % COPIES, first, scores[:, :BLOCK])
            fold((2 * u + 1) % COPIES, second, scores[:, BLOCK:])
        return known

    known = lax.fori_loop(0, list_ref[0], functools.partial(step, 0, PAIRS), jnp.int32(0))
    known = lax.fori_loop(0, list_ref[1], functools.partial(step, list_ref[0] * PAIRS, TAIL), known)
    wait_for(known, PARTS)

    def finish(octet, carry):
        rows = []
        for k in range(8):
            r = octet * 8 + k
            tops = [peaks[copy, r] for copy in range(COPIES)]
            top = jnp.max(functools.reduce(jnp.maximum, tops), axis=0, keepdims=True)
            mass = sum(masses[copy, r] * jnp.exp2(tops[copy] - top) for copy in range(COPIES))
            rows.append(top + jnp.log2(jnp.sum(mass, axis=0, keepdims=True)))
        out_ref[0, pl.ds(pl.multiple_of(octet * 8, 8), 8), :] = jnp.concatenate(rows, axis=0)
        return carry

    lax.fori_loop(0, rights // 8, finish, 0)
    for k in range(1, out_ref.shape[0]):
        out_ref[k] = out_ref[0]
    if kind == FIRST:
        hand_on.wait()


def log_sums(kind, pairs, halves, remotes, parts, copies, keep=False):
    slots = 2 * GROUP
    lefts, rights = (halves, slots) if kind == COLUMNS else (slots, halves)
    form = (2 * GROUP // CAP, CAP * D, BLOCK) if kind == COLUMNS else (rights, BLOCK, BLOCK)
    held = lefts
    outs, bias = [shape((copies, rights, BLOCK))], pltpu.VMEM((lefts, BLOCK), jnp.float32)
    if kind == FIRST:
        held = lefts + 2
        outs.append(shape((held, BLOCK, BLOCK), jnp.bfloat16))
        scratch = [bias, bias, pltpu.VMEM((2 * GROUP // CAP, CAP * (D + EXTRA), BLOCK), jnp.bfloat16)]
        scratch.append(pltpu.VMEM((D, halves * BLOCK), jnp.bfloat16))
    elif kind == ROWS:
        scratch = [bias, pltpu.VMEM((2, BLOCK, BLOCK), jnp.bfloat16)]
    else:
        scratch = [pltpu.VMEM((BLOCK, BLOCK), jnp.bfloat16)]
        if keep:
            outs.append(shape((lefts, BLOCK)))
        else:
            scratch.insert(0, bias)
    return pl.pallas_call(
        functools.partial(pass_kernel, kind),
        out_shape=outs,
        in_specs=[HBM] * (1 + len(remotes)) + [SMEM if kind == FIRST else VMEM] * len(parts),
        out_specs=[VMEM, HBM] if kind == FIRST else [VMEM] * len(outs),
        scratch_shapes=scratch
        + [
            pltpu.VMEM((lefts, BLOCK, BLOCK), jnp.bfloat16),
            pltpu.VMEM((COPIES, rights + 1, 8, BLOCK), jnp.float32),
            pltpu.VMEM((COPIES, rights + 1, 8, BLOCK), jnp.float32),
            pltpu.SMEM(list_shape(halves), jnp.int32),
            pltpu.VMEM((held, BLOCK, BLOCK), jnp.bfloat16),
            pltpu.VMEM(form, jnp.bfloat16),
            pltpu.SemaphoreType.DMA((5 + PARTS,)),
        ],
        compiler_params=PREPARE if kind == FIRST else PASS,
    )(pairs, *remotes, *parts)


def ring(values, axis, size, stride=1):
    places = lax.axis_size(axis)
    out = [values]
    for d in range(1, size):
        pairs = []
        for i in range(places):
            place = i // stride % size
            pairs.append((i, i + ((place + d) % size - place) * stride))
        out.append(lax.ppermute(values, axis, pairs))
    return out


def shards(
    source_points,
    source_logmass,
    target_points,
    target_logmass,
    target_potential,
    tile_slot,
    tile_counts,
    fetch_ids,
):
    peers = lax.axis_size("src")
    blocks = tile_counts.shape[0]
    halves = blocks // 2
    per_peer = fetch_ids.shape[1]
    owned = target_potential.shape[0] // BLOCK
    count = peers * per_peer
    place = lax.axis_index("src")
    half = lax.axis_index("grp") % 2

    def swap(values):
        return ring(values, "grp", 2, 1)[1]

    tiles = [tile_slot.T, tile_counts.T]
    ids = ring(fetch_ids, "src", peers)
    ids, tiles = lax.optimization_barrier((ids, tiles + [swap(part) for part in tiles]))
    packed, target_half = pack(
        place,
        ids,
        target_points.T,
        target_potential.reshape(owned, BLOCK),
        target_logmass.reshape(owned, BLOCK),
    )
    row_pairs = make_list(rows_kernel, half, tiles)
    fetched = lax.all_to_all(packed, "src", split_axis=0, concat_axis=0, tiled=True)
    fetched, row_pairs, ids, tiles = lax.optimization_barrier((fetched, row_pairs, ids, tiles))
    col_pairs = make_list(columns_kernel, half, tiles)
    *both, col_pairs = lax.optimization_barrier((fetched, swap(fetched), col_pairs))

    groups = lax.axis_size("grp")
    same_core = [list(range(core, groups, 2)) for core in range(2)]
    for sweep_index in range(ITERS):
        if sweep_index == 0:
            turned = source_points.T
            rows, targets = log_sums(FIRST, row_pairs, halves, [*both, turned], [half.reshape(1)], groups // 2)
            rows, turned, logmass, ids = lax.optimization_barrier((rows, turned, source_logmass, ids))
            points, source_half, same = source(half, halves, turned, logmass.reshape(blocks, BLOCK), ids)
            same = [same, swap(same)]
        else:
            (rows,) = log_sums(ROWS, row_pairs, halves, [targets, points], col_parts + same, groups // 2)
        rows = lax.all_to_all(
            rows, "grp", split_axis=0, concat_axis=0, tiled=True, axis_index_groups=same_core
        )
        last = sweep_index == ITERS - 1
        cols, *fields = log_sums(COLUMNS, col_pairs, halves, [*both, points], [rows], 1, keep=last)
        cols = cols[0]
        if sweep_index < ITERS - 1:
            other = swap(cols)
            cols = log_sum([cols, jnp.concatenate([other[count:], other[:count]], axis=0)])
            col_parts = ring(cols, "src", peers)
    field, half = lax.optimization_barrier((fields[0], half))
    field = field * (1.0 / SCALE) + source_half
    low = half == 0
    other = swap(field)
    source_field = jnp.concatenate([jnp.where(low, field, other), jnp.where(low, other, field)], axis=0)

    cols = log_sum([cols[:count], swap(cols[count:])]).reshape(peers, per_peer, BLOCK)
    cols, last_place, ids, target_half, target_logmass = lax.optimization_barrier(
        (cols, place, ids, target_half, target_logmass)
    )
    back = []
    for d in range(peers):
        wanted = lax.dynamic_slice(cols, ((last_place + d) % peers, 0, 0), (1, per_peer, BLOCK))[0]
        pairs = [(i, (i + d) % peers) for i in range(peers)]
        back.append(wanted if d == 0 else lax.ppermute(wanted, "src", pairs))
    target_field = merge(last_place, back, ids, target_logmass.reshape(owned, BLOCK), target_half).reshape(-1)
    return (source_field.reshape(-1), target_field)


def solution(mesh):
    return jax.shard_map(
        shards,
        mesh=mesh,
        in_specs=(
            P("src", None),
            P("src"),
            P(("src", "grp"), None),
            P(("src", "grp")),
            P(("src", "grp")),
            P("src", "grp"),
            P("src", "grp"),
            P("src", "grp"),
        ),
        out_specs=(P("src"), P(("src", "grp"))),
        check_vma=False,
    )
```

```python
import functools

import jax
import jax.numpy as jnp
from jax import lax
from jax.experimental import pallas as pl
from jax.experimental.pallas import tpu as pltpu
from jax.sharding import PartitionSpec as P

D = 64
BLOCK = 128
KG = 8
ITERS = 3
EPSILON = 0.25
LOWEST = -1e30
LOG2E = 1.4426950408889634
SCALE = LOG2E / EPSILON
PAIRS = 64
TAIL = 16
COPIES = 2
GROUP = 32
CAP = 8
EXTRA = 6
LEFT, RIGHT = 0, 1
FIRST, ROWS, COLUMNS = 0, 1, 2
PARTS = 4
LONG = 1024 * 1024
HEAD = 8
STRIDE = 64


SMEM = pl.BlockSpec(memory_space=pltpu.SMEM)
VMEM = pl.BlockSpec(memory_space=pltpu.VMEM)
HBM = pl.BlockSpec(memory_space=pltpu.HBM)
MIB = 1024 * 1024
PREPARE = pltpu.CompilerParams(vmem_limit_bytes=64 * MIB)
PASS = pltpu.CompilerParams(vmem_limit_bytes=53 * MIB)


def shape(dims, dtype=jnp.float32):
    return jax.ShapeDtypeStruct(dims, dtype)


def start_copies(pairs, sems):
    copies = [pltpu.make_async_copy(src, dst, sems.at[k]) for k, (src, dst) in enumerate(pairs)]
    for copy in copies:
        copy.start()
    return copies


def close_list(ref, hbm, pairs, last, none, sems):
    right = HEAD + (ref.shape[0] - HEAD) // 3
    tails = (pairs + TAIL - 1) // TAIL
    ref[0] = tails // (PAIRS // TAIL)
    ref[1] = tails % (PAIRS // TAIL)

    def pad(k, carry):
        ref[HEAD + pairs + k] = last
        ref[right + 2 * (pairs + k)] = none
        ref[right + 2 * (pairs + k) + 1] = none
        return carry

    lax.fori_loop(0, tails * TAIL - pairs, pad, 0)
    copy = pltpu.make_async_copy(ref, hbm.at[pl.ds(0, ref.shape[0])], sems.at[0])
    copy.start()
    return copy


def columns_kernel(half_ref, *refs):
    remotes, hbm, (*tables, ref, sems) = refs[:4], refs[4], refs[5:]
    for copy in start_copies(list(zip(remotes, tables)), sems):
        copy.wait()
    halves = tables[0].shape[1] // 2
    first = half_ref[0] * halves
    right = HEAD + (ref.shape[0] - HEAD) // 3

    def one_block(b, position):
        at = right + 2 * position
        tiles = jnp.int32(0)
        for group, (slots_ref, counts_ref) in enumerate((tables[0:2], tables[2:4])):
            for k in range(KG):
                ref[at + tiles + k] = slots_ref[k, first + b] + group * GROUP
            tiles = tiles + counts_ref[0, first + b]
        ref[at + tiles] = 2 * GROUP
        for k in range(KG):
            ref[HEAD + position + k] = b
        return position + (tiles + 1) // 2

    pairs = lax.fori_loop(0, halves, one_block, jnp.int32(0))
    close_list(ref, hbm, pairs, halves - 1, 2 * GROUP, sems).wait()


def same_targets(ids, rows, same_ref):
    peers, per_peer = ids[0].shape
    lane = lax.broadcasted_iota(jnp.int32, (1, BLOCK), 1)
    known = jnp.zeros((1, BLOCK), jnp.int32)
    for d in range(peers):
        for p in range(peers):
            for c in range(per_peer):
                known = jnp.where(lane == (d * peers + p) * per_peer + c, ids[d][p, c], known)
    for p in range(peers):
        for c in range(per_peer):
            q = p * per_peer + c
            same = jnp.logical_and(known == ids[0][p, c], lane // per_peer % peers == p)
            for d in range(peers):
                own = jnp.logical_and(same, lane // GROUP == d)
                rows[pl.ds(d * GROUP + q, 1), :] = jnp.where(own, 1.0, 0.0)
    same_ref[...] = rows[...].astype(jnp.bfloat16)


def rows_kernel(half_ref, *refs):
    remotes, hbm, locals_ = refs[:4], refs[4], refs[5:]
    *tables, ref, lists, sizes, sems = locals_
    copies = start_copies(list(zip(remotes, tables)), sems)
    groups = (tables[0:2], tables[2:4])
    halves = tables[0].shape[1] // 2
    slots = 2 * GROUP
    first = half_ref[0] * halves
    right = HEAD + (ref.shape[0] - HEAD) // 3

    def clear(q, carry):
        sizes[q] = 0
        return carry

    lax.fori_loop(0, slots + 1, clear, 0, unroll=13)
    for copy in copies:
        copy.wait()

    def one_block(b, carry):
        def append(named):
            known = [sizes[slot] for slot in named]
            for slot, size in zip(named, known):
                lists[slot * STRIDE + size] = b
            for slot, size in zip(named, known):
                sizes[slot] = size + 1

        append([table[k, first + b] + group * GROUP for group, (table, _) in enumerate(groups) for k in range(2)])
        for group, (table, counts_ref) in enumerate(groups):
            count = counts_ref[0, first + b]

            def more(table=table, group=group, count=count):
                append(
                    [jnp.where(k < count, table[k, first + b] + group * GROUP, slots) for k in range(2, KG)]
                )

            pl.when(count > 2)(more)
        return carry

    lax.fori_loop(0, halves, one_block, 0)
    batch = 4

    def one_pair(q, position, k):
        ref[HEAD + position + k] = q
        for j in range(2):
            ref[right + 2 * (position + k) + j] = lists[q * STRIDE + 2 * k + j]

    def some_slots(t, position):
        counted = [sizes[t * batch + j] for j in range(batch)]
        for j, size in enumerate(counted):
            lists[(t * batch + j) * STRIDE + size] = halves
        counted = [(size + 1) // 2 for size in counted]
        places = [position]
        for pairs in counted:
            places.append(places[-1] + pairs)
        for j in range(batch):
            for k in range(3):
                one_pair(t * batch + j, places[j], k)

        def rest():
            for j in range(batch):

                def another(k, carry, j=j):
                    one_pair(t * batch + j, places[j], k)
                    return carry

                lax.fori_loop(3, counted[j], another, 0)

        pl.when(functools.reduce(jnp.maximum, counted) > 3)(rest)
        return places[-1]

    pairs = lax.fori_loop(0, slots // batch, some_slots, jnp.int32(0))
    close_list(ref, hbm, pairs, slots - 1, halves, sems).wait()


def list_shape(halves):
    room = HEAD + 3 * (halves * KG + 2 * GROUP + PAIRS + KG)
    return ((room + 1023) // 1024 * 1024,)


def make_list(kernel, half, remotes):
    own = [pltpu.SMEM(value.shape, value.dtype) for value in remotes]
    own.append(pltpu.SMEM(list_shape(remotes[0].shape[1] // 2), jnp.int32))
    if kernel is rows_kernel:
        own.append(pltpu.SMEM(((2 * GROUP + 1) * STRIDE,), jnp.int32))
        own.append(pltpu.SMEM((2 * GROUP + 1,), jnp.int32))
    return pl.pallas_call(
        kernel,
        out_shape=shape((LONG,), jnp.int32),
        in_specs=[SMEM] + [HBM] * len(remotes),
        out_specs=HBM,
        scratch_shapes=[*own, pltpu.SemaphoreType.DMA((len(remotes),))],
        compiler_params=PREPARE,
    )(half.reshape(1), *remotes)


def split3(values):
    high = values.astype(jnp.bfloat16)
    rest = values - high.astype(jnp.float32)
    middle = rest.astype(jnp.bfloat16)
    low = (rest - middle.astype(jnp.float32)).astype(jnp.bfloat16)
    return high, middle, low


def whole(parts):
    high, middle, low = [part.astype(jnp.float32) for part in parts]
    return high + middle + low


def log_sum(values):
    top = functools.reduce(jnp.maximum, values)
    return top + jnp.log2(sum(jnp.exp2(value - top) for value in values))


def pack_kernel(place_ref, *refs):
    count = (len(refs) - 3) // 2
    remotes, (out_ref, norm_ref, *locals_, sems) = refs[:count], refs[count:]
    *ids_refs, points, potential, logmass = locals_
    copies = start_copies(list(zip(remotes, locals_)), sems)
    place = place_ref[0]
    peers, per_peer = ids_refs[0].shape
    for copy in copies:
        copy.wait()

    def one_norm(t, carry):
        wide = points[:, pl.ds(pl.multiple_of(t * BLOCK, BLOCK), BLOCK)].astype(jnp.float32)
        norm_ref[pl.ds(t, 1), :] = 0.5 * jnp.sum(wide * wide, axis=0, keepdims=True)
        return carry

    lax.fori_loop(0, norm_ref.shape[0], one_norm, 0, unroll=8)
    for d, ids_ref in enumerate(ids_refs):
        other = lax.rem(place - d + peers, peers)
        rows = []
        for c in range(per_peer):
            t = ids_ref[place, c]
            block = points[:, pl.ds(pl.multiple_of(t * BLOCK, BLOCK), BLOCK)]
            start = SCALE * (potential[pl.ds(t, 1), :] - norm_ref[pl.ds(t, 1), :])
            mass = LOG2E * logmass[pl.ds(t, 1), :]
            rows += [part.astype(jnp.float32) for part in split3(start) + split3(mass)]
            out_ref[other, c * D : (c + 1) * D, :] = block
        out_ref[other, per_peer * D :, :] = jnp.concatenate(rows, axis=0).astype(jnp.bfloat16)


def pack(place, ids, *values):
    remotes = [*ids, *values]
    return pl.pallas_call(
        pack_kernel,
        out_shape=[shape((len(ids), CAP * (D + EXTRA), BLOCK), jnp.bfloat16), shape(values[1].shape)],
        in_specs=[SMEM] + [HBM] * len(remotes),
        out_specs=[VMEM, VMEM],
        scratch_shapes=[pltpu.SMEM(value.shape, value.dtype) for value in ids]
        + [pltpu.VMEM(value.shape, value.dtype) for value in values]
        + [pltpu.SemaphoreType.DMA((len(remotes),))],
        compiler_params=PREPARE,
    )(place.reshape(1), *remotes)


def merge_kernel(peers, place_ref, *refs):
    sums, ids, (logmass_ref, norm_ref, out_ref, parts) = refs[:peers], refs[peers : 2 * peers], refs[2 * peers :]
    place = place_ref[0]
    parts[...] = jnp.full_like(parts, LOWEST)
    for d in range(peers):
        for c in range(sums[d].shape[0]):
            parts[d, pl.ds(ids[d][place, c], 1), :] = sums[d][c : c + 1, :]
    merged = log_sum([parts[d] for d in range(peers)])
    out_ref[...] = (LOG2E * logmass_ref[...] - merged) * (1.0 / SCALE) + norm_ref[...]


def merge(place, sums, ids, logmass, norm):
    peers = len(ids)
    return pl.pallas_call(
        functools.partial(merge_kernel, peers),
        out_shape=shape(norm.shape),
        in_specs=[SMEM] + [VMEM] * peers + [SMEM] * peers + [VMEM] * 2,
        out_specs=VMEM,
        scratch_shapes=[pltpu.VMEM((peers, *norm.shape), jnp.float32)],
        compiler_params=PASS,
    )(place.reshape(1), *sums, *ids, logmass, norm)


def scaled_block(points, b):
    wide = points[:, pl.ds(pl.multiple_of(b * BLOCK, BLOCK), BLOCK)].astype(jnp.float32)
    scaled = SCALE * wide
    high = scaled.astype(jnp.bfloat16)
    low = (scaled - high.astype(jnp.float32)).astype(jnp.bfloat16)
    return wide, jnp.concatenate([high, low], axis=0)


def source_kernel(half_ref, points_hbm, logmass_hbm, *refs):
    count = (len(refs) - 8) // 2
    ids_hbm, (blocks_hbm, norm_ref, same_ref, points, logmass, blocks, rows, *ids, sems) = refs[:count], refs[count:]
    halves = blocks.shape[1] - 1
    own = pl.ds(pl.multiple_of(half_ref[0] * halves, halves), halves)
    at = pl.multiple_of(half_ref[0] * (halves * BLOCK), halves * BLOCK)
    pairs = [(points_hbm.at[:, pl.ds(at, halves * BLOCK)], points), (logmass_hbm.at[own], logmass)]
    for copy in start_copies(pairs + list(zip(ids_hbm, ids)), sems):
        copy.wait()
    parts = split3(LOG2E * logmass[...])
    blocks[LEFT, halves] = jnp.concatenate([*parts, jnp.zeros_like(parts[0])], axis=0)
    blocks[RIGHT, halves] = jnp.zeros((BLOCK, BLOCK), jnp.bfloat16)

    part = halves // PARTS

    def one_block(b, carry):
        wide, both = scaled_block(points, b)
        norm_ref[pl.ds(b, 1), :] = 0.5 * jnp.sum(wide * wide, axis=0, keepdims=True)
        blocks[RIGHT, b] = both
        blocks[LEFT, b] = both.T
        return carry

    copies = []
    for k in range(PARTS):
        lax.fori_loop(k * part, (k + 1) * part, one_block, 0, unroll=4)
        own = (slice(None), pl.ds(k * part, part + (k == PARTS - 1)))
        copies.append(pltpu.make_async_copy(blocks.at[own], blocks_hbm.at[own], sems.at[2 + count + k]))
        copies[-1].start()
    same_targets(ids, rows, same_ref)
    for copy in copies:
        copy.wait()


def source(half, halves, points, logmass, ids):
    blocks = (2, halves + 1, BLOCK, BLOCK)
    return pl.pallas_call(
        source_kernel,
        out_shape=[
            shape(blocks, jnp.bfloat16),
            shape((halves, BLOCK)),
            shape((BLOCK, BLOCK), jnp.bfloat16),
        ],
        in_specs=[SMEM] + [HBM] * (2 + len(ids)),
        out_specs=[HBM, VMEM, VMEM],
        scratch_shapes=[
            pltpu.VMEM((D, halves * BLOCK), jnp.bfloat16),
            pltpu.VMEM((halves, BLOCK), jnp.float32),
            pltpu.VMEM(blocks, jnp.bfloat16),
            pltpu.VMEM((BLOCK, BLOCK), jnp.float32),
        ]
        + [pltpu.SMEM(value.shape, value.dtype) for value in ids]
        + [pltpu.SemaphoreType.DMA((2 + len(ids) + PARTS,))],
        compiler_params=PASS,
    )(half.reshape(1), points, logmass, *ids)


def field_bias(mass_ref, parts_ref):
    rows = parts_ref.shape[1]
    mass = whole([mass_ref[k * rows : (k + 1) * rows, :] for k in range(3)])
    return mass - log_sum([parts_ref[k] for k in range(parts_ref.shape[0])])


def potential_bias(mass_ref, chosen_refs, *refs):
    dot = functools.partial(jnp.dot, preferred_element_type=jnp.float32)
    mass = whole([mass_ref[0, : 2 * GROUP, :], mass_ref[0, 2 * GROUP :, :], mass_ref[1, : 2 * GROUP, :]])
    out = []
    for group in range(2):
        own = slice(group * GROUP, (group + 1) * GROUP)
        chosen = chosen_refs[group][...]
        sums = jnp.concatenate([ref[own, :] for ref in refs], axis=0)
        parts = sum(dot(chosen, part) for part in split3(sums))
        known = dot(chosen, jnp.ones_like(chosen)) > 0.5
        parts = jnp.where(known, parts, LOWEST)
        merged = log_sum([parts[k * GROUP : (k + 1) * GROUP] for k in range(len(refs))])
        out.append(mass[own, :] - merged)
    return jnp.concatenate(out, axis=0)


def unpack(raw, left, start_ref, mass_ref, first, stop):
    def one_peer(peer, carry):
        rows = raw[peer, CAP * D :, :].astype(jnp.float32)
        for c in range(CAP):
            q = peer * CAP + c
            block = raw[peer, c * D : (c + 1) * D, :]
            left[q] = jnp.concatenate([block, block], axis=0).T
            high, middle, low, *mass = [rows[EXTRA * c + k : EXTRA * c + k + 1] for k in range(EXTRA)]
            start_ref[pl.ds(q, 1), :] = high + middle + low
            mass_ref[pl.ds(q, 1), :] = mass[0] + mass[1] + mass[2]
        return carry

    lax.fori_loop(first, stop, one_peer, 0)


def pass_kernel(kind, *refs):
    columns, peaks, masses, list_ref, left_ref, right_ref, sems = refs[-7:]
    lefts, rights = columns.shape[0], peaks.shape[1] - 1
    peers = GROUP // CAP
    part = lefts // PARTS
    left_parts = []
    if kind == FIRST:
        list_hbm, near_hbm, far_hbm, points_hbm, half_ref = refs[:5]
        out_ref, left_hbm, mass_ref, bias_ref, raw, points = refs[5:-7]
        own = rights * BLOCK
        at = pl.multiple_of(half_ref[0] * own, own)
        early = [(near_hbm, raw.at[pl.ds(0, peers)]), (far_hbm, raw.at[pl.ds(peers, peers)])]
        early.insert(0, (points_hbm.at[:, pl.ds(at, own)], points))
        late = []
    elif kind == ROWS:
        list_hbm, left_hbm, points_hbm = refs[:3]
        *col_parts, near_same, far_same, out_ref, bias_ref, mass = refs[3:-7]
        early = [(left_hbm.at[pl.ds(lefts, 2)], mass)]
        late = [(points_hbm.at[RIGHT, pl.ds(0, rights)], right_ref)]
        left_parts = [left_hbm.at[pl.ds(k * part, part)] for k in range(PARTS)]
    else:
        list_hbm, near_hbm, far_hbm, points_hbm, rows_ref, out_ref, bias_ref, mass = refs[:-7]
        early = [(points_hbm.at[LEFT, lefts], mass)]
        late = [
            (raw_hbm.at[:, pl.ds(0, CAP * D)], right_ref.at[pl.ds(group * peers, peers)])
            for group, raw_hbm in enumerate((near_hbm, far_hbm))
        ]
        left_parts = [points_hbm.at[LEFT, pl.ds(k * part, part)] for k in range(PARTS)]
    late.append((list_hbm.at[pl.ds(0, list_ref.shape[0])], list_ref))
    pairs = early + late + [(ref, left_ref.at[pl.ds(k * part, part)]) for k, ref in enumerate(left_parts)]
    copies = start_copies(pairs, sems)
    peaks[...] = jnp.full_like(peaks, LOWEST)
    masses[...] = jnp.zeros_like(masses)
    if kind == FIRST:
        copies[0].wait()

        def scale(b, carry):
            right_ref[b] = scaled_block(points, b)[1]
            return carry

        lax.fori_loop(0, rights, scale, 0, unroll=8)
        for group in range(2):
            copies[1 + group].wait()
            unpack(raw, left_ref, bias_ref, mass_ref, group * peers, (group + 1) * peers)
        high, middle, low = split3(mass_ref[...])
        left_ref[lefts] = jnp.concatenate([high, middle], axis=0)
        left_ref[lefts + 1] = jnp.concatenate([low, jnp.zeros_like(low)], axis=0)
        hand_on = pltpu.make_async_copy(left_ref, left_hbm, sems.at[len(pairs)])
        hand_on.start()
    else:
        for copy in copies[: len(early)]:
            copy.wait()
    if kind == ROWS:
        bias_ref[...] = potential_bias(mass, (near_same, far_same), *col_parts)
    elif kind == COLUMNS:
        bias_ref[...] = field_bias(mass, rows_ref)
    square = (BLOCK, BLOCK)
    lane = lax.broadcasted_iota(jnp.int32, square, 1)
    eye = jnp.where(lane == lax.broadcasted_iota(jnp.int32, square, 0), 1.0, 0.0).astype(jnp.bfloat16)
    lane = jnp.where(lane < 3 * GROUP, lane % GROUP, -1)
    for group in range(lefts // GROUP):
        high, middle, low = split3(bias_ref[group * GROUP : (group + 1) * GROUP, :])
        parts = jnp.concatenate([high, middle, low, jnp.zeros_like(high)], axis=0)
        turned = lax.dot_general(
            eye, parts, (((1,), (1,)), ((), ())), preferred_element_type=jnp.float32
        )

        def fill(k, carry, group=group, turned=turned):
            columns[group * GROUP + k] = jnp.where(lane == k, turned, 0.0).astype(jnp.bfloat16)
            return carry

        lax.fori_loop(0, GROUP, fill, 0, unroll=8)
    for copy in copies[len(early) : len(early) + len(late)]:
        copy.wait()
    rights_at = HEAD + (list_ref.shape[0] - HEAD) // 3
    ones = jnp.ones((BLOCK, 2 * BLOCK), jnp.bfloat16)

    def fold(copy, r, scores):
        scores = scores.reshape(BLOCK // 8, 8, BLOCK)
        old = peaks[copy, r]
        top = jnp.maximum(old, jnp.max(scores, axis=0))
        mass = jnp.sum(jnp.exp2(scores - top[None]), axis=0)
        masses[copy, r] = masses[copy, r] * jnp.exp2(old - top) + mass
        peaks[copy, r] = top

    def right_block(r):
        r = jnp.minimum(r, rights - 1)
        if kind != COLUMNS:
            return right_ref[r]
        block = right_ref[r // CAP, pl.ds(pl.multiple_of(r % CAP * D, D), D), :]
        return jnp.concatenate([block, block], axis=0)

    def wait_for(known, needed):
        if not left_parts:
            return known

        def wait(k, carry):
            at = pl.ds(k * part, part)
            source = left_hbm.at[at] if kind == ROWS else points_hbm.at[LEFT, at]
            pltpu.make_async_copy(source, left_ref.at[at], sems.at[len(early) + len(late) + k]).wait()
            return carry

        lax.fori_loop(known, needed, wait, 0)
        return jnp.maximum(known, needed)

    def step(start, count, t, known):
        known = wait_for(known, list_ref[HEAD + start + t * count + count - 1] // part + 1)
        for u in range(count):
            i = start + t * count + u
            l = list_ref[HEAD + i]
            first, second = list_ref[rights_at + 2 * i], list_ref[rights_at + 2 * i + 1]
            left = jnp.concatenate([left_ref[l], columns[l]], axis=1)
            right = jnp.concatenate([right_block(first), right_block(second)], axis=1)
            scores = jnp.dot(
                left, jnp.concatenate([right, ones], axis=0), preferred_element_type=jnp.float32
            )
            fold((2 * u) % COPIES, first, scores[:, :BLOCK])
            fold((2 * u + 1) % COPIES, second, scores[:, BLOCK:])
        return known

    known = lax.fori_loop(0, list_ref[0], functools.partial(step, 0, PAIRS), jnp.int32(0))
    known = lax.fori_loop(0, list_ref[1], functools.partial(step, list_ref[0] * PAIRS, TAIL), known)
    wait_for(known, PARTS)

    def finish(octet, carry):
        rows = []
        for k in range(8):
            r = octet * 8 + k
            tops = [peaks[copy, r] for copy in range(COPIES)]
            top = jnp.max(functools.reduce(jnp.maximum, tops), axis=0, keepdims=True)
            mass = sum(masses[copy, r] * jnp.exp2(tops[copy] - top) for copy in range(COPIES))
            rows.append(top + jnp.log2(jnp.sum(mass, axis=0, keepdims=True)))
        out_ref[0, pl.ds(pl.multiple_of(octet * 8, 8), 8), :] = jnp.concatenate(rows, axis=0)
        return carry

    lax.fori_loop(0, rights // 8, finish, 0, unroll=4)
    for k in range(1, out_ref.shape[0]):
        out_ref[k] = out_ref[0]
    if kind == FIRST:
        hand_on.wait()


def log_sums(kind, pairs, halves, remotes, parts, copies, keep=False):
    slots = 2 * GROUP
    lefts, rights = (halves, slots) if kind == COLUMNS else (slots, halves)
    form = (2 * GROUP // CAP, CAP * D, BLOCK) if kind == COLUMNS else (rights, BLOCK, BLOCK)
    held = lefts
    outs, bias = [shape((copies, rights, BLOCK))], pltpu.VMEM((lefts, BLOCK), jnp.float32)
    if kind == FIRST:
        held = lefts + 2
        outs.append(shape((held, BLOCK, BLOCK), jnp.bfloat16))
        scratch = [bias, bias, pltpu.VMEM((2 * GROUP // CAP, CAP * (D + EXTRA), BLOCK), jnp.bfloat16)]
        scratch.append(pltpu.VMEM((D, halves * BLOCK), jnp.bfloat16))
    elif kind == ROWS:
        scratch = [bias, pltpu.VMEM((2, BLOCK, BLOCK), jnp.bfloat16)]
    else:
        scratch = [pltpu.VMEM((BLOCK, BLOCK), jnp.bfloat16)]
        if keep:
            outs.append(shape((lefts, BLOCK)))
        else:
            scratch.insert(0, bias)
    return pl.pallas_call(
        functools.partial(pass_kernel, kind),
        out_shape=outs,
        in_specs=[HBM] * (1 + len(remotes)) + [SMEM if kind == FIRST else VMEM] * len(parts),
        out_specs=[VMEM, HBM] if kind == FIRST else [VMEM] * len(outs),
        scratch_shapes=scratch
        + [
            pltpu.VMEM((lefts, BLOCK, BLOCK), jnp.bfloat16),
            pltpu.VMEM((COPIES, rights + 1, 8, BLOCK), jnp.float32),
            pltpu.VMEM((COPIES, rights + 1, 8, BLOCK), jnp.float32),
            pltpu.SMEM(list_shape(halves), jnp.int32),
            pltpu.VMEM((held, BLOCK, BLOCK), jnp.bfloat16),
            pltpu.VMEM(form, jnp.bfloat16),
            pltpu.SemaphoreType.DMA((5 + PARTS,)),
        ],
        compiler_params=PREPARE if kind == FIRST else PASS,
    )(pairs, *remotes, *parts)


def ring(values, axis, size, stride=1):
    places = lax.axis_size(axis)
    out = [values]
    for d in range(1, size):
        pairs = []
        for i in range(places):
            place = i // stride % size
            pairs.append((i, i + ((place + d) % size - place) * stride))
        out.append(lax.ppermute(values, axis, pairs))
    return out


def shards(
    source_points,
    source_logmass,
    target_points,
    target_logmass,
    target_potential,
    tile_slot,
    tile_counts,
    fetch_ids,
):
    peers = lax.axis_size("src")
    blocks = tile_counts.shape[0]
    halves = blocks // 2
    per_peer = fetch_ids.shape[1]
    owned = target_potential.shape[0] // BLOCK
    count = peers * per_peer
    place = lax.axis_index("src")
    half = lax.axis_index("grp") % 2

    def swap(values):
        return ring(values, "grp", 2, 1)[1]

    tiles = [tile_slot.T, tile_counts.T]
    ids = ring(fetch_ids, "src", peers)
    ids, tiles = lax.optimization_barrier((ids, tiles + [swap(part) for part in tiles]))
    packed, target_half = pack(
        place,
        ids,
        target_points.T,
        target_potential.reshape(owned, BLOCK),
        target_logmass.reshape(owned, BLOCK),
    )
    row_pairs = make_list(rows_kernel, half, tiles)
    col_pairs = make_list(columns_kernel, half, tiles)
    fetched = lax.all_to_all(packed, "src", split_axis=0, concat_axis=0, tiled=True)
    fetched, row_pairs, col_pairs, ids = lax.optimization_barrier((fetched, row_pairs, col_pairs, ids))
    both = lax.optimization_barrier([fetched, swap(fetched)])

    groups = lax.axis_size("grp")
    same_core = [list(range(core, groups, 2)) for core in range(2)]
    for sweep_index in range(ITERS):
        if sweep_index == 0:
            turned = source_points.T
            rows, targets = log_sums(FIRST, row_pairs, halves, [*both, turned], [half.reshape(1)], groups // 2)
            rows, turned, logmass, ids = lax.optimization_barrier((rows, turned, source_logmass, ids))
            points, source_half, same = source(half, halves, turned, logmass.reshape(blocks, BLOCK), ids)
            same = [same, swap(same)]
        else:
            (rows,) = log_sums(ROWS, row_pairs, halves, [targets, points], col_parts + same, groups // 2)
        rows = lax.all_to_all(
            rows, "grp", split_axis=0, concat_axis=0, tiled=True, axis_index_groups=same_core
        )
        last = sweep_index == ITERS - 1
        cols, *fields = log_sums(COLUMNS, col_pairs, halves, [*both, points], [rows], 1, keep=last)
        cols = cols[0]
        if sweep_index < ITERS - 1:
            other = swap(cols)
            cols = log_sum([cols, jnp.concatenate([other[count:], other[:count]], axis=0)])
            col_parts = ring(cols, "src", peers)
    field, half = lax.optimization_barrier((fields[0], half))
    field = field * (1.0 / SCALE) + source_half
    low = half == 0
    other = swap(field)
    source_field = jnp.concatenate([jnp.where(low, field, other), jnp.where(low, other, field)], axis=0)

    cols = log_sum([cols[:count], swap(cols[count:])]).reshape(peers, per_peer, BLOCK)
    cols, last_place, ids, target_half, target_logmass = lax.optimization_barrier(
        (cols, place, ids, target_half, target_logmass)
    )
    back = []
    for d in range(peers):
        wanted = lax.dynamic_slice(cols, ((last_place + d) % peers, 0, 0), (1, per_peer, BLOCK))[0]
        pairs = [(i, (i + d) % peers) for i in range(peers)]
        back.append(wanted if d == 0 else lax.ppermute(wanted, "src", pairs))
    target_field = merge(last_place, back, ids, target_logmass.reshape(owned, BLOCK), target_half).reshape(-1)
    return (source_field.reshape(-1), target_field)


def solution(mesh):
    return jax.shard_map(
        shards,
        mesh=mesh,
        in_specs=(
            P("src", None),
            P("src"),
            P(("src", "grp"), None),
            P(("src", "grp")),
            P(("src", "grp")),
            P("src", "grp"),
            P("src", "grp"),
            P("src", "grp"),
        ),
        out_specs=(P("src"), P(("src", "grp"))),
        check_vma=False,
    )
```

```python
import functools

import jax
import jax.numpy as jnp
from jax import lax
from jax.experimental import pallas as pl
from jax.experimental.pallas import tpu as pltpu
from jax.sharding import PartitionSpec as P

D = 64
BLOCK = 128
KG = 8
ITERS = 3
EPSILON = 0.25
LOWEST = -1e30
LOG2E = 1.4426950408889634
SCALE = LOG2E / EPSILON
PAIRS = 64
TAIL = 16
COPIES = 2
GROUP = 32
CAP = 8
EXTRA = 6
LEFT, RIGHT = 0, 1
FIRST, ROWS, COLUMNS = 0, 1, 2
PARTS = 4
LONG = 1024 * 1024
HEAD = 8
STRIDE = 64


SMEM = pl.BlockSpec(memory_space=pltpu.SMEM)
VMEM = pl.BlockSpec(memory_space=pltpu.VMEM)
HBM = pl.BlockSpec(memory_space=pltpu.HBM)
MIB = 1024 * 1024
PREPARE = pltpu.CompilerParams(vmem_limit_bytes=64 * MIB)
PASS = pltpu.CompilerParams(vmem_limit_bytes=53 * MIB)


def shape(dims, dtype=jnp.float32):
    return jax.ShapeDtypeStruct(dims, dtype)


def start_copies(pairs, sems):
    copies = [pltpu.make_async_copy(src, dst, sems.at[k]) for k, (src, dst) in enumerate(pairs)]
    for copy in copies:
        copy.start()
    return copies


def close_list(ref, hbm, pairs, last, none, sems):
    right = HEAD + (ref.shape[0] - HEAD) // 3
    tails = (pairs + TAIL - 1) // TAIL
    ref[0] = tails // (PAIRS // TAIL)
    ref[1] = tails % (PAIRS // TAIL)

    def pad(k, carry):
        ref[HEAD + pairs + k] = last
        ref[right + 2 * (pairs + k)] = none
        ref[right + 2 * (pairs + k) + 1] = none
        return carry

    lax.fori_loop(0, tails * TAIL - pairs, pad, 0)
    copy = pltpu.make_async_copy(ref, hbm.at[pl.ds(0, ref.shape[0])], sems.at[0])
    copy.start()
    return copy


def columns_kernel(half_ref, *refs):
    remotes, hbm, (*tables, ref, sems) = refs[:4], refs[4], refs[5:]
    for copy in start_copies(list(zip(remotes, tables)), sems):
        copy.wait()
    halves = tables[0].shape[1] // 2
    first = half_ref[0] * halves
    right = HEAD + (ref.shape[0] - HEAD) // 3

    def one_block(b, position):
        at = right + 2 * position
        tiles = jnp.int32(0)
        for group, (slots_ref, counts_ref) in enumerate((tables[0:2], tables[2:4])):
            for k in range(KG):
                ref[at + tiles + k] = slots_ref[k, first + b] + group * GROUP
            tiles = tiles + counts_ref[0, first + b]
        ref[at + tiles] = 2 * GROUP
        for k in range(KG):
            ref[HEAD + position + k] = b
        return position + (tiles + 1) // 2

    pairs = lax.fori_loop(0, halves, one_block, jnp.int32(0))
    close_list(ref, hbm, pairs, halves - 1, 2 * GROUP, sems).wait()


def same_targets(ids, rows, same_ref):
    peers, per_peer = ids[0].shape
    lane = lax.broadcasted_iota(jnp.int32, (1, BLOCK), 1)
    known = jnp.zeros((1, BLOCK), jnp.int32)
    for d in range(peers):
        for p in range(peers):
            for c in range(per_peer):
                known = jnp.where(lane == (d * peers + p) * per_peer + c, ids[d][p, c], known)
    for p in range(peers):
        for c in range(per_peer):
            q = p * per_peer + c
            same = jnp.logical_and(known == ids[0][p, c], lane // per_peer % peers == p)
            for d in range(peers):
                own = jnp.logical_and(same, lane // GROUP == d)
                rows[pl.ds(d * GROUP + q, 1), :] = jnp.where(own, 1.0, 0.0)
    same_ref[...] = rows[...].astype(jnp.bfloat16)


def rows_kernel(half_ref, *refs):
    remotes, hbm, locals_ = refs[:4], refs[4], refs[5:]
    *tables, ref, lists, sizes, sems = locals_
    copies = start_copies(list(zip(remotes, tables)), sems)
    groups = (tables[0:2], tables[2:4])
    halves = tables[0].shape[1] // 2
    slots = 2 * GROUP
    first = half_ref[0] * halves
    right = HEAD + (ref.shape[0] - HEAD) // 3

    def clear(q, carry):
        sizes[q] = 0
        return carry

    lax.fori_loop(0, slots + 1, clear, 0, unroll=13)
    for copy in copies:
        copy.wait()

    def one_block(b, carry):
        def append(named):
            known = [sizes[slot] for slot in named]
            for slot, size in zip(named, known):
                lists[slot * STRIDE + size] = b
            for slot, size in zip(named, known):
                sizes[slot] = size + 1

        append([table[k, first + b] + group * GROUP for group, (table, _) in enumerate(groups) for k in range(2)])
        for group, (table, counts_ref) in enumerate(groups):
            count = counts_ref[0, first + b]

            def more(table=table, group=group, count=count):
                append(
                    [jnp.where(k < count, table[k, first + b] + group * GROUP, slots) for k in range(2, KG)]
                )

            pl.when(count > 2)(more)
        return carry

    lax.fori_loop(0, halves, one_block, 0)
    batch = 4

    def one_pair(q, position, k):
        ref[HEAD + position + k] = q
        for j in range(2):
            ref[right + 2 * (position + k) + j] = lists[q * STRIDE + 2 * k + j]

    def some_slots(t, position):
        counted = [sizes[t * batch + j] for j in range(batch)]
        for j, size in enumerate(counted):
            lists[(t * batch + j) * STRIDE + size] = halves
        counted = [(size + 1) // 2 for size in counted]
        places = [position]
        for pairs in counted:
            places.append(places[-1] + pairs)
        for j in range(batch):
            for k in range(3):
                one_pair(t * batch + j, places[j], k)

        def rest():
            for j in range(batch):

                def another(k, carry, j=j):
                    one_pair(t * batch + j, places[j], k)
                    return carry

                lax.fori_loop(3, counted[j], another, 0)

        pl.when(functools.reduce(jnp.maximum, counted) > 3)(rest)
        return places[-1]

    pairs = lax.fori_loop(0, slots // batch, some_slots, jnp.int32(0))
    close_list(ref, hbm, pairs, slots - 1, halves, sems).wait()


def list_shape(halves):
    room = HEAD + 3 * (halves * KG + 2 * GROUP + PAIRS + KG)
    return ((room + 1023) // 1024 * 1024,)


def make_list(kernel, half, remotes):
    own = [pltpu.SMEM(value.shape, value.dtype) for value in remotes]
    own.append(pltpu.SMEM(list_shape(remotes[0].shape[1] // 2), jnp.int32))
    if kernel is rows_kernel:
        own.append(pltpu.SMEM(((2 * GROUP + 1) * STRIDE,), jnp.int32))
        own.append(pltpu.SMEM((2 * GROUP + 1,), jnp.int32))
    return pl.pallas_call(
        kernel,
        out_shape=shape((LONG,), jnp.int32),
        in_specs=[SMEM] + [HBM] * len(remotes),
        out_specs=HBM,
        scratch_shapes=[*own, pltpu.SemaphoreType.DMA((len(remotes),))],
        compiler_params=PREPARE,
    )(half.reshape(1), *remotes)


def split3(values):
    high = values.astype(jnp.bfloat16)
    rest = values - high.astype(jnp.float32)
    middle = rest.astype(jnp.bfloat16)
    low = (rest - middle.astype(jnp.float32)).astype(jnp.bfloat16)
    return high, middle, low


def whole(parts):
    high, middle, low = [part.astype(jnp.float32) for part in parts]
    return high + middle + low


def log_sum(values):
    top = functools.reduce(jnp.maximum, values)
    return top + jnp.log2(sum(jnp.exp2(value - top) for value in values))


def pack_kernel(place_ref, *refs):
    count = (len(refs) - 3) // 2
    remotes, (out_ref, norm_ref, *locals_, sems) = refs[:count], refs[count:]
    *ids_refs, points, potential, logmass = locals_
    copies = start_copies(list(zip(remotes, locals_)), sems)
    place = place_ref[0]
    peers, per_peer = ids_refs[0].shape
    for copy in copies:
        copy.wait()

    def one_norm(t, carry):
        wide = points[:, pl.ds(pl.multiple_of(t * BLOCK, BLOCK), BLOCK)].astype(jnp.float32)
        norm_ref[pl.ds(t, 1), :] = 0.5 * jnp.sum(wide * wide, axis=0, keepdims=True)
        return carry

    lax.fori_loop(0, norm_ref.shape[0], one_norm, 0, unroll=8)
    for d, ids_ref in enumerate(ids_refs):
        other = lax.rem(place - d + peers, peers)
        rows = []
        for c in range(per_peer):
            t = ids_ref[place, c]
            block = points[:, pl.ds(pl.multiple_of(t * BLOCK, BLOCK), BLOCK)]
            start = SCALE * (potential[pl.ds(t, 1), :] - norm_ref[pl.ds(t, 1), :])
            mass = LOG2E * logmass[pl.ds(t, 1), :]
            rows += [part.astype(jnp.float32) for part in split3(start) + split3(mass)]
            out_ref[other, c * D : (c + 1) * D, :] = block
        out_ref[other, per_peer * D :, :] = jnp.concatenate(rows, axis=0).astype(jnp.bfloat16)
    norm_ref[...] += EPSILON * logmass[...]


def pack(place, ids, *values):
    remotes = [*ids, *values]
    return pl.pallas_call(
        pack_kernel,
        out_shape=[shape((len(ids), CAP * (D + EXTRA), BLOCK), jnp.bfloat16), shape(values[1].shape)],
        in_specs=[SMEM] + [HBM] * len(remotes),
        out_specs=[VMEM, VMEM],
        scratch_shapes=[pltpu.SMEM(value.shape, value.dtype) for value in ids]
        + [pltpu.VMEM(value.shape, value.dtype) for value in values]
        + [pltpu.SemaphoreType.DMA((len(remotes),))],
        compiler_params=PREPARE,
    )(place.reshape(1), *remotes)


def merge_kernel(wanted_ref, *refs):
    *sums, base_ref, out_ref, parts = refs
    per_peer = sums[0].shape[0]
    parts[...] = jnp.full_like(parts, LOWEST)
    for d, sums_ref in enumerate(sums):
        for c in range(per_peer):
            parts[d, pl.ds(wanted_ref[d * per_peer + c], 1), :] = sums_ref[c : c + 1, :]
    merged = log_sum([parts[d] for d in range(len(sums))])
    out_ref[...] = base_ref[...] - (1.0 / SCALE) * merged


def merge(wanted, sums, base):
    return pl.pallas_call(
        merge_kernel,
        out_shape=shape(base.shape),
        in_specs=[SMEM] + [VMEM] * (len(sums) + 1),
        out_specs=VMEM,
        scratch_shapes=[pltpu.VMEM((len(sums), *base.shape), jnp.float32)],
        compiler_params=PASS,
    )(wanted, *sums, base)


def scaled_block(points, b):
    wide = points[:, pl.ds(pl.multiple_of(b * BLOCK, BLOCK), BLOCK)].astype(jnp.float32)
    scaled = SCALE * wide
    high = scaled.astype(jnp.bfloat16)
    low = (scaled - high.astype(jnp.float32)).astype(jnp.bfloat16)
    return wide, jnp.concatenate([high, low], axis=0)


def source_kernel(half_ref, place_ref, points_hbm, logmass_hbm, *refs):
    count = (len(refs) - 9) // 2
    ids_hbm, (blocks_hbm, norm_ref, same_ref, wanted_ref, *locals_) = refs[:count], refs[count:]
    points, logmass, blocks, rows, *ids, sems = locals_
    halves = blocks.shape[1] - 1
    own = pl.ds(pl.multiple_of(half_ref[0] * halves, halves), halves)
    at = pl.multiple_of(half_ref[0] * (halves * BLOCK), halves * BLOCK)
    pairs = [(points_hbm.at[:, pl.ds(at, halves * BLOCK)], points), (logmass_hbm.at[own], logmass)]
    for copy in start_copies(pairs + list(zip(ids_hbm, ids)), sems):
        copy.wait()
    parts = split3(LOG2E * logmass[...])
    blocks[LEFT, halves] = jnp.concatenate([*parts, jnp.zeros_like(parts[0])], axis=0)
    blocks[RIGHT, halves] = jnp.zeros((BLOCK, BLOCK), jnp.bfloat16)

    part = halves // PARTS

    def one_block(b, carry):
        wide, both = scaled_block(points, b)
        norm_ref[pl.ds(b, 1), :] = 0.5 * jnp.sum(wide * wide, axis=0, keepdims=True)
        blocks[RIGHT, b] = both
        blocks[LEFT, b] = both.T
        return carry

    copies = []
    for k in range(PARTS):
        lax.fori_loop(k * part, (k + 1) * part, one_block, 0, unroll=4)
        own = (slice(None), pl.ds(k * part, part + (k == PARTS - 1)))
        copies.append(pltpu.make_async_copy(blocks.at[own], blocks_hbm.at[own], sems.at[2 + count + k]))
        copies[-1].start()
    same_targets(ids, rows, same_ref)
    peers, per_peer = ids[0].shape
    for d in range(peers):
        for c in range(per_peer):
            wanted_ref[d * per_peer + c] = ids[d][place_ref[0], c]
    for copy in copies:
        copy.wait()


def source(half, place, halves, points, logmass, ids):
    blocks = (2, halves + 1, BLOCK, BLOCK)
    return pl.pallas_call(
        source_kernel,
        out_shape=[
            shape(blocks, jnp.bfloat16),
            shape((halves, BLOCK)),
            shape((BLOCK, BLOCK), jnp.bfloat16),
            shape((GROUP,), jnp.int32),
        ],
        in_specs=[SMEM] * 2 + [HBM] * (2 + len(ids)),
        out_specs=[HBM, VMEM, VMEM, SMEM],
        scratch_shapes=[
            pltpu.VMEM((D, halves * BLOCK), jnp.bfloat16),
            pltpu.VMEM((halves, BLOCK), jnp.float32),
            pltpu.VMEM(blocks, jnp.bfloat16),
            pltpu.VMEM((BLOCK, BLOCK), jnp.float32),
        ]
        + [pltpu.SMEM(value.shape, value.dtype) for value in ids]
        + [pltpu.SemaphoreType.DMA((2 + len(ids) + PARTS,))],
        compiler_params=PASS,
    )(half.reshape(1), place.reshape(1), points, logmass, *ids)


def field_bias(mass_ref, parts_ref):
    rows = parts_ref.shape[1]
    mass = whole([mass_ref[k * rows : (k + 1) * rows, :] for k in range(3)])
    return mass - log_sum([parts_ref[k] for k in range(parts_ref.shape[0])])


def potential_bias(mass_ref, chosen_refs, *refs):
    dot = functools.partial(jnp.dot, preferred_element_type=jnp.float32)
    mass = whole([mass_ref[0, : 2 * GROUP, :], mass_ref[0, 2 * GROUP :, :], mass_ref[1, : 2 * GROUP, :]])
    out = []
    for group in range(2):
        own = slice(group * GROUP, (group + 1) * GROUP)
        chosen = chosen_refs[group][...]
        sums = jnp.concatenate([ref[own, :] for ref in refs], axis=0)
        parts = sum(dot(chosen, part) for part in split3(sums))
        known = dot(chosen, jnp.ones_like(chosen)) > 0.5
        parts = jnp.where(known, parts, LOWEST)
        merged = log_sum([parts[k * GROUP : (k + 1) * GROUP] for k in range(len(refs))])
        out.append(mass[own, :] - merged)
    return jnp.concatenate(out, axis=0)


def unpack(raw, left, start_ref, mass_ref, first, stop):
    def one_peer(peer, carry):
        rows = raw[peer, CAP * D :, :].astype(jnp.float32)
        for c in range(CAP):
            q = peer * CAP + c
            block = raw[peer, c * D : (c + 1) * D, :]
            left[q] = jnp.concatenate([block, block], axis=0).T
            high, middle, low, *mass = [rows[EXTRA * c + k : EXTRA * c + k + 1] for k in range(EXTRA)]
            start_ref[pl.ds(q, 1), :] = high + middle + low
            mass_ref[pl.ds(q, 1), :] = mass[0] + mass[1] + mass[2]
        return carry

    lax.fori_loop(first, stop, one_peer, 0)


def pass_kernel(kind, *refs):
    columns, peaks, masses, list_ref, left_ref, right_ref, sems = refs[-7:]
    lefts, rights = columns.shape[0], peaks.shape[1] - 1
    peers = GROUP // CAP
    part = lefts // PARTS
    left_parts = []
    if kind == FIRST:
        list_hbm, near_hbm, far_hbm, points_hbm, half_ref = refs[:5]
        out_ref, left_hbm, mass_ref, bias_ref, raw, points = refs[5:-7]
        own = rights * BLOCK
        at = pl.multiple_of(half_ref[0] * own, own)
        early = [(near_hbm, raw.at[pl.ds(0, peers)]), (far_hbm, raw.at[pl.ds(peers, peers)])]
        early.insert(0, (points_hbm.at[:, pl.ds(at, own)], points))
        late = []
    elif kind == ROWS:
        list_hbm, left_hbm, points_hbm = refs[:3]
        *col_parts, near_same, far_same, out_ref, bias_ref, mass = refs[3:-7]
        early = [(left_hbm.at[pl.ds(lefts, 2)], mass)]
        late = [(points_hbm.at[RIGHT, pl.ds(0, rights)], right_ref)]
        left_parts = [left_hbm.at[pl.ds(k * part, part)] for k in range(PARTS)]
    else:
        list_hbm, near_hbm, far_hbm, points_hbm, rows_ref, out_ref, bias_ref, mass = refs[:-7]
        early = [(points_hbm.at[LEFT, lefts], mass)]
        late = [
            (raw_hbm.at[:, pl.ds(0, CAP * D)], right_ref.at[pl.ds(group * peers, peers)])
            for group, raw_hbm in enumerate((near_hbm, far_hbm))
        ]
        left_parts = [points_hbm.at[LEFT, pl.ds(k * part, part)] for k in range(PARTS)]
    late.append((list_hbm.at[pl.ds(0, list_ref.shape[0])], list_ref))
    pairs = early + late + [(ref, left_ref.at[pl.ds(k * part, part)]) for k, ref in enumerate(left_parts)]
    copies = start_copies(pairs, sems)
    peaks[...] = jnp.full_like(peaks, LOWEST)
    masses[...] = jnp.zeros_like(masses)
    if kind == FIRST:
        copies[0].wait()

        def scale(b, carry):
            right_ref[b] = scaled_block(points, b)[1]
            return carry

        lax.fori_loop(0, rights, scale, 0, unroll=8)
        for group in range(2):
            copies[1 + group].wait()
            unpack(raw, left_ref, bias_ref, mass_ref, group * peers, (group + 1) * peers)
        high, middle, low = split3(mass_ref[...])
        left_ref[lefts] = jnp.concatenate([high, middle], axis=0)
        left_ref[lefts + 1] = jnp.concatenate([low, jnp.zeros_like(low)], axis=0)
        hand_on = pltpu.make_async_copy(left_ref, left_hbm, sems.at[len(pairs)])
        hand_on.start()
    else:
        for copy in copies[: len(early)]:
            copy.wait()
    if kind == ROWS:
        bias_ref[...] = potential_bias(mass, (near_same, far_same), *col_parts)
    elif kind == COLUMNS:
        bias_ref[...] = field_bias(mass, rows_ref)
    square = (BLOCK, BLOCK)
    lane = lax.broadcasted_iota(jnp.int32, square, 1)
    eye = jnp.where(lane == lax.broadcasted_iota(jnp.int32, square, 0), 1.0, 0.0).astype(jnp.bfloat16)
    lane = jnp.where(lane < 3 * GROUP, lane % GROUP, -1)
    for group in range(lefts // GROUP):
        high, middle, low = split3(bias_ref[group * GROUP : (group + 1) * GROUP, :])
        parts = jnp.concatenate([high, middle, low, jnp.zeros_like(high)], axis=0)
        turned = lax.dot_general(
            eye, parts, (((1,), (1,)), ((), ())), preferred_element_type=jnp.float32
        )

        def fill(k, carry, group=group, turned=turned):
            columns[group * GROUP + k] = jnp.where(lane == k, turned, 0.0).astype(jnp.bfloat16)
            return carry

        lax.fori_loop(0, GROUP, fill, 0, unroll=8)
    for copy in copies[len(early) : len(early) + len(late)]:
        copy.wait()
    rights_at = HEAD + (list_ref.shape[0] - HEAD) // 3
    ones = jnp.ones((BLOCK, 2 * BLOCK), jnp.bfloat16)

    def fold(copy, r, scores):
        scores = scores.reshape(BLOCK // 8, 8, BLOCK)
        old = peaks[copy, r]
        top = jnp.maximum(old, jnp.max(scores, axis=0))
        mass = jnp.sum(jnp.exp2(scores - top[None]), axis=0)
        masses[copy, r] = masses[copy, r] * jnp.exp2(old - top) + mass
        peaks[copy, r] = top

    def right_block(r):
        r = jnp.minimum(r, rights - 1)
        if kind != COLUMNS:
            return right_ref[r]
        block = right_ref[r // CAP, pl.ds(pl.multiple_of(r % CAP * D, D), D), :]
        return jnp.concatenate([block, block], axis=0)

    def wait_for(known, needed):
        if not left_parts:
            return known

        def wait(k, carry):
            at = pl.ds(k * part, part)
            source = left_hbm.at[at] if kind == ROWS else points_hbm.at[LEFT, at]
            pltpu.make_async_copy(source, left_ref.at[at], sems.at[len(early) + len(late) + k]).wait()
            return carry

        lax.fori_loop(known, needed, wait, 0)
        return jnp.maximum(known, needed)

    def step(start, count, t, known):
        known = wait_for(known, list_ref[HEAD + start + t * count + count - 1] // part + 1)
        for u in range(count):
            i = start + t * count + u
            l = list_ref[HEAD + i]
            first, second = list_ref[rights_at + 2 * i], list_ref[rights_at + 2 * i + 1]
            left = jnp.concatenate([left_ref[l], columns[l]], axis=1)
            right = jnp.concatenate([right_block(first), right_block(second)], axis=1)
            scores = jnp.dot(
                left, jnp.concatenate([right, ones], axis=0), preferred_element_type=jnp.float32
            )
            fold((2 * u) % COPIES, first, scores[:, :BLOCK])
            fold((2 * u + 1) % COPIES, second, scores[:, BLOCK:])
        return known

    known = lax.fori_loop(0, list_ref[0], functools.partial(step, 0, PAIRS), jnp.int32(0))
    known = lax.fori_loop(0, list_ref[1], functools.partial(step, list_ref[0] * PAIRS, TAIL), known)
    wait_for(known, PARTS)

    def finish(octet, carry):
        rows = []
        for k in range(8):
            r = octet * 8 + k
            tops = [peaks[copy, r] for copy in range(COPIES)]
            top = jnp.max(functools.reduce(jnp.maximum, tops), axis=0, keepdims=True)
            mass = sum(masses[copy, r] * jnp.exp2(tops[copy] - top) for copy in range(COPIES))
            rows.append(top + jnp.log2(jnp.sum(mass, axis=0, keepdims=True)))
        out_ref[0, pl.ds(pl.multiple_of(octet * 8, 8), 8), :] = jnp.concatenate(rows, axis=0)
        return carry

    lax.fori_loop(0, rights // 8, finish, 0, unroll=4)
    for k in range(1, out_ref.shape[0]):
        out_ref[k] = out_ref[0]
    if kind == FIRST:
        hand_on.wait()


def log_sums(kind, pairs, halves, remotes, parts, copies, keep=False):
    slots = 2 * GROUP
    lefts, rights = (halves, slots) if kind == COLUMNS else (slots, halves)
    form = (2 * GROUP // CAP, CAP * D, BLOCK) if kind == COLUMNS else (rights, BLOCK, BLOCK)
    held = lefts
    outs, bias = [shape((copies, rights, BLOCK))], pltpu.VMEM((lefts, BLOCK), jnp.float32)
    if kind == FIRST:
        held = lefts + 2
        outs.append(shape((held, BLOCK, BLOCK), jnp.bfloat16))
        scratch = [bias, bias, pltpu.VMEM((2 * GROUP // CAP, CAP * (D + EXTRA), BLOCK), jnp.bfloat16)]
        scratch.append(pltpu.VMEM((D, halves * BLOCK), jnp.bfloat16))
    elif kind == ROWS:
        scratch = [bias, pltpu.VMEM((2, BLOCK, BLOCK), jnp.bfloat16)]
    else:
        scratch = [pltpu.VMEM((BLOCK, BLOCK), jnp.bfloat16)]
        if keep:
            outs.append(shape((lefts, BLOCK)))
        else:
            scratch.insert(0, bias)
    return pl.pallas_call(
        functools.partial(pass_kernel, kind),
        out_shape=outs,
        in_specs=[HBM] * (1 + len(remotes)) + [SMEM if kind == FIRST else VMEM] * len(parts),
        out_specs=[VMEM, HBM] if kind == FIRST else [VMEM] * len(outs),
        scratch_shapes=scratch
        + [
            pltpu.VMEM((lefts, BLOCK, BLOCK), jnp.bfloat16),
            pltpu.VMEM((COPIES, rights + 1, 8, BLOCK), jnp.float32),
            pltpu.VMEM((COPIES, rights + 1, 8, BLOCK), jnp.float32),
            pltpu.SMEM(list_shape(halves), jnp.int32),
            pltpu.VMEM((held, BLOCK, BLOCK), jnp.bfloat16),
            pltpu.VMEM(form, jnp.bfloat16),
            pltpu.SemaphoreType.DMA((5 + PARTS,)),
        ],
        compiler_params=PREPARE if kind == FIRST else PASS,
    )(pairs, *remotes, *parts)


def ring(values, axis, size, stride=1):
    places = lax.axis_size(axis)
    out = [values]
    for d in range(1, size):
        pairs = []
        for i in range(places):
            place = i // stride % size
            pairs.append((i, i + ((place + d) % size - place) * stride))
        out.append(lax.ppermute(values, axis, pairs))
    return out


def shards(
    source_points,
    source_logmass,
    target_points,
    target_logmass,
    target_potential,
    tile_slot,
    tile_counts,
    fetch_ids,
):
    peers = lax.axis_size("src")
    blocks = tile_counts.shape[0]
    halves = blocks // 2
    per_peer = fetch_ids.shape[1]
    owned = target_potential.shape[0] // BLOCK
    count = peers * per_peer
    place = lax.axis_index("src")
    half = lax.axis_index("grp") % 2

    def swap(values):
        return ring(values, "grp", 2, 1)[1]

    tiles = [tile_slot.T, tile_counts.T]
    ids = ring(fetch_ids, "src", peers)
    ids, tiles = lax.optimization_barrier((ids, tiles + [swap(part) for part in tiles]))
    packed, target_base = pack(
        place,
        ids,
        target_points.T,
        target_potential.reshape(owned, BLOCK),
        target_logmass.reshape(owned, BLOCK),
    )
    row_pairs = make_list(rows_kernel, half, tiles)
    col_pairs = make_list(columns_kernel, half, tiles)
    fetched = lax.all_to_all(packed, "src", split_axis=0, concat_axis=0, tiled=True)
    fetched, row_pairs, col_pairs, ids = lax.optimization_barrier((fetched, row_pairs, col_pairs, ids))
    both = lax.optimization_barrier([fetched, swap(fetched)])

    groups = lax.axis_size("grp")
    same_core = [list(range(core, groups, 2)) for core in range(2)]
    for sweep_index in range(ITERS):
        if sweep_index == 0:
            turned = source_points.T
            rows, targets = log_sums(FIRST, row_pairs, halves, [*both, turned], [half.reshape(1)], groups // 2)
            rows, turned, logmass, ids = lax.optimization_barrier((rows, turned, source_logmass, ids))
            logmass = logmass.reshape(blocks, BLOCK)
            points, source_half, same, wanted = source(half, place, halves, turned, logmass, ids)
            same = [same, swap(same)]
        else:
            (rows,) = log_sums(ROWS, row_pairs, halves, [targets, points], col_parts + same, groups // 2)
        rows = lax.all_to_all(
            rows, "grp", split_axis=0, concat_axis=0, tiled=True, axis_index_groups=same_core
        )
        last = sweep_index == ITERS - 1
        cols, *fields = log_sums(COLUMNS, col_pairs, halves, [*both, points], [rows], 1, keep=last)
        cols = cols[0]
        if sweep_index < ITERS - 1:
            other = swap(cols)
            cols = log_sum([cols, jnp.concatenate([other[count:], other[:count]], axis=0)])
            col_parts = ring(cols, "src", peers)
    field, half = lax.optimization_barrier((fields[0], half))
    field = field * (1.0 / SCALE) + source_half
    low = half == 0
    other = swap(field)
    source_field = jnp.concatenate([jnp.where(low, field, other), jnp.where(low, other, field)], axis=0)

    cols = log_sum([cols[:count], swap(cols[count:])]).reshape(peers, per_peer, BLOCK)
    cols, last_place, wanted, target_base = lax.optimization_barrier((cols, place, wanted, target_base))
    back = []
    for d in range(peers):
        part = lax.dynamic_slice(cols, ((last_place + d) % peers, 0, 0), (1, per_peer, BLOCK))[0]
        pairs = [(i, (i + d) % peers) for i in range(peers)]
        back.append(part if d == 0 else lax.ppermute(part, "src", pairs))
    target_field = merge(wanted, back, target_base).reshape(-1)
    return (source_field.reshape(-1), target_field)


def solution(mesh):
    return jax.shard_map(
        shards,
        mesh=mesh,
        in_specs=(
            P("src", None),
            P("src"),
            P(("src", "grp"), None),
            P(("src", "grp")),
            P(("src", "grp")),
            P("src", "grp"),
            P("src", "grp"),
            P("src", "grp"),
        ),
        out_specs=(P("src"), P(("src", "grp"))),
        check_vma=False,
    )
```

```python
import functools

import jax
import jax.numpy as jnp
from jax import lax
from jax.experimental import pallas as pl
from jax.experimental.pallas import tpu as pltpu
from jax.sharding import PartitionSpec as P

D = 64
BLOCK = 128
KG = 8
ITERS = 3
EPSILON = 0.25
LOWEST = -1e30
LOG2E = 1.4426950408889634
SCALE = LOG2E / EPSILON
PAIRS = 64
TAIL = 16
COPIES = 2
GROUP = 32
CAP = 8
EXTRA = 6
LEFT, RIGHT = 0, 1
FIRST, ROWS, COLUMNS = 0, 1, 2
PARTS = 4
LONG = 1024 * 1024
HEAD = 8
STRIDE = 64


SMEM = pl.BlockSpec(memory_space=pltpu.SMEM)
VMEM = pl.BlockSpec(memory_space=pltpu.VMEM)
HBM = pl.BlockSpec(memory_space=pltpu.HBM)
MIB = 1024 * 1024
PREPARE = pltpu.CompilerParams(vmem_limit_bytes=64 * MIB)
PASS = pltpu.CompilerParams(vmem_limit_bytes=53 * MIB)


def shape(dims, dtype=jnp.float32):
    return jax.ShapeDtypeStruct(dims, dtype)


def start_copies(pairs, sems):
    copies = [pltpu.make_async_copy(src, dst, sems.at[k]) for k, (src, dst) in enumerate(pairs)]
    for copy in copies:
        copy.start()
    return copies


def close_list(ref, hbm, pairs, last, none, sems):
    right = HEAD + (ref.shape[0] - HEAD) // 3
    tails = (pairs + TAIL - 1) // TAIL
    ref[0] = tails // (PAIRS // TAIL)
    ref[1] = tails % (PAIRS // TAIL)

    def pad(k, carry):
        ref[HEAD + pairs + k] = last
        ref[right + 2 * (pairs + k)] = none
        ref[right + 2 * (pairs + k) + 1] = none
        return carry

    lax.fori_loop(0, tails * TAIL - pairs, pad, 0)
    copy = pltpu.make_async_copy(ref, hbm.at[pl.ds(0, ref.shape[0])], sems.at[0])
    copy.start()
    return copy


def columns_kernel(half_ref, *refs):
    remotes, hbm, (*tables, ref, sems) = refs[:4], refs[4], refs[5:]
    for copy in start_copies(list(zip(remotes, tables)), sems):
        copy.wait()
    halves = tables[0].shape[1] // 2
    first = half_ref[0] * halves
    right = HEAD + (ref.shape[0] - HEAD) // 3

    def one_block(b, position):
        at = right + 2 * position
        tiles = jnp.int32(0)
        for group, (slots_ref, counts_ref) in enumerate((tables[0:2], tables[2:4])):
            for k in range(KG):
                ref[at + tiles + k] = slots_ref[k, first + b] + group * GROUP
            tiles = tiles + counts_ref[0, first + b]
        ref[at + tiles] = 2 * GROUP
        for k in range(KG):
            ref[HEAD + position + k] = b
        return position + (tiles + 1) // 2

    pairs = lax.fori_loop(0, halves, one_block, jnp.int32(0))
    close_list(ref, hbm, pairs, halves - 1, 2 * GROUP, sems).wait()


def same_targets(ids, rows, same_ref):
    peers, per_peer = ids[0].shape
    lane = lax.broadcasted_iota(jnp.int32, (1, BLOCK), 1)
    known = jnp.zeros((1, BLOCK), jnp.int32)
    for d in range(peers):
        for p in range(peers):
            for c in range(per_peer):
                known = jnp.where(lane == (d * peers + p) * per_peer + c, ids[d][p, c], known)
    for p in range(peers):
        for c in range(per_peer):
            q = p * per_peer + c
            same = jnp.logical_and(known == ids[0][p, c], lane // per_peer % peers == p)
            for d in range(peers):
                own = jnp.logical_and(same, lane // GROUP == d)
                rows[pl.ds(d * GROUP + q, 1), :] = jnp.where(own, 1.0, 0.0)
    same_ref[...] = rows[...].astype(jnp.bfloat16)


def rows_kernel(half_ref, *refs):
    remotes, hbm, locals_ = refs[:4], refs[4], refs[5:]
    *tables, ref, lists, sizes, sems = locals_
    copies = start_copies(list(zip(remotes, tables)), sems)
    groups = (tables[0:2], tables[2:4])
    halves = tables[0].shape[1] // 2
    slots = 2 * GROUP
    first = half_ref[0] * halves
    right = HEAD + (ref.shape[0] - HEAD) // 3

    def clear(q, carry):
        sizes[q] = 0
        return carry

    lax.fori_loop(0, slots + 1, clear, 0, unroll=13)
    for copy in copies:
        copy.wait()

    def one_block(b, carry):
        def append(named):
            known = [sizes[slot] for slot in named]
            for slot, size in zip(named, known):
                lists[slot * STRIDE + size] = b
            for slot, size in zip(named, known):
                sizes[slot] = size + 1

        append([table[k, first + b] + group * GROUP for group, (table, _) in enumerate(groups) for k in range(2)])
        for group, (table, counts_ref) in enumerate(groups):
            count = counts_ref[0, first + b]

            def more(table=table, group=group, count=count):
                append(
                    [jnp.where(k < count, table[k, first + b] + group * GROUP, slots) for k in range(2, KG)]
                )

            pl.when(count > 2)(more)
        return carry

    lax.fori_loop(0, halves, one_block, 0)
    batch = 4

    def one_pair(q, position, k):
        ref[HEAD + position + k] = q
        for j in range(2):
            ref[right + 2 * (position + k) + j] = lists[q * STRIDE + 2 * k + j]

    def some_slots(t, position):
        counted = [sizes[t * batch + j] for j in range(batch)]
        for j, size in enumerate(counted):
            lists[(t * batch + j) * STRIDE + size] = halves
        counted = [(size + 1) // 2 for size in counted]
        places = [position]
        for pairs in counted:
            places.append(places[-1] + pairs)
        for j in range(batch):
            for k in range(3):
                one_pair(t * batch + j, places[j], k)

        def rest():
            for j in range(batch):

                def another(k, carry, j=j):
                    one_pair(t * batch + j, places[j], k)
                    return carry

                lax.fori_loop(3, counted[j], another, 0)

        pl.when(functools.reduce(jnp.maximum, counted) > 3)(rest)
        return places[-1]

    pairs = lax.fori_loop(0, slots // batch, some_slots, jnp.int32(0))
    close_list(ref, hbm, pairs, slots - 1, halves, sems).wait()


def list_shape(halves):
    room = HEAD + 3 * (halves * KG + 2 * GROUP + PAIRS + KG)
    return ((room + 1023) // 1024 * 1024,)


def make_list(kernel, half, remotes):
    own = [pltpu.SMEM(value.shape, value.dtype) for value in remotes]
    own.append(pltpu.SMEM(list_shape(remotes[0].shape[1] // 2), jnp.int32))
    if kernel is rows_kernel:
        own.append(pltpu.SMEM(((2 * GROUP + 1) * STRIDE,), jnp.int32))
        own.append(pltpu.SMEM((2 * GROUP + 1,), jnp.int32))
    return pl.pallas_call(
        kernel,
        out_shape=shape((LONG,), jnp.int32),
        in_specs=[SMEM] + [HBM] * len(remotes),
        out_specs=HBM,
        scratch_shapes=[*own, pltpu.SemaphoreType.DMA((len(remotes),))],
        compiler_params=PREPARE,
    )(half.reshape(1), *remotes)


def split3(values):
    high = values.astype(jnp.bfloat16)
    rest = values - high.astype(jnp.float32)
    middle = rest.astype(jnp.bfloat16)
    low = (rest - middle.astype(jnp.float32)).astype(jnp.bfloat16)
    return high, middle, low


def whole(parts):
    high, middle, low = [part.astype(jnp.float32) for part in parts]
    return high + middle + low


def log_sum(values):
    top = functools.reduce(jnp.maximum, values)
    return top + jnp.log2(sum(jnp.exp2(value - top) for value in values))


def pack_kernel(place_ref, *refs):
    count = (len(refs) - 3) // 2
    remotes, (out_ref, norm_ref, *locals_, sems) = refs[:count], refs[count:]
    *ids_refs, points, potential, logmass = locals_
    copies = start_copies(list(zip(remotes, locals_)), sems)
    place = place_ref[0]
    peers, per_peer = ids_refs[0].shape
    for copy in copies:
        copy.wait()

    def one_norm(t, carry):
        wide = points[:, pl.ds(pl.multiple_of(t * BLOCK, BLOCK), BLOCK)].astype(jnp.float32)
        norm_ref[pl.ds(t, 1), :] = 0.5 * jnp.sum(wide * wide, axis=0, keepdims=True)
        return carry

    lax.fori_loop(0, norm_ref.shape[0], one_norm, 0, unroll=8)
    for d, ids_ref in enumerate(ids_refs):
        other = lax.rem(place - d + peers, peers)
        rows = []
        for c in range(per_peer):
            t = ids_ref[place, c]
            block = points[:, pl.ds(pl.multiple_of(t * BLOCK, BLOCK), BLOCK)]
            start = SCALE * (potential[pl.ds(t, 1), :] - norm_ref[pl.ds(t, 1), :])
            mass = LOG2E * logmass[pl.ds(t, 1), :]
            rows += [part.astype(jnp.float32) for part in split3(start) + split3(mass)]
            out_ref[other, c * D : (c + 1) * D, :] = block
        out_ref[other, per_peer * D :, :] = jnp.concatenate(rows, axis=0).astype(jnp.bfloat16)
    norm_ref[...] += EPSILON * logmass[...]


def pack(place, ids, *values):
    remotes = [*ids, *values]
    return pl.pallas_call(
        pack_kernel,
        out_shape=[shape((len(ids), CAP * (D + EXTRA), BLOCK), jnp.bfloat16), shape(values[1].shape)],
        in_specs=[SMEM] + [HBM] * len(remotes),
        out_specs=[VMEM, VMEM],
        scratch_shapes=[pltpu.SMEM(value.shape, value.dtype) for value in ids]
        + [pltpu.VMEM(value.shape, value.dtype) for value in values]
        + [pltpu.SemaphoreType.DMA((len(remotes),))],
        compiler_params=PREPARE,
    )(place.reshape(1), *remotes)


def merge_kernel(wanted_ref, *refs):
    *sums, base_ref, out_ref, parts = refs
    per_peer = sums[0].shape[0]
    parts[...] = jnp.full_like(parts, LOWEST)
    for d, sums_ref in enumerate(sums):
        for c in range(per_peer):
            parts[d, pl.ds(wanted_ref[d * per_peer + c], 1), :] = sums_ref[c : c + 1, :]
    merged = log_sum([parts[d] for d in range(len(sums))])
    out_ref[...] = base_ref[...] - (1.0 / SCALE) * merged


def merge(wanted, sums, base):
    return pl.pallas_call(
        merge_kernel,
        out_shape=shape(base.shape),
        in_specs=[SMEM] + [VMEM] * (len(sums) + 1),
        out_specs=VMEM,
        scratch_shapes=[pltpu.VMEM((len(sums), *base.shape), jnp.float32)],
        compiler_params=PASS,
    )(wanted, *sums, base)


def scaled_block(points, b):
    wide = points[:, pl.ds(pl.multiple_of(b * BLOCK, BLOCK), BLOCK)].astype(jnp.float32)
    scaled = SCALE * wide
    high = scaled.astype(jnp.bfloat16)
    low = (scaled - high.astype(jnp.float32)).astype(jnp.bfloat16)
    return wide, jnp.concatenate([high, low], axis=0)


def source_kernel(half_ref, place_ref, points_hbm, logmass_hbm, *refs):
    count = (len(refs) - 9) // 2
    ids_hbm, (blocks_hbm, norm_ref, same_ref, wanted_ref, *locals_) = refs[:count], refs[count:]
    points, logmass, blocks, rows, *ids, sems = locals_
    halves = blocks.shape[1] - 1
    own = pl.ds(pl.multiple_of(half_ref[0] * halves, halves), halves)
    at = pl.multiple_of(half_ref[0] * (halves * BLOCK), halves * BLOCK)
    pairs = [(points_hbm.at[:, pl.ds(at, halves * BLOCK)], points), (logmass_hbm.at[own], logmass)]
    for copy in start_copies(pairs + list(zip(ids_hbm, ids)), sems):
        copy.wait()
    parts = split3(LOG2E * logmass[...])
    blocks[LEFT, halves] = jnp.concatenate([*parts, jnp.zeros_like(parts[0])], axis=0)
    blocks[RIGHT, halves] = jnp.zeros((BLOCK, BLOCK), jnp.bfloat16)

    part = halves // PARTS

    def one_block(b, carry):
        wide, both = scaled_block(points, b)
        norm_ref[pl.ds(b, 1), :] = 0.5 * jnp.sum(wide * wide, axis=0, keepdims=True)
        blocks[RIGHT, b] = both
        blocks[LEFT, b] = both.T
        return carry

    copies = []
    for k in range(PARTS):
        lax.fori_loop(k * part, (k + 1) * part, one_block, 0, unroll=4)
        own = (slice(None), pl.ds(k * part, part + (k == PARTS - 1)))
        copies.append(pltpu.make_async_copy(blocks.at[own], blocks_hbm.at[own], sems.at[2 + count + k]))
        copies[-1].start()
    same_targets(ids, rows, same_ref)
    peers, per_peer = ids[0].shape
    for d in range(peers):
        for c in range(per_peer):
            wanted_ref[d * per_peer + c] = ids[d][place_ref[0], c]
    for copy in copies:
        copy.wait()


def source(half, place, halves, points, logmass, ids):
    blocks = (2, halves + 1, BLOCK, BLOCK)
    return pl.pallas_call(
        source_kernel,
        out_shape=[
            shape(blocks, jnp.bfloat16),
            shape((halves, BLOCK)),
            shape((BLOCK, BLOCK), jnp.bfloat16),
            shape((GROUP,), jnp.int32),
        ],
        in_specs=[SMEM] * 2 + [HBM] * (2 + len(ids)),
        out_specs=[HBM, VMEM, VMEM, SMEM],
        scratch_shapes=[
            pltpu.VMEM((D, halves * BLOCK), jnp.bfloat16),
            pltpu.VMEM((halves, BLOCK), jnp.float32),
            pltpu.VMEM(blocks, jnp.bfloat16),
            pltpu.VMEM((BLOCK, BLOCK), jnp.float32),
        ]
        + [pltpu.SMEM(value.shape, value.dtype) for value in ids]
        + [pltpu.SemaphoreType.DMA((2 + len(ids) + PARTS,))],
        compiler_params=PASS,
    )(half.reshape(1), place.reshape(1), points, logmass, *ids)


def field_bias(mass_ref, parts_ref):
    rows = parts_ref.shape[1]
    mass = whole([mass_ref[k * rows : (k + 1) * rows, :] for k in range(3)])
    return mass - log_sum([parts_ref[k] for k in range(parts_ref.shape[0])])


def potential_bias(mass_ref, chosen_refs, *refs):
    dot = functools.partial(jnp.dot, preferred_element_type=jnp.float32)
    mass = whole([mass_ref[0, : 2 * GROUP, :], mass_ref[0, 2 * GROUP :, :], mass_ref[1, : 2 * GROUP, :]])
    out = []
    for group in range(2):
        own = slice(group * GROUP, (group + 1) * GROUP)
        chosen = chosen_refs[group][...]
        sums = jnp.concatenate([ref[own, :] for ref in refs], axis=0)
        parts = sum(dot(chosen, part) for part in split3(sums))
        known = dot(chosen, jnp.ones_like(chosen)) > 0.5
        parts = jnp.where(known, parts, LOWEST)
        merged = log_sum([parts[k * GROUP : (k + 1) * GROUP] for k in range(len(refs))])
        out.append(mass[own, :] - merged)
    return jnp.concatenate(out, axis=0)


def unpack(raw, left, start_ref, mass_ref, first, stop):
    def one_peer(peer, carry):
        rows = raw[peer, CAP * D :, :].astype(jnp.float32)
        for c in range(CAP):
            q = peer * CAP + c
            block = raw[peer, c * D : (c + 1) * D, :]
            left[q] = jnp.concatenate([block, block], axis=0).T
            high, middle, low, *mass = [rows[EXTRA * c + k : EXTRA * c + k + 1] for k in range(EXTRA)]
            start_ref[pl.ds(q, 1), :] = high + middle + low
            mass_ref[pl.ds(q, 1), :] = mass[0] + mass[1] + mass[2]
        return carry

    lax.fori_loop(first, stop, one_peer, 0, unroll=True)


def pass_kernel(kind, *refs):
    columns, peaks, masses, list_ref, left_ref, right_ref, sems = refs[-7:]
    lefts, rights = columns.shape[0], peaks.shape[1] - 1
    peers = GROUP // CAP
    part = lefts // PARTS
    left_parts = []
    if kind == FIRST:
        list_hbm, near_hbm, far_hbm, points_hbm, half_ref = refs[:5]
        out_ref, left_hbm, mass_ref, bias_ref, raw, points = refs[5:-7]
        own = rights * BLOCK
        at = pl.multiple_of(half_ref[0] * own, own)
        early = [(near_hbm, raw.at[pl.ds(0, peers)]), (far_hbm, raw.at[pl.ds(peers, peers)])]
        early.insert(0, (points_hbm.at[:, pl.ds(at, own)], points))
        late = []
    elif kind == ROWS:
        list_hbm, left_hbm, points_hbm = refs[:3]
        *col_parts, near_same, far_same, out_ref, bias_ref, mass = refs[3:-7]
        early = [(left_hbm.at[pl.ds(lefts, 2)], mass)]
        late = [(points_hbm.at[RIGHT, pl.ds(0, rights)], right_ref)]
        left_parts = [left_hbm.at[pl.ds(k * part, part)] for k in range(PARTS)]
    else:
        list_hbm, near_hbm, far_hbm, points_hbm, rows_ref, out_ref, bias_ref, mass = refs[:-7]
        early = [(points_hbm.at[LEFT, lefts], mass)]
        late = [
            (raw_hbm.at[:, pl.ds(0, CAP * D)], right_ref.at[pl.ds(group * peers, peers)])
            for group, raw_hbm in enumerate((near_hbm, far_hbm))
        ]
        left_parts = [points_hbm.at[LEFT, pl.ds(k * part, part)] for k in range(PARTS)]
    late.append((list_hbm.at[pl.ds(0, list_ref.shape[0])], list_ref))
    pairs = early + late + [(ref, left_ref.at[pl.ds(k * part, part)]) for k, ref in enumerate(left_parts)]
    copies = start_copies(pairs, sems)
    peaks[...] = jnp.full_like(peaks, LOWEST)
    masses[...] = jnp.zeros_like(masses)
    if kind == FIRST:
        copies[0].wait()

        def scale(b, carry):
            right_ref[b] = scaled_block(points, b)[1]
            return carry

        lax.fori_loop(0, rights, scale, 0, unroll=8)
        for group in range(2):
            copies[1 + group].wait()
            unpack(raw, left_ref, bias_ref, mass_ref, group * peers, (group + 1) * peers)
        high, middle, low = split3(mass_ref[...])
        left_ref[lefts] = jnp.concatenate([high, middle], axis=0)
        left_ref[lefts + 1] = jnp.concatenate([low, jnp.zeros_like(low)], axis=0)
        hand_on = pltpu.make_async_copy(left_ref, left_hbm, sems.at[len(pairs)])
        hand_on.start()
    else:
        for copy in copies[: len(early)]:
            copy.wait()
    if kind == ROWS:
        bias_ref[...] = potential_bias(mass, (near_same, far_same), *col_parts)
    elif kind == COLUMNS:
        bias_ref[...] = field_bias(mass, rows_ref)
    square = (BLOCK, BLOCK)
    lane = lax.broadcasted_iota(jnp.int32, square, 1)
    eye = jnp.where(lane == lax.broadcasted_iota(jnp.int32, square, 0), 1.0, 0.0).astype(jnp.bfloat16)
    lane = jnp.where(lane < 3 * GROUP, lane % GROUP, -1)
    for group in range(lefts // GROUP):
        high, middle, low = split3(bias_ref[group * GROUP : (group + 1) * GROUP, :])
        parts = jnp.concatenate([high, middle, low, jnp.zeros_like(high)], axis=0)
        turned = lax.dot_general(
            eye, parts, (((1,), (1,)), ((), ())), preferred_element_type=jnp.float32
        )

        def fill(k, carry, group=group, turned=turned):
            columns[group * GROUP + k] = jnp.where(lane == k, turned, 0.0).astype(jnp.bfloat16)
            return carry

        lax.fori_loop(0, GROUP, fill, 0, unroll=8)
    for copy in copies[len(early) : len(early) + len(late)]:
        copy.wait()
    rights_at = HEAD + (list_ref.shape[0] - HEAD) // 3
    ones = jnp.ones((BLOCK, 2 * BLOCK), jnp.bfloat16)

    def fold(copy, r, scores):
        scores = scores.reshape(BLOCK // 8, 8, BLOCK)
        old = peaks[copy, r]
        top = jnp.maximum(old, jnp.max(scores, axis=0))
        mass = jnp.sum(jnp.exp2(scores - top[None]), axis=0)
        masses[copy, r] = masses[copy, r] * jnp.exp2(old - top) + mass
        peaks[copy, r] = top

    def right_block(r):
        r = jnp.minimum(r, rights - 1)
        if kind != COLUMNS:
            return right_ref[r]
        block = right_ref[r // CAP, pl.ds(pl.multiple_of(r % CAP * D, D), D), :]
        return jnp.concatenate([block, block], axis=0)

    def wait_for(known, needed):
        if not left_parts:
            return known

        def wait(k, carry):
            at = pl.ds(k * part, part)
            source = left_hbm.at[at] if kind == ROWS else points_hbm.at[LEFT, at]
            pltpu.make_async_copy(source, left_ref.at[at], sems.at[len(early) + len(late) + k]).wait()
            return carry

        lax.fori_loop(known, needed, wait, 0)
        return jnp.maximum(known, needed)

    def step(start, count, t, known):
        known = wait_for(known, list_ref[HEAD + start + t * count + count - 1] // part + 1)
        for u in range(count):
            i = start + t * count + u
            l = list_ref[HEAD + i]
            first, second = list_ref[rights_at + 2 * i], list_ref[rights_at + 2 * i + 1]
            left = jnp.concatenate([left_ref[l], columns[l]], axis=1)
            right = jnp.concatenate([right_block(first), right_block(second)], axis=1)
            scores = jnp.dot(
                left, jnp.concatenate([right, ones], axis=0), preferred_element_type=jnp.float32
            )
            fold((2 * u) % COPIES, first, scores[:, :BLOCK])
            fold((2 * u + 1) % COPIES, second, scores[:, BLOCK:])
        return known

    known = lax.fori_loop(0, list_ref[0], functools.partial(step, 0, PAIRS), jnp.int32(0))
    known = lax.fori_loop(0, list_ref[1], functools.partial(step, list_ref[0] * PAIRS, TAIL), known)
    wait_for(known, PARTS)

    def finish(octet, carry):
        rows = []
        for k in range(8):
            r = octet * 8 + k
            tops = [peaks[copy, r] for copy in range(COPIES)]
            top = jnp.max(functools.reduce(jnp.maximum, tops), axis=0, keepdims=True)
            mass = sum(masses[copy, r] * jnp.exp2(tops[copy] - top) for copy in range(COPIES))
            rows.append(top + jnp.log2(jnp.sum(mass, axis=0, keepdims=True)))
        out_ref[0, pl.ds(pl.multiple_of(octet * 8, 8), 8), :] = jnp.concatenate(rows, axis=0)
        return carry

    lax.fori_loop(0, rights // 8, finish, 0, unroll=4)
    for k in range(1, out_ref.shape[0]):
        out_ref[k] = out_ref[0]
    if kind == FIRST:
        hand_on.wait()


def log_sums(kind, pairs, halves, remotes, parts, copies, keep=False):
    slots = 2 * GROUP
    lefts, rights = (halves, slots) if kind == COLUMNS else (slots, halves)
    form = (2 * GROUP // CAP, CAP * D, BLOCK) if kind == COLUMNS else (rights, BLOCK, BLOCK)
    held = lefts
    outs, bias = [shape((copies, rights, BLOCK))], pltpu.VMEM((lefts, BLOCK), jnp.float32)
    if kind == FIRST:
        held = lefts + 2
        outs.append(shape((held, BLOCK, BLOCK), jnp.bfloat16))
        scratch = [bias, bias, pltpu.VMEM((2 * GROUP // CAP, CAP * (D + EXTRA), BLOCK), jnp.bfloat16)]
        scratch.append(pltpu.VMEM((D, halves * BLOCK), jnp.bfloat16))
    elif kind == ROWS:
        scratch = [bias, pltpu.VMEM((2, BLOCK, BLOCK), jnp.bfloat16)]
    else:
        scratch = [pltpu.VMEM((BLOCK, BLOCK), jnp.bfloat16)]
        if keep:
            outs.append(shape((lefts, BLOCK)))
        else:
            scratch.insert(0, bias)
    return pl.pallas_call(
        functools.partial(pass_kernel, kind),
        out_shape=outs,
        in_specs=[HBM] * (1 + len(remotes)) + [SMEM if kind == FIRST else VMEM] * len(parts),
        out_specs=[VMEM, HBM] if kind == FIRST else [VMEM] * len(outs),
        scratch_shapes=scratch
        + [
            pltpu.VMEM((lefts, BLOCK, BLOCK), jnp.bfloat16),
            pltpu.VMEM((COPIES, rights + 1, 8, BLOCK), jnp.float32),
            pltpu.VMEM((COPIES, rights + 1, 8, BLOCK), jnp.float32),
            pltpu.SMEM(list_shape(halves), jnp.int32),
            pltpu.VMEM((held, BLOCK, BLOCK), jnp.bfloat16),
            pltpu.VMEM(form, jnp.bfloat16),
            pltpu.SemaphoreType.DMA((5 + PARTS,)),
        ],
        compiler_params=PREPARE if kind == FIRST else PASS,
    )(pairs, *remotes, *parts)


def ring(values, axis, size, stride=1):
    places = lax.axis_size(axis)
    out = [values]
    for d in range(1, size):
        pairs = []
        for i in range(places):
            place = i // stride % size
            pairs.append((i, i + ((place + d) % size - place) * stride))
        out.append(lax.ppermute(values, axis, pairs))
    return out


def shards(
    source_points,
    source_logmass,
    target_points,
    target_logmass,
    target_potential,
    tile_slot,
    tile_counts,
    fetch_ids,
):
    peers = lax.axis_size("src")
    blocks = tile_counts.shape[0]
    halves = blocks // 2
    per_peer = fetch_ids.shape[1]
    owned = target_potential.shape[0] // BLOCK
    count = peers * per_peer
    place = lax.axis_index("src")
    half = lax.axis_index("grp") % 2

    def swap(values):
        return ring(values, "grp", 2, 1)[1]

    tiles = [tile_slot.T, tile_counts.T]
    ids = ring(fetch_ids, "src", peers)
    ids, tiles = lax.optimization_barrier((ids, tiles + [swap(part) for part in tiles]))
    packed, target_base = pack(
        place,
        ids,
        target_points.T,
        target_potential.reshape(owned, BLOCK),
        target_logmass.reshape(owned, BLOCK),
    )
    row_pairs = make_list(rows_kernel, half, tiles)
    col_pairs = make_list(columns_kernel, half, tiles)
    fetched = lax.all_to_all(packed, "src", split_axis=0, concat_axis=0, tiled=True)
    fetched, row_pairs, col_pairs, ids = lax.optimization_barrier((fetched, row_pairs, col_pairs, ids))
    both = lax.optimization_barrier([fetched, swap(fetched)])

    groups = lax.axis_size("grp")
    same_core = [list(range(core, groups, 2)) for core in range(2)]
    for sweep_index in range(ITERS):
        if sweep_index == 0:
            turned = source_points.T
            rows, targets = log_sums(FIRST, row_pairs, halves, [*both, turned], [half.reshape(1)], groups // 2)
            rows, turned, logmass, ids = lax.optimization_barrier((rows, turned, source_logmass, ids))
            logmass = logmass.reshape(blocks, BLOCK)
            points, source_half, same, wanted = source(half, place, halves, turned, logmass, ids)
            same = [same, swap(same)]
        else:
            (rows,) = log_sums(ROWS, row_pairs, halves, [targets, points], col_parts + same, groups // 2)
        rows = lax.all_to_all(
            rows, "grp", split_axis=0, concat_axis=0, tiled=True, axis_index_groups=same_core
        )
        last = sweep_index == ITERS - 1
        cols, *fields = log_sums(COLUMNS, col_pairs, halves, [*both, points], [rows], 1, keep=last)
        cols = cols[0]
        if sweep_index < ITERS - 1:
            other = swap(cols)
            cols = log_sum([cols, jnp.concatenate([other[count:], other[:count]], axis=0)])
            col_parts = ring(cols, "src", peers)
    field, half = lax.optimization_barrier((fields[0], half))
    field = field * (1.0 / SCALE) + source_half
    low = half == 0
    other = swap(field)
    source_field = jnp.concatenate([jnp.where(low, field, other), jnp.where(low, other, field)], axis=0)

    cols = log_sum([cols[:count], swap(cols[count:])]).reshape(peers, per_peer, BLOCK)
    cols, last_place, wanted, target_base = lax.optimization_barrier((cols, place, wanted, target_base))
    back = []
    for d in range(peers):
        part = lax.dynamic_slice(cols, ((last_place + d) % peers, 0, 0), (1, per_peer, BLOCK))[0]
        pairs = [(i, (i + d) % peers) for i in range(peers)]
        back.append(part if d == 0 else lax.ppermute(part, "src", pairs))
    target_field = merge(wanted, back, target_base).reshape(-1)
    return (source_field.reshape(-1), target_field)


def solution(mesh):
    return jax.shard_map(
        shards,
        mesh=mesh,
        in_specs=(
            P("src", None),
            P("src"),
            P(("src", "grp"), None),
            P(("src", "grp")),
            P(("src", "grp")),
            P("src", "grp"),
            P("src", "grp"),
            P("src", "grp"),
        ),
        out_specs=(P("src"), P(("src", "grp"))),
        check_vma=False,
    )
```
